32 devices in a mesh: row: 8 (over z, core), col: 4 (over y, x).
Axes of the slice: x: 2, y: 2, z: 4, core: 2. Of those that a mesh axis runs over, the one named last changes fastest.
Arguments:
- new_velocity: float32 [3, 160, 160, 160], P(None, 'row', 'col'), may hold values from -6 to 6
- stored_velocity: float32 [6, 3, 256, 256, 256], P(None, None, 'row', 'col'), may hold values from -6 to 6
- stored_vorticity: float32 [6, 3, 256, 256, 256], P(None, None, 'row', 'col'), may hold values from -6 to 6
Outputs:
- next_velocity: float32 [3, 160, 160, 160], P(None, 'row', 'col')
The draws below stay inside these ranges and needn't reach their ends.
All inputs are finite; a program needn't handle non-finite values.
Results may differ from the reference program's by a relative error of at most 0.00007.
Values sent between devices are 32-bit elements; how exact they have to be, the bound alone decides.
No kernel may reach another device: no remote copies, remote signals or barrier semaphores. Data moves between devices by JAX's collectives and lax.ppermute only.
A program may use at most 256 MiB of HBM per device.

```python
import math
import jax
import jax.numpy as jnp
from jax import lax

N = 256
MODES = 160
ORDERS = 6
KMAX = 79


def shard_levels(key, dims, split, least, high):
    level = 1.0
    for dim, blocks in split:
        heights = jax.random.uniform(jax.random.fold_in(jax.random.fold_in(key, 6), dim), (blocks,), jnp.float32, least / len(split), high / len(split))
        level = level * jnp.repeat(jnp.exp(heights), dims[dim] // blocks).reshape((-1,) + (1,) * (len(dims) - 1 - dim))
    return level


def normal_values(key, dims, spread, bound, cuts=(), held_as=jnp.bfloat16):
    level = shard_levels(key, dims, cuts, -0.22, 0.18) if cuts else 1.0
    array = jax.random.normal(key, dims, jnp.float32) * spread * level
    return jnp.minimum(jnp.maximum(array, -bound), bound).astype(held_as)


def setup_inputs(seed: int = 0) -> dict:
    seeds = jax.random.split(jax.random.key(seed), 4)
    return {
        "new_velocity": normal_values(seeds[0], (3, MODES, MODES, MODES), 1.0, 6.0, ((1, 8), (2, 4)), jnp.float32),
        "stored_velocity": normal_values(seeds[1], (ORDERS, 3, N, N, N), 1.0, 6.0, ((2, 8), (3, 4)), jnp.float32),
        "stored_vorticity": normal_values(seeds[2], (ORDERS, 3, N, N, N), 1.0, 6.0, ((2, 8), (3, 4)), jnp.float32),
    }


highest = lax.Precision.HIGHEST

def synth_table(grid_len, mode_count):
    points = jnp.arange(grid_len, dtype=jnp.int32)[:, None]
    mode_index = jnp.arange(mode_count, dtype=jnp.int32)[None, :]
    wave_index = jnp.where(mode_index == 1, grid_len // 2, mode_index // 2)
    angles = (points * wave_index % grid_len).astype(jnp.float32) * (2.0 * math.pi / grid_len)
    trig_values = jnp.where((mode_index % 2 == 0) | (mode_index == 1), jnp.cos(angles), jnp.sin(angles))
    weight = jnp.where(mode_index < 2, 1.0, 2.0).astype(jnp.float32) / grid_len
    return trig_values * jnp.sqrt(weight)

def keep_modes(mode_index):
    return (mode_index != 1).astype(jnp.float32)

def pair_slope(spectra, axis_pos, wavenum):
    full_shape = spectra.shape
    half_len = full_shape[axis_pos] // 2
    paired = spectra.reshape(full_shape[:axis_pos] + (half_len, 2) + full_shape[axis_pos + 1:])
    pair_view = [1] * (len(full_shape) + 1)
    pair_view[axis_pos] = half_len
    scaled = wavenum.reshape(tuple(pair_view))
    even_part = lax.slice_in_dim(paired, 0, 1, axis=axis_pos + 1)
    odd_part = lax.slice_in_dim(paired, 1, 2, axis=axis_pos + 1)
    return jnp.concatenate([scaled * odd_part, -scaled * even_part], axis=axis_pos + 1).reshape(full_shape)

def synth_three(spectra, basis_table):
    section_one = jnp.einsum('yzm,xm->xyz', spectra, basis_table, precision=highest)
    section_two = jnp.einsum('xmz,ym->xyz', section_one, basis_table, precision=highest)
    return jnp.einsum('xym,zm->xyz', section_two, basis_table, precision=highest)

def analyze_three(physical, basis_table):
    section_one = jnp.einsum('xyz,zc->xyc', physical, basis_table, precision=highest)
    section_two = jnp.einsum('xyc,yk->xkc', section_one, basis_table, precision=highest)
    return jnp.einsum('xkc,xj->kcj', section_two, basis_table, precision=highest)

def cross_prod(left, right):
    return jnp.stack([left[1] * right[2] - left[2] * right[1], left[2] * right[0] - left[0] * right[2], left[0] * right[1] - left[1] * right[0]])

def reference(new_velocity, stored_velocity, stored_vorticity):
    mode_index = jnp.arange(MODES, dtype=jnp.int32)
    keep_flag = keep_modes(mode_index)
    wavenum = (mode_index[0::2] // 2).astype(jnp.float32) / KMAX
    keep_mask = keep_flag[:, None, None] * keep_flag[None, :, None] * keep_flag[None, None, :]
    coeffs = new_velocity * keep_mask
    coef_x, coef_y, coef_z = (coeffs[0], coeffs[1], coeffs[2])
    vort_x = pair_slope(coef_z, 0, wavenum) - pair_slope(coef_y, 1, wavenum)
    vort_y = pair_slope(coef_x, 1, wavenum) - pair_slope(coef_z, 2, wavenum)
    vort_z = pair_slope(coef_y, 2, wavenum) - pair_slope(coef_x, 0, wavenum)
    basis_table = synth_table(N, MODES)
    velocity_new = jnp.stack([synth_three(coef_x, basis_table), synth_three(coef_y, basis_table), synth_three(coef_z, basis_table)])
    vorticity_new = jnp.stack([synth_three(vort_x, basis_table), synth_three(vort_y, basis_table), synth_three(vort_z, basis_table)])
    cauchy_sum = cross_prod(velocity_new, stored_vorticity[0]) + cross_prod(stored_velocity[0], vorticity_new)
    for order_idx in range(1, ORDERS):
        cauchy_sum = cauchy_sum + cross_prod(stored_velocity[order_idx], stored_vorticity[ORDERS - order_idx])
    spectral = jnp.stack([analyze_three(cauchy_sum[0], basis_table), analyze_three(cauchy_sum[1], basis_table), analyze_three(cauchy_sum[2], basis_table)]) * keep_mask
    wave_mode = (mode_index // 2).astype(jnp.float32) / KMAX
    wave_square = wave_mode[:, None, None] ** 2 + wave_mode[None, :, None] ** 2 + wave_mode[None, None, :] ** 2
    divergence = pair_slope(spectral[0], 2, wavenum) + pair_slope(spectral[1], 0, wavenum) + pair_slope(spectral[2], 1, wavenum)
    potential = jnp.where(wave_square > 0, divergence / jnp.where(wave_square > 0, wave_square, 1.0), 0.0)
    result = jnp.stack([spectral[0] + pair_slope(potential, 2, wavenum), spectral[1] + pair_slope(potential, 0, wavenum), spectral[2] + pair_slope(potential, 1, wavenum)])
    return result / (ORDERS + 1)
```

```python
import functools
import math

import jax
import jax.numpy as jnp
import ml_dtypes
import numpy as np
from jax import lax
from jax.experimental import pallas as pl
from jax.experimental.pallas import tpu as pltpu
from jax.sharding import PartitionSpec as P

LANES = 128
XC = 8
BF16 = jnp.bfloat16
F32 = jnp.float32
NN = (((1,), (0,)), ((), ()))
NT = (((1,), (1,)), ((), ()))


def round_up(value, step):
    return -(-value // step) * step


def synth_np(grid_len, mode_count):
    points = np.arange(grid_len)[:, None]
    mode_index = np.arange(mode_count)[None, :]
    wave_index = np.where(mode_index == 1, grid_len // 2, mode_index // 2)
    angles = (points * wave_index % grid_len) * (2.0 * math.pi / grid_len)
    trig = np.where((mode_index % 2 == 0) | (mode_index == 1), np.cos(angles), np.sin(angles))
    weight = np.where(mode_index < 2, 1.0, 2.0) / grid_len
    return np.where(mode_index == 1, 0.0, trig * np.sqrt(weight))


def slope_np(table, kmax):
    paired = table.reshape(table.shape[0], -1, 2)
    wavenum = np.arange(paired.shape[1]) / kmax
    return np.stack([-wavenum * paired[:, :, 1], wavenum * paired[:, :, 0]], -1).reshape(table.shape)


def halves(table):
    high = table.astype(ml_dtypes.bfloat16)
    low = (table - high.astype(np.float64)).astype(ml_dtypes.bfloat16)
    return jnp.asarray(high), jnp.asarray(low)


def pieces_of(values):
    high = values.astype(BF16)
    return high, (values - high.astype(F32)).astype(BF16)


def dot(left, right, dims):
    return lax.dot_general(left, right, dims, preferred_element_type=F32)


def dot_data_left(values, high, low, dims=NN):
    top, rest = pieces_of(values)
    return dot(top, high, dims) + (dot(top, low, dims) + dot(rest, high, dims))


def dot_data_right(high, low, values, dims=NT):
    top, rest = pieces_of(values)
    return dot(high, top, dims) + (dot(low, top, dims) + dot(high, rest, dims))


def turn(values, shift):
    shift = shift % values.shape[-1]
    return values if shift == 0 else pltpu.roll(values, shift, axis=values.ndim - 1)


def lane_pack(parts, width, source_lane=0):
    tiles = []
    lane = lax.broadcasted_iota(jnp.int32, parts[0].shape, 1)
    for tile in range(-(-len(parts) * width // LANES)):
        start = tile * LANES
        acc = None
        for idx in range(start // width, min(len(parts) - 1, (start + LANES - 1) // width) + 1):
            moved = turn(parts[idx], idx * width - source_lane)
            acc = moved if acc is None else jnp.where(lane >= idx * width - start, moved, acc)
        tiles.append(acc)
    return tiles


def params(kind):
    return pltpu.CompilerParams(
        dimension_semantics=(kind,), vmem_limit_bytes=40 * 1024 * 1024
    )


def whole(array):
    rank = len(array.shape)
    return pl.BlockSpec(array.shape, lambda *_: (0,) * rank)


def first_synth_kernel(dims, x_ref, high_ref, low_ref, wave_ref, *rest):
    chunks, dests, xc = dims
    outs, rows = rest[:chunks], rest[chunks]
    _, ky_len, kz_len, modes = x_ref.shape
    group = 5 * kz_len
    wide = rows.shape[1]
    tail = modes // LANES * LANES
    if tail < wide:
        rows[:, tail:] = jnp.zeros((rows.shape[0], wide - tail), F32)
    if ky_len * group < rows.shape[0]:
        rows[ky_len * group :, :] = jnp.zeros((rows.shape[0] - ky_len * group, wide), F32)
    even = lax.broadcasted_iota(jnp.int32, (kz_len, wide), 1) % 2 == 0
    wave = wave_ref[0:1, :]

    def fill(ky, carry):
        base = ky * group
        for comp in range(3):
            start = pl.multiple_of(base + comp * kz_len, 8)
            rows[pl.ds(start, kz_len), 0:modes] = x_ref[comp, ky]
            if comp:
                value = rows[pl.ds(start, kz_len), :]
                swapped = jnp.where(even, turn(value, -1), -turn(value, 1)) * wave
                rows[pl.ds(pl.multiple_of(start + 2 * kz_len, 8), kz_len), :] = swapped
        return carry

    lax.fori_loop(0, ky_len, fill, 0)
    step = 256
    tiles = rows.shape[0] // LANES

    def mult(blk, carry):
        start = pl.multiple_of(blk * step, step)
        result = dot_data_right(high_ref[...], low_ref[...], rows[pl.ds(start, step), :])
        for idx in range(chunks):
            for dest in range(dests):
                at = (idx * dests + dest) * xc
                for tile in range(step // LANES):
                    spot = pl.multiple_of((dest * tiles + blk * (step // LANES) + tile) * xc, 8)
                    outs[idx][pl.ds(spot, xc), :] = result[
                        at : at + xc, tile * LANES : (tile + 1) * LANES
                    ]
        return carry

    lax.fori_loop(0, rows.shape[0] // step, mult, 0)


def first_synth(coeffs, table, wave, dims, lanes):
    chunks = dims[0]
    grid_len = table[0].shape[0]
    height = grid_len // chunks * (lanes // LANES)
    return pl.pallas_call(
        functools.partial(first_synth_kernel, dims),
        out_shape=[jax.ShapeDtypeStruct((height, LANES), F32)] * chunks,
        scratch_shapes=[pltpu.VMEM((lanes, table[0].shape[1]), F32)],
        compiler_params=pltpu.CompilerParams(vmem_limit_bytes=40 * 1024 * 1024),
        cost_estimate=pl.CostEstimate(
            flops=6 * grid_len * lanes * 256, bytes_accessed=4 * grid_len * lanes, transcendentals=0
        ),
        name="first_synth",
    )(coeffs, table[0], table[1], wave)


def second_synth_kernel(dims, a_ref, high_ref, low_ref, shigh_ref, slow_ref, out_ref):
    rows, xc, ky_len, kz_len, cols, y_len, pack = dims
    group = 5 * kz_len
    wide = round_up(group, LANES)
    at = pl.program_id(0)
    turned = []
    for part in range(pack):
        tiles = a_ref.shape[0] // (rows * xc)
        line = [
            a_ref[pl.ds(tile * xc + at * pack + part, rows, stride=tiles * xc), :]
            for tile in range(tiles)
        ]
        found = []
        for ky in range(ky_len):
            start = ky * group
            low, off = divmod(start, LANES)
            window = line[low : low + (wide // LANES) + (1 if off else 0)]
            found.append(turn(jnp.concatenate(window, axis=1), -off)[:, :wide])
        turned.append(jnp.concatenate(found, axis=0).T[:group])
    plain = dot_data_left(jnp.concatenate(turned, axis=0), high_ref[...], low_ref[...])
    slope_in = [t[c * kz_len : (c + 1) * kz_len] for t in turned for c in (0, 2)]
    slope = dot_data_left(jnp.concatenate(slope_in, axis=0), shigh_ref[...], slow_ref[...])
    fields = []
    for part in range(pack):
        own = plain[part * group : (part + 1) * group]
        sl = slope[part * 2 * kz_len : (part + 1) * 2 * kz_len]
        fields.append(
            jnp.concatenate(
                [
                    own[: 3 * kz_len],
                    own[3 * kz_len : 4 * kz_len] - sl[:kz_len],
                    sl[kz_len:],
                    -own[4 * kz_len :],
                ],
                axis=0,
            )
        )
    for dest in range(cols):
        tile, off = divmod(dest * y_len, LANES)
        out_ref[dest, 0] = lane_pack(
            [f[:, tile * LANES : (tile + 1) * LANES] for f in fields], y_len, off
        )[0]


def second_synth(arrived, table, slopes, dims):
    rows, xc, ky_len, kz_len, cols, y_len, pack = dims
    packs = xc // pack
    return pl.pallas_call(
        functools.partial(second_synth_kernel, dims),
        grid=(packs,),
        in_specs=[whole(a) for a in (arrived, *table, *slopes)],
        out_specs=pl.BlockSpec((cols, 1, 6 * kz_len, LANES), lambda i: (0, i, 0, 0)),
        out_shape=jax.ShapeDtypeStruct((cols, packs, 6 * kz_len, LANES), F32),
        compiler_params=params("arbitrary"),
        cost_estimate=pl.CostEstimate(
            flops=6 * xc * 7 * kz_len * 256 * 256 * 2,
            bytes_accessed=4 * arrived.size + 4 * cols * packs * 6 * kz_len * LANES,
            transcendentals=0,
        ),
        name="second_synth",
    )(arrived, *table, *slopes)


def cross(left, right):
    return [
        left[1] * right[2] - left[2] * right[1],
        left[2] * right[0] - left[0] * right[2],
        left[0] * right[1] - left[1] * right[0],
    ]


def earlier_kernel(count, *refs):
    vels, vorts, out_ref = refs[:count], refs[count : 2 * count], refs[2 * count]
    pack, y_len = out_ref.shape[1:3]
    for part in range(pack):
        def body(step, carry):
            at = pl.ds(pl.multiple_of(step * 8, 8), 8)
            total = None
            for vel, vort in zip(vels, vorts):
                term = cross(
                    [vel[0, c, part, at, :] for c in range(3)],
                    [vort[0, c, part, at, :] for c in range(3)],
                )
                total = term if total is None else [a + b for a, b in zip(total, term)]
            for comp in range(3):
                out_ref[comp, part, at, :] = total[comp]
            return carry

        lax.fori_loop(0, y_len // 8, body, 0, unroll=2)


def earlier(velocity, vorticity, chunk, xc, pack):
    orders, _, _, y_len, grid_len = velocity.shape
    packs = xc // pack
    block = (1, 3, pack, y_len, grid_len)

    def at(order):
        return pl.BlockSpec(block, lambda i: (order, 0, chunk * packs + i, 0, 0))

    specs = [at(k) for k in range(1, orders)] + [at(orders - k) for k in range(1, orders)]
    size = xc * y_len * grid_len
    return pl.pallas_call(
        functools.partial(earlier_kernel, orders - 1),
        grid=(packs,),
        in_specs=specs,
        out_specs=pl.BlockSpec((3, pack, y_len, grid_len), lambda i: (0, i, 0, 0)),
        out_shape=jax.ShapeDtypeStruct((3, xc, y_len, grid_len), F32),
        compiler_params=params("arbitrary"),
        cost_estimate=pl.CostEstimate(
            flops=size * 9 * 2 * orders, bytes_accessed=4 * size * (6 * orders - 3), transcendentals=0
        ),
        name="earlier_orders",
    )(*[velocity] * (orders - 1), *[vorticity] * (orders - 1))


def third_kernel(dims, b_ref, vel_ref, vort_ref, base_ref, high_ref, low_ref, shigh_ref, slow_ref, out_ref):
    kz_len, cols, y_len, pack = dims
    grid_len = high_ref.shape[1]

    def stack(field):
        return jnp.concatenate(
            [b_ref[src, 0, field * kz_len : (field + 1) * kz_len, :] for src in range(cols)], axis=0
        ).T

    lines = jnp.concatenate([stack(field) for field in range(6)], axis=0)
    plain = dot_data_left(lines, high_ref[...], low_ref[...])
    slope = dot_data_left(lines[: 2 * LANES], shigh_ref[...], slow_ref[...])
    at = [plain[f * LANES : (f + 1) * LANES] for f in range(6)]
    vel_new = at[:3]
    vort_new = [at[4] - slope[LANES:], slope[:LANES] + at[5], at[3]]
    flat = (pack * y_len, grid_len)
    vel = [vel_ref[0, c].reshape(flat) for c in range(3)]
    vort = [vort_ref[0, c].reshape(flat) for c in range(3)]
    one, two = cross(vel_new, vort), cross(vel, vort_new)
    total = [one[c] + two[c] + base_ref[c].reshape(flat) for c in range(3)]
    result = dot_data_right(high_ref[...], low_ref[...], jnp.concatenate(total, axis=0))
    for dest in range(cols):
        for comp in range(3):
            out_ref[dest, 0, comp * kz_len : (comp + 1) * kz_len, :] = result[
                dest * kz_len : (dest + 1) * kz_len, comp * LANES : (comp + 1) * LANES
            ]


def third(arrived, velocity, vorticity, base, table, slopes, chunk, dims):
    kz_len, cols, y_len, pack = dims
    packs = arrived.shape[1]
    grid_len = velocity.shape[-1]
    stored = pl.BlockSpec((1, 3, pack, y_len, grid_len), lambda i: (0, 0, chunk * packs + i, 0, 0))
    return pl.pallas_call(
        functools.partial(third_kernel, dims),
        grid=(packs,),
        in_specs=[
            pl.BlockSpec((cols, 1, 6 * kz_len, LANES), lambda i: (0, i, 0, 0)),
            stored,
            stored,
            pl.BlockSpec((3, pack, y_len, grid_len), lambda i: (0, i, 0, 0)),
            *[whole(a) for a in (*table, *slopes)],
        ],
        out_specs=pl.BlockSpec((cols, 1, 3 * kz_len, LANES), lambda i: (0, i, 0, 0)),
        out_shape=jax.ShapeDtypeStruct((cols, packs, 3 * kz_len, LANES), F32),
        compiler_params=params("arbitrary"),
        cost_estimate=pl.CostEstimate(
            flops=6 * packs * LANES * 11 * 256 * 256 * 2,
            bytes_accessed=4 * (arrived.size * 3 // 2 + packs * LANES * grid_len * 9),
            transcendentals=0,
        ),
        name="third_dimension",
    )(arrived, velocity, vorticity, base, *table, *slopes)


def second_back_kernel(dims, c_ref, high_ref, low_ref, out_ref):
    rows, xc, ky_len, kz_len, cols, y_len, pack = dims
    width = 3 * kz_len
    high_pad = round_up(width, LANES)
    lines = []
    for part in range(pack):
        tiles = lane_pack([c_ref[src, 0] for src in range(cols)], y_len, part * y_len)
        lines.append(jnp.concatenate(tiles, axis=1))
        if high_pad > width:
            lines.append(jnp.zeros((high_pad - width, cols * y_len), F32))
    result = dot_data_right(high_ref[...], low_ref[...], jnp.concatenate(lines, axis=0))
    for part in range(pack):
        own = result[:, part * high_pad : (part + 1) * high_pad]
        tiles = lane_pack([own[ky * rows : (ky + 1) * rows] for ky in range(ky_len)], width)
        at = pl.program_id(0) * pack + part
        for idx, tile in enumerate(tiles):
            out_ref[pl.ds(idx * xc + at, rows, stride=len(tiles) * xc), :] = tile


def second_back(arrived, table, dims):
    rows, xc, ky_len, kz_len, cols, y_len, pack = dims
    packs = xc // pack
    lanes = round_up(ky_len * 3 * kz_len, LANES)
    return pl.pallas_call(
        functools.partial(second_back_kernel, dims),
        grid=(packs,),
        in_specs=[
            pl.BlockSpec((cols, 1, 3 * kz_len, LANES), lambda i: (0, i, 0, 0)),
            *[whole(a) for a in table],
        ],
        out_specs=pl.BlockSpec((rows * xc * lanes // LANES, LANES), lambda i: (0, 0)),
        out_shape=jax.ShapeDtypeStruct((rows * xc * lanes // LANES, LANES), F32),
        compiler_params=params("arbitrary"),
        cost_estimate=pl.CostEstimate(
            flops=6 * xc * LANES * 256 * 256 * 2,
            bytes_accessed=4 * (arrived.size + rows * xc * lanes),
            transcendentals=0,
        ),
        name="second_back",
    )(arrived, *table)


def last_kernel(dims, *refs):
    chunks, xc, kz_len, modes, scale = dims
    wave_y_ref = refs[0]
    parts = refs[1 : 1 + chunks]
    high_ref, low_ref, wave_x_ref, wave_z_ref, out_ref, rows = refs[1 + chunks :]
    pair = 2 * 3 * kz_len
    at = pl.program_id(0)

    @pl.when(at == 0)
    def _():
        tiles = rows.shape[0] // LANES
        for tile in range(tiles):
            found = [
                part[(src * tiles + tile) * xc : (src * tiles + tile + 1) * xc, :]
                for part in parts
                for src in range(part.shape[0] // (tiles * xc))
            ]
            rows[tile * LANES : (tile + 1) * LANES, :] = jnp.concatenate(found, axis=0).T

    data = rows[pl.ds(pl.multiple_of(at * pair, 8), pair), :]
    spec = dot_data_left(data, high_ref[...], low_ref[...])
    wide = spec.shape[1]
    wave_x = jnp.broadcast_to(wave_x_ref[0:1, :], (kz_len, wide))
    wave_z = wave_z_ref[...]
    wave_y = wave_y_ref[at]
    even_x = lax.broadcasted_iota(jnp.int32, (kz_len, wide), 1) % 2 == 0
    even_z = lax.broadcasted_iota(jnp.int32, (kz_len, wide), 0) % 2 == 0

    def slope_x(value):
        return jnp.where(even_x, turn(value, -1), -turn(value, 1)) * wave_x

    def slope_z(value):
        return (
            jnp.where(
                even_z,
                pltpu.roll(value, kz_len - 1, axis=0),
                -pltpu.roll(value, 1, axis=0),
            )
            * wave_z
        )

    s = [
        [spec[(y * 3 + c) * kz_len : (y * 3 + c + 1) * kz_len] for c in range(3)] for y in range(2)
    ]
    square = wave_x * wave_x + wave_z * wave_z + wave_y * wave_y
    positive = square > 0
    safe = jnp.where(positive, square, 1.0)
    potential = []
    for y in range(2):
        along_y = s[1 - y][1] * (wave_y if y == 0 else -wave_y)
        divergence = slope_x(s[y][0]) + along_y + slope_z(s[y][2])
        potential.append(jnp.where(positive, divergence / safe, 0.0))
    for y in range(2):
        along_y = potential[1 - y] * (wave_y if y == 0 else -wave_y)
        found = [
            s[y][0] + slope_x(potential[y]),
            s[y][1] + along_y,
            s[y][2] + slope_z(potential[y]),
        ]
        for comp in range(3):
            out_ref[comp, y] = (found[comp] * scale)[:, :modes]


def last(parts, table, wave_y, wave_x, wave_z, xc, ky_len, kz_len, modes, scale):
    chunks = len(parts)
    grid_len = table[0].shape[0]
    lanes = parts[0].size * chunks // grid_len
    return pl.pallas_call(
        functools.partial(last_kernel, (chunks, xc, kz_len, modes, scale)),
        grid=(ky_len // 2,),
        in_specs=[
            pl.BlockSpec(memory_space=pltpu.SMEM),
            *[whole(a) for a in (*parts, *table, wave_x, wave_z)],
        ],
        out_specs=pl.BlockSpec((3, 2, kz_len, modes), lambda i: (0, i, 0, 0)),
        out_shape=jax.ShapeDtypeStruct((3, ky_len, kz_len, modes), F32),
        scratch_shapes=[pltpu.VMEM((lanes, grid_len), F32)],
        compiler_params=params("arbitrary"),
        cost_estimate=pl.CostEstimate(
            flops=6 * lanes * 256 * 256,
            bytes_accessed=4 * (grid_len * lanes + 3 * ky_len * kz_len * modes),
            transcendentals=0,
        ),
        name="last_projection",
    )(wave_y, *parts, *table, wave_x, wave_z)


def shards(new_velocity, stored_velocity, stored_vorticity):
    rows = lax.axis_size("row")
    cols = lax.axis_size("col")
    _, ky_len, kz_own, modes = new_velocity.shape
    orders, _, x_len, y_len, grid_len = stored_velocity.shape
    kz_len = round_up(kz_own, 8)
    kmax = modes // 2 - 1
    xc = min(XC, x_len)
    chunks = x_len // xc
    pack = LANES // y_len
    packs = xc // pack
    wide = round_up(modes, LANES)
    group = 5 * kz_len
    lanes = round_up(ky_len * group, 256)

    basis = synth_np(grid_len, modes)
    slope = slope_np(basis, kmax)
    x_order = (
        np.arange(rows)[None, :, None] * x_len
        + np.arange(chunks)[:, None, None] * xc
        + np.arange(xc)[None, None, :]
    ).reshape(-1)
    y_order = (np.arange(rows)[None, :] * ky_len + np.arange(ky_len)[:, None]).reshape(-1)

    def spread_z(table):
        parts = table.T.reshape(cols, kz_own, grid_len)
        return np.pad(parts, ((0, 0), (0, kz_len - kz_own), (0, 0))).reshape(cols * kz_len, grid_len)

    table_x = halves(np.pad(basis[x_order], ((0, 0), (0, wide - modes))))
    table_y, slope_y = halves(basis.T[y_order]), halves(slope.T[y_order])
    table_z, slope_z = halves(spread_z(basis)), halves(spread_z(slope))

    def wave_of(index):
        return (index // 2).astype(F32) / kmax

    mode = jnp.arange(wide, dtype=jnp.int32)
    wave_x = jnp.broadcast_to(jnp.where(mode < modes, wave_of(mode), 0.0)[None, :], (8, wide))
    ky_first = lax.axis_index("row") * ky_len + 2 * jnp.arange(ky_len // 2, dtype=jnp.int32)
    wave_y = wave_of(ky_first)
    kz = lax.axis_index("col") * kz_own + jnp.arange(kz_len, dtype=jnp.int32)
    wave_z = jnp.broadcast_to(wave_of(kz)[:, None], (kz_len, wide))

    coeffs = new_velocity
    if kz_len > kz_own:
        coeffs = jnp.pad(coeffs, ((0, 0), (0, 0), (0, kz_len - kz_own), (0, 0)))

    def swap(value, axis):
        return lax.all_to_all(value, axis, split_axis=0, concat_axis=0, tiled=True)

    dims = (rows, xc, ky_len, kz_len, cols, y_len, pack)
    sent = first_synth(coeffs, table_x, wave_x, (chunks, rows, xc), lanes)
    back = []
    for chunk in range(chunks):
        arrived = swap(sent[chunk], "row")
        base = earlier(stored_velocity, stored_vorticity, chunk, xc, pack)
        arrived = swap(second_synth(arrived, table_y, slope_y, dims), "col")
        found = third(
            arrived, stored_velocity, stored_vorticity, base, table_z, slope_z, chunk, dims[3:]
        )
        found = second_back(swap(found, "col"), table_y, dims)
        back.append(swap(found, "row"))
    result = last(
        back, table_x, wave_y, wave_x, wave_z, xc, ky_len, kz_len, modes, 1.0 / (orders + 1)
    )
    return result[:, :, :kz_own] if kz_len > kz_own else result


def solution(mesh):
    return jax.shard_map(
        shards,
        mesh=mesh,
        in_specs=(
            P(None, "row", "col", None),
            P(None, None, "row", "col", None),
            P(None, None, "row", "col", None),
        ),
        out_specs=P(None, "row", "col", None),
        check_vma=False,
    )
```

```python
import functools
import math

import jax
import jax.numpy as jnp
import ml_dtypes
import numpy as np
from jax import lax
from jax.experimental import pallas as pl
from jax.experimental.pallas import tpu as pltpu
from jax.sharding import PartitionSpec as P

LANES = 128
XC = 8
BF16 = jnp.bfloat16
F32 = jnp.float32
NN = (((1,), (0,)), ((), ()))
NT = (((1,), (1,)), ((), ()))


def round_up(value, step):
    return -(-value // step) * step


def synth_np(grid_len, mode_count):
    points = np.arange(grid_len)[:, None]
    mode_index = np.arange(mode_count)[None, :]
    wave_index = np.where(mode_index == 1, grid_len // 2, mode_index // 2)
    angles = (points * wave_index % grid_len) * (2.0 * math.pi / grid_len)
    trig = np.where((mode_index % 2 == 0) | (mode_index == 1), np.cos(angles), np.sin(angles))
    weight = np.where(mode_index < 2, 1.0, 2.0) / grid_len
    return np.where(mode_index == 1, 0.0, trig * np.sqrt(weight))


def slope_np(table, kmax):
    paired = table.reshape(table.shape[0], -1, 2)
    wavenum = np.arange(paired.shape[1]) / kmax
    return np.stack([-wavenum * paired[:, :, 1], wavenum * paired[:, :, 0]], -1).reshape(table.shape)


def halves(table):
    high = table.astype(ml_dtypes.bfloat16)
    low = (table - high.astype(np.float64)).astype(ml_dtypes.bfloat16)
    return high, low


def pieces_of(values):
    high = values.astype(BF16)
    return high, (values - high.astype(F32)).astype(BF16)


def dot(left, right, dims):
    return lax.dot_general(left, right, dims, preferred_element_type=F32)


def dot_data_left(values, high, low, dims=NN):
    top, rest = pieces_of(values)
    return dot(top, high, dims) + (dot(top, low, dims) + dot(rest, high, dims))


def dot_data_right(high, low, values, dims=NT):
    top, rest = pieces_of(values)
    return dot(high, top, dims) + (dot(low, top, dims) + dot(high, rest, dims))


def turn(values, shift):
    shift = shift % values.shape[-1]
    return values if shift == 0 else pltpu.roll(values, shift, axis=values.ndim - 1)


def lane_pack(parts, width, source_lane=0):
    tiles = []
    lane = lax.broadcasted_iota(jnp.int32, parts[0].shape, 1)
    for tile in range(-(-len(parts) * width // LANES)):
        start = tile * LANES
        acc = None
        for idx in range(start // width, min(len(parts) - 1, (start + LANES - 1) // width) + 1):
            moved = turn(parts[idx], idx * width - source_lane)
            acc = moved if acc is None else jnp.where(lane >= idx * width - start, moved, acc)
        tiles.append(acc)
    return tiles


def params(kind):
    return pltpu.CompilerParams(
        dimension_semantics=(kind,), vmem_limit_bytes=40 * 1024 * 1024
    )


def whole(array):
    rank = len(array.shape)
    return pl.BlockSpec(array.shape, lambda *_: (0,) * rank)


def first_synth_kernel(dims, x_ref, high_ref, low_ref, wave_ref, *rest):
    chunks, dests, xc = dims
    outs, rows = rest[:chunks], rest[chunks]
    _, ky_len, kz_len, modes = x_ref.shape
    group = 5 * kz_len
    wide = rows.shape[1]
    tail = modes // LANES * LANES
    if tail < wide:
        rows[:, tail:] = jnp.zeros((rows.shape[0], wide - tail), F32)
    if ky_len * group < rows.shape[0]:
        rows[ky_len * group :, :] = jnp.zeros((rows.shape[0] - ky_len * group, wide), F32)
    even = lax.broadcasted_iota(jnp.int32, (kz_len, wide), 1) % 2 == 0
    wave = wave_ref[0:1, :]

    def fill(ky, carry):
        base = ky * group
        for comp in range(3):
            start = pl.multiple_of(base + comp * kz_len, 8)
            rows[pl.ds(start, kz_len), 0:modes] = x_ref[comp, ky]
            if comp:
                value = rows[pl.ds(start, kz_len), :]
                swapped = jnp.where(even, turn(value, -1), -turn(value, 1)) * wave
                rows[pl.ds(pl.multiple_of(start + 2 * kz_len, 8), kz_len), :] = swapped
        return carry

    lax.fori_loop(0, ky_len, fill, 0)
    step = 256
    tiles = rows.shape[0] // LANES

    def mult(blk, carry):
        start = pl.multiple_of(blk * step, step)
        result = dot_data_right(high_ref[...], low_ref[...], rows[pl.ds(start, step), :])
        for idx in range(chunks):
            for dest in range(dests):
                at = (idx * dests + dest) * xc
                for tile in range(step // LANES):
                    spot = pl.multiple_of((dest * tiles + blk * (step // LANES) + tile) * xc, 8)
                    outs[idx][pl.ds(spot, xc), :] = result[
                        at : at + xc, tile * LANES : (tile + 1) * LANES
                    ]
        return carry

    lax.fori_loop(0, rows.shape[0] // step, mult, 0)


def first_synth(coeffs, table, wave, dims, lanes):
    table = [jnp.asarray(part) for part in table]
    chunks = dims[0]
    grid_len = table[0].shape[0]
    height = grid_len // chunks * (lanes // LANES)
    return pl.pallas_call(
        functools.partial(first_synth_kernel, dims),
        out_shape=[jax.ShapeDtypeStruct((height, LANES), F32)] * chunks,
        scratch_shapes=[pltpu.VMEM((lanes, table[0].shape[1]), F32)],
        compiler_params=pltpu.CompilerParams(vmem_limit_bytes=40 * 1024 * 1024),
        cost_estimate=pl.CostEstimate(
            flops=6 * grid_len * lanes * 256, bytes_accessed=4 * grid_len * lanes, transcendentals=0
        ),
        name="first_synth",
    )(coeffs, table[0], table[1], wave)


def second_synth_kernel(dims, a_ref, table_ref, *out_refs):
    rows, xc, ky_len, kz_len, cols, y_len, pack = dims
    group = 5 * kz_len
    wide = round_up(group, LANES)
    at = pl.program_id(0)
    turned = []
    for part in range(pack):
        tiles = a_ref.shape[0] // (rows * xc)
        line = [
            a_ref[pl.ds(tile * xc + at * pack + part, rows, stride=tiles * xc), :]
            for tile in range(tiles)
        ]
        found = []
        for ky in range(ky_len):
            start = ky * group
            low, off = divmod(start, LANES)
            window = line[low : low + (wide // LANES) + (1 if off else 0)]
            found.append(turn(jnp.concatenate(window, axis=1), -off)[:, :wide])
        turned.append(jnp.concatenate(found, axis=0).T[:group])
    plain = dot_data_left(jnp.concatenate(turned, axis=0), table_ref[0], table_ref[1])
    slope_in = [t[c * kz_len : (c + 1) * kz_len] for t in turned for c in (0, 2)]
    slope = dot_data_left(jnp.concatenate(slope_in, axis=0), table_ref[2], table_ref[3])
    fields = []
    for part in range(pack):
        own = plain[part * group : (part + 1) * group]
        sl = slope[part * 2 * kz_len : (part + 1) * 2 * kz_len]
        fields.append(
            jnp.concatenate(
                [
                    own[: 3 * kz_len],
                    own[3 * kz_len : 4 * kz_len] - sl[:kz_len],
                    sl[kz_len:],
                    -own[4 * kz_len :],
                ],
                axis=0,
            )
        )
    for dest in range(cols):
        tile, off = divmod(dest * y_len, LANES)
        out_refs[dest][0] = lane_pack(
            [f[:, tile * LANES : (tile + 1) * LANES] for f in fields], y_len, off
        )[0]


def second_synth(arrived, table, dims):
    rows, xc, ky_len, kz_len, cols, y_len, pack = dims
    packs = xc // pack
    return pl.pallas_call(
        functools.partial(second_synth_kernel, dims),
        grid=(packs,),
        in_specs=[whole(arrived), whole(table)],
        out_specs=[pl.BlockSpec((1, 6 * kz_len, LANES), lambda i: (i, 0, 0))] * cols,
        out_shape=[jax.ShapeDtypeStruct((packs, 6 * kz_len, LANES), F32)] * cols,
        compiler_params=params("arbitrary"),
        cost_estimate=pl.CostEstimate(
            flops=6 * xc * 7 * kz_len * 256 * 256 * 2,
            bytes_accessed=4 * arrived.size + 4 * cols * packs * 6 * kz_len * LANES,
            transcendentals=0,
        ),
        name="second_synth",
    )(arrived, table)


def cross(left, right):
    return [
        left[1] * right[2] - left[2] * right[1],
        left[2] * right[0] - left[0] * right[2],
        left[0] * right[1] - left[1] * right[0],
    ]


def earlier_kernel(count, *refs):
    vels, vorts, out_ref = refs[:count], refs[count : 2 * count], refs[2 * count]
    pack, y_len = out_ref.shape[1:3]
    for part in range(pack):
        def body(step, carry):
            at = pl.ds(pl.multiple_of(step * 8, 8), 8)
            total = None
            for vel, vort in zip(vels, vorts):
                term = cross(
                    [vel[0, c, part, at, :] for c in range(3)],
                    [vort[0, c, part, at, :] for c in range(3)],
                )
                total = term if total is None else [a + b for a, b in zip(total, term)]
            for comp in range(3):
                out_ref[comp, part, at, :] = total[comp]
            return carry

        lax.fori_loop(0, y_len // 8, body, 0, unroll=2)


def earlier(velocity, vorticity, chunk, xc, pack):
    orders, _, _, y_len, grid_len = velocity.shape
    packs = xc // pack
    block = (1, 3, pack, y_len, grid_len)

    def at(order):
        return pl.BlockSpec(block, lambda i: (order, 0, chunk * packs + i, 0, 0))

    specs = [at(k) for k in range(1, orders)] + [at(orders - k) for k in range(1, orders)]
    size = xc * y_len * grid_len
    return pl.pallas_call(
        functools.partial(earlier_kernel, orders - 1),
        grid=(packs,),
        in_specs=specs,
        out_specs=pl.BlockSpec((3, pack, y_len, grid_len), lambda i: (0, i, 0, 0)),
        out_shape=jax.ShapeDtypeStruct((3, xc, y_len, grid_len), F32),
        compiler_params=params("arbitrary"),
        cost_estimate=pl.CostEstimate(
            flops=size * 9 * 2 * orders, bytes_accessed=4 * size * (6 * orders - 3), transcendentals=0
        ),
        name="earlier_orders",
    )(*[velocity] * (orders - 1), *[vorticity] * (orders - 1))


def third_kernel(dims, *refs):
    kz_len, cols, y_len, pack = dims
    b_refs, out_refs = refs[:cols], refs[cols + 4 :]
    vel_ref, vort_ref, base_ref, table_ref = refs[cols : cols + 4]
    grid_len = table_ref.shape[2]

    def stack(field):
        return jnp.concatenate(
            [b_ref[0, field * kz_len : (field + 1) * kz_len, :] for b_ref in b_refs], axis=0
        ).T

    lines = jnp.concatenate([stack(field) for field in range(6)], axis=0)
    plain = dot_data_left(lines, table_ref[0], table_ref[1])
    slope = dot_data_left(lines[: 2 * LANES], table_ref[2], table_ref[3])
    at = [plain[f * LANES : (f + 1) * LANES] for f in range(6)]
    vel_new = at[:3]
    vort_new = [at[4] - slope[LANES:], slope[:LANES] + at[5], at[3]]
    flat = (pack * y_len, grid_len)
    vel = [vel_ref[0, c].reshape(flat) for c in range(3)]
    vort = [vort_ref[0, c].reshape(flat) for c in range(3)]
    one, two = cross(vel_new, vort), cross(vel, vort_new)
    total = [one[c] + two[c] + base_ref[c].reshape(flat) for c in range(3)]
    result = dot_data_right(table_ref[0], table_ref[1], jnp.concatenate(total, axis=0))
    for dest in range(cols):
        for comp in range(3):
            out_refs[dest][0, comp * kz_len : (comp + 1) * kz_len, :] = result[
                dest * kz_len : (dest + 1) * kz_len, comp * LANES : (comp + 1) * LANES
            ]


def third(arrived, velocity, vorticity, base, table, chunk, dims):
    kz_len, cols, y_len, pack = dims
    packs = arrived[0].shape[0]
    grid_len = velocity.shape[-1]
    stored = pl.BlockSpec((1, 3, pack, y_len, grid_len), lambda i: (0, 0, chunk * packs + i, 0, 0))
    return pl.pallas_call(
        functools.partial(third_kernel, dims),
        grid=(packs,),
        in_specs=[
            *[pl.BlockSpec((1, 6 * kz_len, LANES), lambda i: (i, 0, 0))] * cols,
            stored,
            stored,
            pl.BlockSpec((3, pack, y_len, grid_len), lambda i: (0, i, 0, 0)),
            whole(table),
        ],
        out_specs=[pl.BlockSpec((1, 3 * kz_len, LANES), lambda i: (i, 0, 0))] * cols,
        out_shape=[jax.ShapeDtypeStruct((packs, 3 * kz_len, LANES), F32)] * cols,
        compiler_params=params("arbitrary"),
        cost_estimate=pl.CostEstimate(
            flops=6 * packs * LANES * 11 * 256 * 256 * 2,
            bytes_accessed=4 * (cols * arrived[0].size * 3 // 2 + packs * LANES * grid_len * 9),
            transcendentals=0,
        ),
        name="third_dimension",
    )(*arrived, velocity, vorticity, base, table)


def second_back_kernel(dims, *refs):
    rows, xc, ky_len, kz_len, cols, y_len, pack = dims
    c_refs, table_ref, out_ref = refs[:cols], refs[cols], refs[cols + 1]
    width = 3 * kz_len
    high_pad = round_up(width, LANES)
    lines = []
    for part in range(pack):
        tiles = lane_pack([c_ref[0] for c_ref in c_refs], y_len, part * y_len)
        lines.append(jnp.concatenate(tiles, axis=1))
        if high_pad > width:
            lines.append(jnp.zeros((high_pad - width, cols * y_len), F32))
    result = dot_data_right(table_ref[0], table_ref[1], jnp.concatenate(lines, axis=0))
    for part in range(pack):
        own = result[:, part * high_pad : (part + 1) * high_pad]
        tiles = lane_pack([own[ky * rows : (ky + 1) * rows] for ky in range(ky_len)], width)
        at = pl.program_id(0) * pack + part
        for idx, tile in enumerate(tiles):
            out_ref[pl.ds(idx * xc + at, rows, stride=len(tiles) * xc), :] = tile


def second_back(arrived, table, dims):
    rows, xc, ky_len, kz_len, cols, y_len, pack = dims
    packs = xc // pack
    lanes = round_up(ky_len * 3 * kz_len, LANES)
    return pl.pallas_call(
        functools.partial(second_back_kernel, dims),
        grid=(packs,),
        in_specs=[
            *[pl.BlockSpec((1, 3 * kz_len, LANES), lambda i: (i, 0, 0))] * cols,
            whole(table),
        ],
        out_specs=pl.BlockSpec((rows * xc * lanes // LANES, LANES), lambda i: (0, 0)),
        out_shape=jax.ShapeDtypeStruct((rows * xc * lanes // LANES, LANES), F32),
        compiler_params=params("arbitrary"),
        cost_estimate=pl.CostEstimate(
            flops=6 * xc * LANES * 256 * 256 * 2,
            bytes_accessed=4 * (cols * arrived[0].size + rows * xc * lanes),
            transcendentals=0,
        ),
        name="second_back",
    )(*arrived, table)


def last_kernel(dims, *refs):
    chunks, xc, kz_len, modes, scale = dims
    wave_y_ref = refs[0]
    parts = refs[1 : 1 + chunks]
    high_ref, low_ref, wave_x_ref, wave_z_ref, out_ref, rows = refs[1 + chunks :]
    pair = 2 * 3 * kz_len
    at = pl.program_id(0)

    @pl.when(at == 0)
    def _():
        tiles = rows.shape[0] // LANES
        for tile in range(tiles):
            found = [
                part[(src * tiles + tile) * xc : (src * tiles + tile + 1) * xc, :]
                for part in parts
                for src in range(part.shape[0] // (tiles * xc))
            ]
            rows[tile * LANES : (tile + 1) * LANES, :] = jnp.concatenate(found, axis=0).T

    data = rows[pl.ds(pl.multiple_of(at * pair, 8), pair), :]
    spec = dot_data_left(data, high_ref[...], low_ref[...])
    wide = spec.shape[1]
    wave_x = jnp.broadcast_to(wave_x_ref[0:1, :], (kz_len, wide))
    wave_z = wave_z_ref[...]
    wave_y = wave_y_ref[at]
    even_x = lax.broadcasted_iota(jnp.int32, (kz_len, wide), 1) % 2 == 0
    even_z = lax.broadcasted_iota(jnp.int32, (kz_len, wide), 0) % 2 == 0

    def slope_x(value):
        return jnp.where(even_x, turn(value, -1), -turn(value, 1)) * wave_x

    def slope_z(value):
        return (
            jnp.where(
                even_z,
                pltpu.roll(value, kz_len - 1, axis=0),
                -pltpu.roll(value, 1, axis=0),
            )
            * wave_z
        )

    s = [
        [spec[(y * 3 + c) * kz_len : (y * 3 + c + 1) * kz_len] for c in range(3)] for y in range(2)
    ]
    square = wave_x * wave_x + wave_z * wave_z + wave_y * wave_y
    positive = square > 0
    safe = jnp.where(positive, square, 1.0)
    potential = []
    for y in range(2):
        along_y = s[1 - y][1] * (wave_y if y == 0 else -wave_y)
        divergence = slope_x(s[y][0]) + along_y + slope_z(s[y][2])
        potential.append(jnp.where(positive, divergence / safe, 0.0))
    for y in range(2):
        along_y = potential[1 - y] * (wave_y if y == 0 else -wave_y)
        found = [
            s[y][0] + slope_x(potential[y]),
            s[y][1] + along_y,
            s[y][2] + slope_z(potential[y]),
        ]
        for comp in range(3):
            out_ref[comp, y] = (found[comp] * scale)[:, :modes]


def last(parts, table, wave_y, wave_x, wave_z, xc, ky_len, kz_len, modes, scale):
    chunks = len(parts)
    table = [jnp.asarray(part) for part in table]
    grid_len = table[0].shape[0]
    lanes = parts[0].size * chunks // grid_len
    return pl.pallas_call(
        functools.partial(last_kernel, (chunks, xc, kz_len, modes, scale)),
        grid=(ky_len // 2,),
        in_specs=[
            pl.BlockSpec(memory_space=pltpu.SMEM),
            *[whole(a) for a in (*parts, *table, wave_x, wave_z)],
        ],
        out_specs=pl.BlockSpec((3, 2, kz_len, modes), lambda i: (0, i, 0, 0)),
        out_shape=jax.ShapeDtypeStruct((3, ky_len, kz_len, modes), F32),
        scratch_shapes=[pltpu.VMEM((lanes, grid_len), F32)],
        compiler_params=params("arbitrary"),
        cost_estimate=pl.CostEstimate(
            flops=6 * lanes * 256 * 256,
            bytes_accessed=4 * (grid_len * lanes + 3 * ky_len * kz_len * modes),
            transcendentals=0,
        ),
        name="last_projection",
    )(wave_y, *parts, *table, wave_x, wave_z)


def shards(new_velocity, stored_velocity, stored_vorticity):
    rows = lax.axis_size("row")
    cols = lax.axis_size("col")
    _, ky_len, kz_own, modes = new_velocity.shape
    orders, _, x_len, y_len, grid_len = stored_velocity.shape
    kz_len = round_up(kz_own, 8)
    kmax = modes // 2 - 1
    xc = min(XC, x_len)
    chunks = x_len // xc
    pack = LANES // y_len
    packs = xc // pack
    wide = round_up(modes, LANES)
    group = 5 * kz_len
    lanes = round_up(ky_len * group, 256)

    basis = synth_np(grid_len, modes)
    slope = slope_np(basis, kmax)
    x_order = (
        np.arange(rows)[None, :, None] * x_len
        + np.arange(chunks)[:, None, None] * xc
        + np.arange(xc)[None, None, :]
    ).reshape(-1)
    y_order = (np.arange(rows)[None, :] * ky_len + np.arange(ky_len)[:, None]).reshape(-1)

    def own_table(stack):
        return lax.dynamic_index_in_dim(jnp.asarray(stack), lax.axis_index("col"), 0, False)

    def halves_of(plain, sloped):
        return np.stack([part for table in (plain, sloped) for part in halves(table)])

    def y_table(col):
        points = np.concatenate([(col ^ k) * y_len + np.arange(y_len) for k in range(cols)])
        return halves_of(basis[points].T[y_order], slope[points].T[y_order])

    def z_table(col):
        def spread(table):
            parts = table.T.reshape(cols, kz_own, grid_len)[[col ^ k for k in range(cols)]]
            parts = np.pad(parts, ((0, 0), (0, kz_len - kz_own), (0, 0)))
            return parts.reshape(cols * kz_len, grid_len)

        return halves_of(spread(basis), spread(slope))

    table_x = halves(np.pad(basis[x_order], ((0, 0), (0, wide - modes))))
    table_y = own_table(np.stack([y_table(col) for col in range(cols)]))
    table_z = own_table(np.stack([z_table(col) for col in range(cols)]))

    def wave_of(index):
        return (index // 2).astype(F32) / kmax

    mode = jnp.arange(wide, dtype=jnp.int32)
    wave_x = jnp.broadcast_to(jnp.where(mode < modes, wave_of(mode), 0.0)[None, :], (8, wide))
    ky_first = lax.axis_index("row") * ky_len + 2 * jnp.arange(ky_len // 2, dtype=jnp.int32)
    wave_y = wave_of(ky_first)
    kz = lax.axis_index("col") * kz_own + jnp.arange(kz_len, dtype=jnp.int32)
    wave_z = jnp.broadcast_to(wave_of(kz)[:, None], (kz_len, wide))

    coeffs = new_velocity
    if kz_len > kz_own:
        coeffs = jnp.pad(coeffs, ((0, 0), (0, 0), (0, kz_len - kz_own), (0, 0)))

    def row_swap(value):
        return lax.all_to_all(value, "row", split_axis=0, concat_axis=0, tiled=True)

    def col_swap(values):
        return [
            lax.ppermute(value, "col", [(src, src ^ k) for src in range(cols)]) if k else value
            for k, value in enumerate(values)
        ]

    dims = (rows, xc, ky_len, kz_len, cols, y_len, pack)
    sent = list(first_synth(coeffs, table_x, wave_x, (chunks, rows, xc), lanes))
    sent, *stored = lax.optimization_barrier((sent, stored_velocity, stored_vorticity))
    base = [earlier(*stored, k, xc, pack) for k in range(chunks)]
    first, second, middle, back = {}, {}, {}, {}
    for step in range(chunks + 3):
        live = {}
        if step < chunks:
            live["first", step] = row_swap(sent[step])
        if 0 <= step - 1 < chunks:
            live["second", step - 1] = col_swap(second_synth(first[step - 1], table_y, dims))
        if 0 <= step - 2 < chunks:
            at = step - 2
            live["middle", at] = col_swap(
                third(second[at], stored_velocity, stored_vorticity, base[at], table_z, at, dims[3:])
            )
        if 0 <= step - 3 < chunks:
            live["back", step - 3] = row_swap(second_back(middle[step - 3], table_y, dims))
        ready = {k: base[k] for k in range(chunks) if max(k - 1, 0) == step}
        later = sent[step + 1 :]
        live, ready, later = lax.optimization_barrier((live, ready, later))
        sent[step + 1 :] = later
        for k, value in ready.items():
            base[k] = value
        for (kind, at), value in live.items():
            {"first": first, "second": second, "middle": middle, "back": back}[kind][at] = value
    back = [back[k] for k in range(chunks)]
    result = last(
        back, table_x, wave_y, wave_x, wave_z, xc, ky_len, kz_len, modes, 1.0 / (orders + 1)
    )
    return result[:, :, :kz_own] if kz_len > kz_own else result


def solution(mesh):
    return jax.shard_map(
        shards,
        mesh=mesh,
        in_specs=(
            P(None, "row", "col", None),
            P(None, None, "row", "col", None),
            P(None, None, "row", "col", None),
        ),
        out_specs=P(None, "row", "col", None),
        check_vma=False,
    )
```

```python
import functools
import math

import jax
import jax.numpy as jnp
import ml_dtypes
import numpy as np
from jax import lax
from jax.experimental import pallas as pl
from jax.experimental.pallas import tpu as pltpu
from jax.sharding import PartitionSpec as P

LANES = 128
XC = 8
BF16 = jnp.bfloat16
F32 = jnp.float32
NN = (((1,), (0,)), ((), ()))
NT = (((1,), (1,)), ((), ()))


def round_up(value, step):
    return -(-value // step) * step


def synth_np(grid_len, mode_count):
    points = np.arange(grid_len)[:, None]
    mode_index = np.arange(mode_count)[None, :]
    wave_index = np.where(mode_index == 1, grid_len // 2, mode_index // 2)
    angles = (points * wave_index % grid_len) * (2.0 * math.pi / grid_len)
    trig = np.where((mode_index % 2 == 0) | (mode_index == 1), np.cos(angles), np.sin(angles))
    weight = np.where(mode_index < 2, 1.0, 2.0) / grid_len
    return np.where(mode_index == 1, 0.0, trig * np.sqrt(weight))


def slope_np(table, kmax):
    paired = table.reshape(table.shape[0], -1, 2)
    wavenum = np.arange(paired.shape[1]) / kmax
    return np.stack([-wavenum * paired[:, :, 1], wavenum * paired[:, :, 0]], -1).reshape(table.shape)


def halves(table):
    high = table.astype(ml_dtypes.bfloat16)
    low = (table - high.astype(np.float64)).astype(ml_dtypes.bfloat16)
    return high, low


def pieces_of(values):
    high = values.astype(BF16)
    return high, (values - high.astype(F32)).astype(BF16)


def dot(left, right, dims):
    return lax.dot_general(left, right, dims, preferred_element_type=F32)


def dot_data_left(values, high, low, dims=NN):
    top, rest = pieces_of(values)
    return dot(top, high, dims) + (dot(top, low, dims) + dot(rest, high, dims))


def dot_data_right(high, low, values, dims=NT):
    top, rest = pieces_of(values)
    return dot(high, top, dims) + (dot(low, top, dims) + dot(high, rest, dims))


def turn(values, shift):
    shift = shift % values.shape[-1]
    return values if shift == 0 else pltpu.roll(values, shift, axis=values.ndim - 1)


def lane_pack(parts, width, source_lane=0):
    tiles = []
    lane = lax.broadcasted_iota(jnp.int32, parts[0].shape, 1)
    for tile in range(-(-len(parts) * width // LANES)):
        start = tile * LANES
        acc = None
        for idx in range(start // width, min(len(parts) - 1, (start + LANES - 1) // width) + 1):
            moved = turn(parts[idx], idx * width - source_lane)
            acc = moved if acc is None else jnp.where(lane >= idx * width - start, moved, acc)
        tiles.append(acc)
    return tiles


VMEM_LIMIT = 32 * 1024 * 1024
SHORT = pl.CostEstimate(flops=1024, bytes_accessed=1024, transcendentals=0)
HBM = pl.BlockSpec(memory_space=pl.ANY)
SMEM = pl.BlockSpec(memory_space=pltpu.SMEM)


def params():
    return pltpu.CompilerParams(dimension_semantics=("arbitrary",), vmem_limit_bytes=VMEM_LIMIT)


def fetch(sources, buffers, sem):
    at = pl.program_id(0)

    def copy(k, step):
        return pltpu.make_async_copy(sources[k].at[step], buffers.at[k, step], sem.at[k, step])

    @pl.when(at == 0)
    def _():
        for step in range(buffers.shape[1]):
            for k in range(len(sources)):
                copy(k, step).start()

    for k in range(len(sources)):
        copy(k, at).wait()


def whole(array):
    rank = len(array.shape)
    return pl.BlockSpec(array.shape, lambda *_: (0,) * rank)


def first_synth_kernel(dims, place_ref, own_ref, other_ref, table_ref, wave_ref, *rest):
    chunks, dests, xc = dims
    outs, rows = rest[: chunks * dests], rest[chunks * dests]
    _, ky_len, kz_len, modes = own_ref.shape
    group = 5 * kz_len
    half, wide = rows.shape[0] // 2, rows.shape[1]
    tail = modes // LANES * LANES
    if tail < wide:
        rows[:, tail:] = jnp.zeros((2 * half, wide - tail), F32)
    if ky_len * group < half:
        for core in range(2):
            rows[core * half + ky_len * group : (core + 1) * half, :] = jnp.zeros(
                (half - ky_len * group, wide), F32
            )
    even = lax.broadcasted_iota(jnp.int32, (kz_len, wide), 1) % 2 == 0
    wave = wave_ref[0:1, :]
    core = place_ref[1]

    def fill(ky, carry):
        for ref, side in ((own_ref, core), (other_ref, 1 - core)):
            base = side * half + ky * group
            for comp in range(3):
                start = pl.multiple_of(base + comp * kz_len, 8)
                rows[pl.ds(start, kz_len), 0:modes] = ref[comp, ky]
                if comp:
                    value = rows[pl.ds(start, kz_len), :]
                    swapped = jnp.where(even, turn(value, -1), -turn(value, 1)) * wave
                    rows[pl.ds(pl.multiple_of(start + 2 * kz_len, 8), kz_len), :] = swapped
        return carry

    lax.fori_loop(0, ky_len, fill, 0)
    step = 256
    points = table_ref.shape[0] // 2

    def mult(blk, carry):
        start = pl.multiple_of(blk * step, step)
        high, low = pieces_of(rows[pl.ds(start, step), :])
        both = dot(table_ref[...], high, NT)
        result = both[:points] + (both[points:] + dot(table_ref[:points], low, NT))
        for idx, out in enumerate(outs):
            for tile in range(step // LANES):
                spot = pl.multiple_of((blk * (step // LANES) + tile) * xc, 8)
                out[pl.ds(spot, xc), :] = result[
                    idx * xc : (idx + 1) * xc, tile * LANES : (tile + 1) * LANES
                ]
        return carry

    lax.fori_loop(0, 2 * half // step, mult, 0)


def first_synth(place, own, other, table, wave, dims, lanes):
    chunks, dests, xc = dims
    out = jax.ShapeDtypeStruct((2 * lanes // LANES * xc, LANES), F32)
    found = pl.pallas_call(
        functools.partial(first_synth_kernel, dims),
        in_specs=[SMEM] + [pl.BlockSpec(memory_space=pltpu.VMEM)] * 4,
        out_shape=[out] * (chunks * dests),
        scratch_shapes=[pltpu.VMEM((2 * lanes, table.shape[1]), F32)],
        compiler_params=pltpu.CompilerParams(vmem_limit_bytes=VMEM_LIMIT),
        cost_estimate=SHORT,
        name="first_synth",
    )(place, own, other, table, wave)
    return [list(found[k * dests : (k + 1) * dests]) for k in range(chunks)]


def second_synth_kernel(dims, place_ref, *refs):
    rows, xc, ky_len, kz_len, cols, y_len, pack = dims
    groups = rows // 2
    parts, table_ref, out_refs = refs[:groups], refs[groups], refs[groups + 1 : -2]
    a_ref, sem = refs[-2:]
    size = a_ref.shape[0] // groups

    @pl.when(pl.program_id(0) == 0)
    def _():
        copies = []
        for k, part in enumerate(parts):
            spot = pl.multiple_of((place_ref[0] ^ k) * size, 8)
            copies.append(pltpu.make_async_copy(part, a_ref.at[pl.ds(spot, size), :], sem.at[k]))
        for copy in copies:
            copy.start()
        for copy in copies:
            copy.wait()

    group = 5 * kz_len
    wide = round_up(group, LANES)
    at = pl.program_id(0)
    turned = []
    for part in range(pack):
        tiles = a_ref.shape[0] // (rows * xc)
        line = [
            a_ref[pl.ds(tile * xc + at * pack + part, rows, stride=tiles * xc), :]
            for tile in range(tiles)
        ]
        found = []
        for ky in range(ky_len):
            start = ky * group
            low, off = divmod(start, LANES)
            window = line[low : low + (wide // LANES) + (1 if off else 0)]
            found.append(turn(jnp.concatenate(window, axis=1), -off)[:, :wide])
        turned.append(jnp.concatenate(found, axis=0).T[:group])
    plain = dot_data_left(jnp.concatenate(turned, axis=0), table_ref[0], table_ref[1])
    slope_in = [t[c * kz_len : (c + 1) * kz_len] for t in turned for c in (0, 2)]
    slope = dot_data_left(jnp.concatenate(slope_in, axis=0), table_ref[2], table_ref[3])
    fields = []
    for part in range(pack):
        own = plain[part * group : (part + 1) * group]
        sl = slope[part * 2 * kz_len : (part + 1) * 2 * kz_len]
        fields.append(
            jnp.concatenate(
                [
                    own[: 3 * kz_len],
                    own[3 * kz_len : 4 * kz_len] - sl[:kz_len],
                    sl[kz_len:],
                    -own[4 * kz_len :],
                ],
                axis=0,
            )
        )
    for dest in range(cols):
        tile, off = divmod(dest * y_len, LANES)
        out_refs[dest][0] = lane_pack(
            [f[:, tile * LANES : (tile + 1) * LANES] for f in fields], y_len, off
        )[0]


def second_synth(place, arrived, table, dims):
    rows, xc, ky_len, kz_len, cols, y_len, pack = dims
    packs = xc // pack
    return pl.pallas_call(
        functools.partial(second_synth_kernel, dims),
        grid=(packs,),
        in_specs=[SMEM] + [HBM] * len(arrived) + [whole(table)],
        out_specs=[pl.BlockSpec((1, 6 * kz_len, LANES), lambda i: (i, 0, 0))] * cols,
        out_shape=[jax.ShapeDtypeStruct((packs, 6 * kz_len, LANES), F32)] * cols,
        scratch_shapes=[
            pltpu.VMEM((len(arrived) * arrived[0].shape[0], LANES), F32),
            pltpu.SemaphoreType.DMA((len(arrived),)),
        ],
        compiler_params=params(),
        cost_estimate=SHORT,
        name="second_synth",
    )(place, *arrived, table)


def cross(left, right):
    return [
        left[1] * right[2] - left[2] * right[1],
        left[2] * right[0] - left[0] * right[2],
        left[0] * right[1] - left[1] * right[0],
    ]


def earlier_kernel(count, *refs):
    vels, vorts, out_ref = refs[:count], refs[count : 2 * count], refs[2 * count]
    pack, y_len = out_ref.shape[1:3]
    for part in range(pack):
        def body(step, carry):
            at = pl.ds(pl.multiple_of(step * 8, 8), 8)
            total = None
            for vel, vort in zip(vels, vorts):
                term = cross(
                    [vel[0, c, part, at, :] for c in range(3)],
                    [vort[0, c, part, at, :] for c in range(3)],
                )
                total = term if total is None else [a + b for a, b in zip(total, term)]
            for comp in range(3):
                out_ref[comp, part, at, :] = total[comp]
            return carry

        lax.fori_loop(0, y_len // 8, body, 0, unroll=2)


def earlier(velocity, vorticity, chunk, xc, pack):
    orders, _, _, y_len, grid_len = velocity.shape
    packs = xc // pack
    block = (1, 3, pack, y_len, grid_len)

    def at(order):
        return pl.BlockSpec(block, lambda i: (order, 0, chunk * packs + i, 0, 0))

    specs = [at(k) for k in range(1, orders)] + [at(orders - k) for k in range(1, orders)]
    size = xc * y_len * grid_len
    return pl.pallas_call(
        functools.partial(earlier_kernel, orders - 1),
        grid=(packs,),
        in_specs=specs,
        out_specs=pl.BlockSpec((3, pack, y_len, grid_len), lambda i: (0, i, 0, 0)),
        out_shape=jax.ShapeDtypeStruct((3, xc, y_len, grid_len), F32),
        compiler_params=params(),
        cost_estimate=SHORT,
        name="earlier_orders",
    )(*[velocity] * (orders - 1), *[vorticity] * (orders - 1))


def third_kernel(dims, *refs):
    kz_len, cols, y_len, pack = dims
    b_refs, out_refs = refs[:cols], refs[cols + 4 : -2]
    buffers, sem = refs[-2:]
    fetch(b_refs, buffers, sem)
    at = pl.program_id(0)
    vel_ref, vort_ref, base_ref, table_ref = refs[cols : cols + 4]
    grid_len = table_ref.shape[2]

    def stack(field):
        return jnp.concatenate(
            [buffers[src, at, field * kz_len : (field + 1) * kz_len, :] for src in range(cols)], axis=0
        ).T

    lines = jnp.concatenate([stack(field) for field in range(6)], axis=0)
    plain = dot_data_left(lines, table_ref[0], table_ref[1])
    slope = dot_data_left(lines[: 2 * LANES], table_ref[2], table_ref[3])
    new = [plain[f * LANES : (f + 1) * LANES] for f in range(6)]
    vel_new = new[:3]
    vort_new = [new[4] - slope[LANES:], slope[:LANES] + new[5], new[3]]
    flat = (pack * y_len, grid_len)
    vel = [vel_ref[0, c].reshape(flat) for c in range(3)]
    vort = [vort_ref[0, c].reshape(flat) for c in range(3)]
    one, two = cross(vel_new, vort), cross(vel, vort_new)
    total = [one[c] + two[c] + base_ref[c].reshape(flat) for c in range(3)]
    result = dot_data_right(table_ref[0], table_ref[1], jnp.concatenate(total, axis=0))
    for dest in range(cols):
        for comp in range(3):
            out_refs[dest][0, comp * kz_len : (comp + 1) * kz_len, :] = result[
                dest * kz_len : (dest + 1) * kz_len, comp * LANES : (comp + 1) * LANES
            ]


def third(arrived, velocity, vorticity, base, table, chunk, dims):
    kz_len, cols, y_len, pack = dims
    packs = arrived[0].shape[0]
    grid_len = velocity.shape[-1]
    stored = pl.BlockSpec((1, 3, pack, y_len, grid_len), lambda i: (0, 0, chunk * packs + i, 0, 0))
    return pl.pallas_call(
        functools.partial(third_kernel, dims),
        grid=(packs,),
        in_specs=[
            *[HBM] * cols,
            stored,
            stored,
            pl.BlockSpec((3, pack, y_len, grid_len), lambda i: (0, i, 0, 0)),
            whole(table),
        ],
        out_specs=[pl.BlockSpec((1, 3 * kz_len, LANES), lambda i: (i, 0, 0))] * cols,
        out_shape=[jax.ShapeDtypeStruct((packs, 3 * kz_len, LANES), F32)] * cols,
        scratch_shapes=[
            pltpu.VMEM((cols, packs, 6 * kz_len, LANES), F32),
            pltpu.SemaphoreType.DMA((cols, packs)),
        ],
        compiler_params=params(),
        cost_estimate=SHORT,
        name="third_dimension",
    )(*arrived, velocity, vorticity, base, table)


def second_back_kernel(dims, place_ref, *refs):
    rows, xc, ky_len, kz_len, cols, y_len, pack = dims
    c_refs, table_ref, out_refs = refs[:cols], refs[cols], refs[cols + 1 : -4]
    out_ref, sem, buffers, fetch_sem = refs[-4:]
    fetch(c_refs, buffers, fetch_sem)
    at = pl.program_id(0)
    width = 3 * kz_len
    high_pad = round_up(width, LANES)
    lines = []
    for part in range(pack):
        tiles = lane_pack([buffers[src, at] for src in range(cols)], y_len, part * y_len)
        lines.append(jnp.concatenate(tiles, axis=1))
        if high_pad > width:
            lines.append(jnp.zeros((high_pad - width, cols * y_len), F32))
    result = dot_data_right(table_ref[0], table_ref[1], jnp.concatenate(lines, axis=0))
    for part in range(pack):
        own = result[:, part * high_pad : (part + 1) * high_pad]
        tiles = lane_pack([own[ky * rows : (ky + 1) * rows] for ky in range(ky_len)], width)
        spot = at * pack + part
        for idx, tile in enumerate(tiles):
            out_ref[pl.ds(idx * xc + spot, rows, stride=len(tiles) * xc), :] = tile

    @pl.when(pl.program_id(0) == pl.num_programs(0) - 1)
    def _():
        size = out_ref.shape[0] // len(out_refs)
        copies = []
        for k, out in enumerate(out_refs):
            spot = pl.multiple_of((place_ref[0] ^ k) * size, 8)
            copies.append(pltpu.make_async_copy(out_ref.at[pl.ds(spot, size), :], out, sem.at[k]))
        for copy in copies:
            copy.start()
        for copy in copies:
            copy.wait()


def second_back(place, arrived, table, dims):
    rows, xc, ky_len, kz_len, cols, y_len, pack = dims
    packs = xc // pack
    size = round_up(ky_len * 3 * kz_len, LANES) // LANES * xc
    groups = rows // 2
    return pl.pallas_call(
        functools.partial(second_back_kernel, dims),
        grid=(packs,),
        in_specs=[
            SMEM,
            *[HBM] * cols,
            whole(table),
        ],
        out_specs=[HBM] * groups,
        out_shape=[jax.ShapeDtypeStruct((2 * size, LANES), F32)] * groups,
        scratch_shapes=[
            pltpu.VMEM((rows * size, LANES), F32),
            pltpu.SemaphoreType.DMA((groups,)),
            pltpu.VMEM((cols, packs, 3 * kz_len, LANES), F32),
            pltpu.SemaphoreType.DMA((cols, packs)),
        ],
        compiler_params=params(),
        cost_estimate=SHORT,
        name="second_back",
    )(place, *arrived, table)


def first_back_kernel(dims, place_ref, *refs):
    count, xc, own = dims
    parts, table_ref, out_ref = refs[:count], refs[count], refs[count + 1]
    data, sem = refs[-2:]
    size = data.shape[1]
    core = place_ref[1] if own else 1 - place_ref[1]
    spot = pl.multiple_of(core * size, 8)
    copies = [
        pltpu.make_async_copy(part.at[pl.ds(spot, size), :], data.at[k], sem.at[k])
        for k, part in enumerate(parts)
    ]
    for copy in copies:
        copy.start()
    for copy in copies:
        copy.wait()
    for tile in range(size // xc):
        found = jnp.concatenate([data[k, tile * xc : (tile + 1) * xc, :] for k in range(count)], axis=0)
        out_ref[:, tile * LANES : (tile + 1) * LANES] = dot_data_right(
            table_ref[0], table_ref[1], found, NN
        )


def first_back(place, parts, table, xc, own):
    count = len(parts)
    size = parts[0].shape[0] // 2
    return pl.pallas_call(
        functools.partial(first_back_kernel, (count, xc, own)),
        in_specs=[SMEM] + [HBM] * count + [pl.BlockSpec(memory_space=pltpu.VMEM)],
        out_shape=jax.ShapeDtypeStruct((table.shape[1], size // xc * LANES), F32),
        scratch_shapes=[pltpu.VMEM((count, size, LANES), F32), pltpu.SemaphoreType.DMA((count,))],
        compiler_params=pltpu.CompilerParams(vmem_limit_bytes=VMEM_LIMIT),
        cost_estimate=SHORT,
        name="first_back",
    )(place, *parts, table)


def last_kernel(dims, *refs):
    kz_len, modes, scale = dims
    wave_y_ref, own_ref, other_ref, wave_x_ref, wave_z_ref, out_ref, rows = refs
    pair = 2 * 3 * kz_len
    at = pl.program_id(0)

    @pl.when(at == 0)
    def _():
        for tile in range(rows.shape[0] // LANES):
            lanes = slice(tile * LANES, (tile + 1) * LANES)
            rows[lanes, 0:modes] = (own_ref[:, lanes] + other_ref[:, lanes]).T

    spec = rows[pl.ds(pl.multiple_of(at * pair, 8), pair), :]
    wide = spec.shape[1]
    wave_x = jnp.broadcast_to(wave_x_ref[0:1, :], (kz_len, wide))
    wave_z = wave_z_ref[...]
    wave_y = wave_y_ref[at]
    even_x = lax.broadcasted_iota(jnp.int32, (kz_len, wide), 1) % 2 == 0
    even_z = lax.broadcasted_iota(jnp.int32, (kz_len, wide), 0) % 2 == 0

    def slope_x(value):
        return jnp.where(even_x, turn(value, -1), -turn(value, 1)) * wave_x

    def slope_z(value):
        return (
            jnp.where(
                even_z,
                pltpu.roll(value, kz_len - 1, axis=0),
                -pltpu.roll(value, 1, axis=0),
            )
            * wave_z
        )

    s = [
        [spec[(y * 3 + c) * kz_len : (y * 3 + c + 1) * kz_len] for c in range(3)] for y in range(2)
    ]
    square = wave_x * wave_x + wave_z * wave_z + wave_y * wave_y
    positive = square > 0
    safe = jnp.where(positive, square, 1.0)
    potential = []
    for y in range(2):
        along_y = s[1 - y][1] * (wave_y if y == 0 else -wave_y)
        divergence = slope_x(s[y][0]) + along_y + slope_z(s[y][2])
        potential.append(jnp.where(positive, divergence / safe, 0.0))
    for y in range(2):
        along_y = potential[1 - y] * (wave_y if y == 0 else -wave_y)
        found = [
            s[y][0] + slope_x(potential[y]),
            s[y][1] + along_y,
            s[y][2] + slope_z(potential[y]),
        ]
        for comp in range(3):
            out_ref[comp, y] = (found[comp] * scale)[:, :modes]


def last(own, other, wave_y, wave_x, wave_z, ky_len, kz_len, scale):
    modes, lanes = own.shape
    return pl.pallas_call(
        functools.partial(last_kernel, (kz_len, modes, scale)),
        grid=(ky_len // 2,),
        in_specs=[SMEM, *[whole(a) for a in (own, other, wave_x, wave_z)]],
        out_specs=pl.BlockSpec((3, 2, kz_len, modes), lambda i: (0, i, 0, 0)),
        out_shape=jax.ShapeDtypeStruct((3, ky_len, kz_len, modes), F32),
        scratch_shapes=[pltpu.VMEM((lanes, wave_x.shape[1]), F32)],
        compiler_params=params(),
        cost_estimate=SHORT,
        name="last_projection",
    )(wave_y, own, other, wave_x, wave_z)


def after(value, *earlier_values):
    return lax.optimization_barrier((value, earlier_values))[0]


def shards(new_velocity, stored_velocity, stored_vorticity):
    rows = lax.axis_size("row")
    cols = lax.axis_size("col")
    _, ky_len, kz_own, modes = new_velocity.shape
    orders, _, x_len, y_len, grid_len = stored_velocity.shape
    kz_len = round_up(kz_own, 8)
    kmax = modes // 2 - 1
    xc = min(XC, x_len)
    chunks = x_len // xc
    pack = LANES // y_len
    packs = xc // pack
    wide = round_up(modes, LANES)
    group = 5 * kz_len
    lanes = round_up(ky_len * group, 256)

    basis = synth_np(grid_len, modes)
    slope = slope_np(basis, kmax)
    y_order = (np.arange(rows)[None, :] * ky_len + np.arange(ky_len)[:, None]).reshape(-1)

    groups = rows // 2
    place = jnp.stack([lax.axis_index("row") // 2, lax.axis_index("row") % 2]).astype(jnp.int32)

    def own_table(tables, axis):
        return lax.dynamic_index_in_dim(jnp.asarray(np.stack(tables)), lax.axis_index(axis), 0, False)

    def x_points(row):
        owner = np.array([row ^ (2 * k) for k in range(groups)])
        return (
            owner[None, :, None] * x_len
            + np.arange(chunks)[:, None, None] * xc
            + np.arange(xc)[None, None, :]
        ).reshape(-1)

    def halves_of(plain, sloped):
        return np.stack([part for table in (plain, sloped) for part in halves(table)])

    def y_table(col):
        points = np.concatenate([(col ^ k) * y_len + np.arange(y_len) for k in range(cols)])
        return halves_of(basis[points].T[y_order], slope[points].T[y_order])

    def z_table(col):
        def spread(table):
            parts = table.T.reshape(cols, kz_own, grid_len)[[col ^ k for k in range(cols)]]
            parts = np.pad(parts, ((0, 0), (0, kz_len - kz_own), (0, 0)))
            return parts.reshape(cols * kz_len, grid_len)

        return halves_of(spread(basis), spread(slope))

    def x_table(row):
        points = np.pad(basis[x_points(row)], ((0, 0), (0, wide - modes)))
        return np.concatenate(halves(points), axis=0)

    table_x = own_table([x_table(row) for row in range(rows)], "row")
    table_x_back = own_table(
        [np.stack(halves(basis[x_points(row)].T)) for row in range(rows)], "row"
    )
    table_y = own_table([y_table(col) for col in range(cols)], "col")
    table_z = own_table([z_table(col) for col in range(cols)], "col")

    def wave_of(index):
        return (index // 2).astype(F32) / kmax

    mode = jnp.arange(wide, dtype=jnp.int32)
    wave_x = jnp.broadcast_to(jnp.where(mode < modes, wave_of(mode), 0.0)[None, :], (8, wide))
    ky_first = lax.axis_index("row") * ky_len + 2 * jnp.arange(ky_len // 2, dtype=jnp.int32)
    wave_y = wave_of(ky_first)
    kz = lax.axis_index("col") * kz_own + jnp.arange(kz_len, dtype=jnp.int32)
    wave_z = jnp.broadcast_to(wave_of(kz)[:, None], (kz_len, wide))

    coeffs = new_velocity
    if kz_len > kz_own:
        coeffs = jnp.pad(coeffs, ((0, 0), (0, 0), (0, kz_len - kz_own), (0, 0)))

    def exchange(values, axis, shift, size):
        return [
            lax.ppermute(value, axis, [(src, src ^ (k << shift)) for src in range(size)]) if k else value
            for k, value in enumerate(values)
        ]

    def core_swap(value):
        return lax.ppermute(value, "row", [(src, src ^ 1) for src in range(rows)])

    dims = (rows, xc, ky_len, kz_len, cols, y_len, pack)
    sent = first_synth(
        place, coeffs, core_swap(coeffs), table_x, wave_x, (chunks, groups, xc), lanes
    )
    latest = sent[0][0]

    def ordered(kernel, operands, *others):
        nonlocal latest
        operands = after(operands, latest)
        found = kernel(operands, *others)
        latest = found[0] if isinstance(found, (list, tuple)) else found
        return found

    stored = (stored_velocity, stored_vorticity)

    def run_earlier(chunk):
        return ordered(lambda values: earlier(*values, chunk, xc, pack), stored)

    first, second, middle, back, base = {}, {}, {}, {}, {}
    for chunk in range(chunks):
        values = sent[chunk]
        if chunk:
            values = [values[0]] + [
                after(value, first[chunk - 1][k]) for k, value in enumerate(values) if k
            ]
        first[chunk] = exchange(values, "row", 1, rows)
    base[0] = run_earlier(0)
    for step in range(chunks + 2):
        if step + 1 < chunks:
            base[step + 1] = run_earlier(step + 1)
        if step < chunks:
            found = ordered(lambda values: second_synth(place, values, table_y, dims), first[step])
            second[step] = exchange(found, "col", 0, cols)
        at = step - 1
        if 0 <= at < chunks:
            found = ordered(
                lambda values: third(values, *stored, base[at], table_z, at, dims[3:]), second[at]
            )
            middle[at] = exchange(found, "col", 0, cols)
        at = step - 2
        if 0 <= at < chunks:
            values = middle[at]
            if at:
                values = after(values, back[at - 1])
            found = ordered(lambda values: second_back(place, values, table_y, dims), values)
            back[at] = exchange(found, "row", 1, rows)
    parts = [value for chunk in range(chunks) for value in back[chunk]]
    away = first_back(place, parts, table_x_back, xc, False)
    home = first_back(place, after(parts, away), table_x_back, xc, True)
    result = last(home, core_swap(away), wave_y, wave_x, wave_z, ky_len, kz_len, 1.0 / (orders + 1))
    return result[:, :, :kz_own] if kz_len > kz_own else result


def solution(mesh):
    return jax.shard_map(
        shards,
        mesh=mesh,
        in_specs=(
            P(None, "row", "col", None),
            P(None, None, "row", "col", None),
            P(None, None, "row", "col", None),
        ),
        out_specs=P(None, "row", "col", None),
        check_vma=False,
    )
```

```python
import functools
import math

import jax
import jax.numpy as jnp
import ml_dtypes
import numpy as np
from jax import lax
from jax.experimental import pallas as pl
from jax.experimental.pallas import tpu as pltpu
from jax.sharding import PartitionSpec as P

LANES = 128
XC = 8
BF16 = jnp.bfloat16
F32 = jnp.float32
NN = (((1,), (0,)), ((), ()))
NT = (((1,), (1,)), ((), ()))


def round_up(value, step):
    return -(-value // step) * step


def synth_np(grid_len, mode_count):
    points = np.arange(grid_len)[:, None]
    mode_index = np.arange(mode_count)[None, :]
    wave_index = np.where(mode_index == 1, grid_len // 2, mode_index // 2)
    angles = (points * wave_index % grid_len) * (2.0 * math.pi / grid_len)
    trig = np.where((mode_index % 2 == 0) | (mode_index == 1), np.cos(angles), np.sin(angles))
    weight = np.where(mode_index < 2, 1.0, 2.0) / grid_len
    return np.where(mode_index == 1, 0.0, trig * np.sqrt(weight))


def slope_np(table, kmax):
    paired = table.reshape(table.shape[0], -1, 2)
    wavenum = np.arange(paired.shape[1]) / kmax
    return np.stack([-wavenum * paired[:, :, 1], wavenum * paired[:, :, 0]], -1).reshape(table.shape)


def halves(table):
    high = table.astype(ml_dtypes.bfloat16)
    low = (table - high.astype(np.float64)).astype(ml_dtypes.bfloat16)
    return high, low


def pieces_of(values):
    high = values.astype(BF16)
    return high, (values - high.astype(F32)).astype(BF16)


def dot(left, right, dims):
    return lax.dot_general(left, right, dims, preferred_element_type=F32)


def dot_data_left(values, high, low, dims=NN):
    top, rest = pieces_of(values)
    return dot(top, high, dims) + (dot(top, low, dims) + dot(rest, high, dims))


def dot_data_right(high, low, values, dims=NT):
    top, rest = pieces_of(values)
    return dot(high, top, dims) + (dot(low, top, dims) + dot(high, rest, dims))


def turn(values, shift):
    shift = shift % values.shape[-1]
    return values if shift == 0 else pltpu.roll(values, shift, axis=values.ndim - 1)


def lane_pack(parts, width, source_lane=0):
    tiles = []
    lane = lax.broadcasted_iota(jnp.int32, parts[0].shape, 1)
    for tile in range(-(-len(parts) * width // LANES)):
        start = tile * LANES
        acc = None
        for idx in range(start // width, min(len(parts) - 1, (start + LANES - 1) // width) + 1):
            moved = turn(parts[idx], idx * width - source_lane)
            acc = moved if acc is None else jnp.where(lane >= idx * width - start, moved, acc)
        tiles.append(acc)
    return tiles


VMEM_LIMIT = 24 * 1024 * 1024
SHORT = pl.CostEstimate(flops=1024, bytes_accessed=1024, transcendentals=0)
HBM = pl.BlockSpec(memory_space=pl.ANY)
SMEM = pl.BlockSpec(memory_space=pltpu.SMEM)
VMEM = pl.BlockSpec(memory_space=pltpu.VMEM)


def params():
    return pltpu.CompilerParams(dimension_semantics=("arbitrary",), vmem_limit_bytes=VMEM_LIMIT)


def still():
    return pltpu.CompilerParams(vmem_limit_bytes=VMEM_LIMIT)


def both_passes(values, high_low, high):
    top, rest = pieces_of(values)
    wide = dot(top, high_low, NN)
    half = high.shape[1]
    return wide[:, :half] + (wide[:, half:] + dot(rest, high, NN))


def whole(array):
    rank = len(array.shape)
    return pl.BlockSpec(array.shape, lambda *_: (0,) * rank)


def first_synth_kernel(dims, place_ref, own_ref, other_ref, table_ref, *rest):
    chunks, dests, xc = dims
    outs = rest[: chunks * dests]
    own_data, other_data, rows, sem = rest[chunks * dests :]
    _, ky_len, kz_len, _ = own_data.shape
    group = 5 * kz_len
    half = rows.shape[0] // 2
    copies = [
        pltpu.make_async_copy(ref.at[comp], data.at[comp], sem.at[side, comp])
        for side, (ref, data) in enumerate(((own_ref, own_data), (other_ref, other_data)))
        for comp in range(3)
    ]
    for copy in copies:
        copy.start()
    if ky_len * group < half:
        for core in range(2):
            rows[core * half + ky_len * group : (core + 1) * half, :] = jnp.zeros(
                (half - ky_len * group, LANES), F32
            )
    plain = jnp.concatenate([table_ref[0], table_ref[1]], axis=1)
    slope = jnp.concatenate([table_ref[2], table_ref[3]], axis=1)
    step = 4 if ky_len % 4 == 0 else 2

    for side, data in enumerate((own_data, other_data)):
        for copy in copies[3 * side : 3 * side + 3]:
            copy.wait()
        core = place_ref[1] if side == 0 else 1 - place_ref[1]

        def body(idx, carry):
            first = idx * step
            lines = [[data[comp, first + k] for comp in range(3)] for k in range(step)]
            found = both_passes(
                jnp.concatenate([v for line in lines for v in line], axis=0), plain, table_ref[0]
            )
            sloped = both_passes(
                jnp.concatenate([v for line in lines for v in line[1:]], axis=0), slope, table_ref[2]
            )
            for k in range(step):
                base = core * half + (first + k) * group
                rows[pl.ds(pl.multiple_of(base, 8), 3 * kz_len), :] = found[
                    3 * k * kz_len : 3 * (k + 1) * kz_len
                ]
                rows[pl.ds(pl.multiple_of(base + 3 * kz_len, 8), 2 * kz_len), :] = sloped[
                    2 * k * kz_len : 2 * (k + 1) * kz_len
                ]
            return carry

        lax.fori_loop(0, ky_len // step, body, 0)

    def flip(tile, carry):
        found = rows[pl.ds(pl.multiple_of(tile * LANES, LANES), LANES), :].T
        for idx, out in enumerate(outs):
            out[pl.ds(pl.multiple_of(tile * xc, 8), xc), :] = found[idx * xc : (idx + 1) * xc]
        return carry

    lax.fori_loop(0, 2 * half // LANES, flip, 0, unroll=2)


def first_synth(place, own, other, table, dims, lanes):
    chunks, dests, xc = dims
    out = jax.ShapeDtypeStruct((2 * lanes // LANES * xc, LANES), F32)
    found = pl.pallas_call(
        functools.partial(first_synth_kernel, dims),
        in_specs=[SMEM, HBM, HBM, VMEM],
        out_specs=[VMEM] * (chunks * dests),
        out_shape=[out] * (chunks * dests),
        scratch_shapes=[
            pltpu.VMEM(own.shape, F32),
            pltpu.VMEM(own.shape, F32),
            pltpu.VMEM((2 * lanes, LANES), F32),
            pltpu.SemaphoreType.DMA((2, 3)),
        ],
        compiler_params=still(),
        cost_estimate=SHORT,
        name="first_synth",
    )(place, own, other, table)
    return [list(found[k * dests : (k + 1) * dests]) for k in range(chunks)]


def second_synth_kernel(dims, place_ref, *refs):
    rows, xc, ky_len, kz_len, cols, y_len, pack = dims
    groups = rows // 2
    parts, table_ref, out_ref, a_ref = refs[:groups], refs[groups], refs[groups + 1], refs[groups + 2]
    size = a_ref.shape[0] // groups
    for k, part in enumerate(parts):
        a_ref[pl.ds(pl.multiple_of((place_ref[0] ^ k) * size, 8), size), :] = part[...]
    group = 5 * kz_len
    wide = round_up(group, LANES)
    tiles = a_ref.shape[0] // (rows * xc)

    def body(at, carry):
        turned = []
        for part in range(pack):
            line = [
                a_ref[pl.ds(tile * xc + at * pack + part, rows, stride=tiles * xc), :]
                for tile in range(tiles)
            ]
            found = []
            for ky in range(ky_len):
                start = ky * group
                low, off = divmod(start, LANES)
                window = line[low : low + (wide // LANES) + (1 if off else 0)]
                found.append(turn(jnp.concatenate(window, axis=1), -off)[:, :wide])
            turned.append(jnp.concatenate(found, axis=0).T[:group])
        plain = dot_data_left(jnp.concatenate(turned, axis=0), table_ref[0], table_ref[1])
        slope_in = [t[c * kz_len : (c + 1) * kz_len] for t in turned for c in (0, 2)]
        slope = dot_data_left(jnp.concatenate(slope_in, axis=0), table_ref[2], table_ref[3])
        fields = []
        for part in range(pack):
            own = plain[part * group : (part + 1) * group]
            sl = slope[part * 2 * kz_len : (part + 1) * 2 * kz_len]
            fields.append(
                jnp.concatenate(
                    [
                        own[: 3 * kz_len],
                        own[3 * kz_len : 4 * kz_len] - sl[:kz_len],
                        sl[kz_len:],
                        -own[4 * kz_len :],
                    ],
                    axis=0,
                )
            )
        for dest in range(cols):
            tile, off = divmod(dest * y_len, LANES)
            out_ref[place_ref[2] ^ dest, at] = lane_pack(
                [f[:, tile * LANES : (tile + 1) * LANES] for f in fields], y_len, off
            )[0]
        return carry

    lax.fori_loop(0, xc // pack, body, 0)


def second_synth(place, arrived, table, dims):
    rows, xc, ky_len, kz_len, cols, y_len, pack = dims
    packs = xc // pack
    return pl.pallas_call(
        functools.partial(second_synth_kernel, dims),
        in_specs=[SMEM] + [VMEM] * (len(arrived) + 1),
        out_specs=VMEM,
        out_shape=jax.ShapeDtypeStruct((cols, packs, 6 * kz_len, LANES), F32),
        scratch_shapes=[pltpu.VMEM((len(arrived) * arrived[0].shape[0], LANES), F32)],
        compiler_params=still(),
        cost_estimate=SHORT,
        name="second_synth",
    )(place, *arrived, table)


def cross(left, right):
    return [
        left[1] * right[2] - left[2] * right[1],
        left[2] * right[0] - left[0] * right[2],
        left[0] * right[1] - left[1] * right[0],
    ]


def earlier_kernel(count, *refs):
    vels, vorts, out_ref = refs[:count], refs[count : 2 * count], refs[2 * count]
    pack, y_len = out_ref.shape[1:3]
    for part in range(pack):
        def body(step, carry):
            at = pl.ds(pl.multiple_of(step * 8, 8), 8)
            total = None
            for vel, vort in zip(vels, vorts):
                term = cross(
                    [vel[0, c, part, at, :] for c in range(3)],
                    [vort[0, c, part, at, :] for c in range(3)],
                )
                total = term if total is None else [a + b for a, b in zip(total, term)]
            for comp in range(3):
                out_ref[comp, part, at, :] = total[comp]
            return carry

        lax.fori_loop(0, y_len // 8, body, 0, unroll=2)


def earlier(velocity, vorticity, chunk, xc, pack):
    orders, _, _, y_len, grid_len = velocity.shape
    packs = xc // pack
    block = (1, 3, pack, y_len, grid_len)

    def at(order):
        return pl.BlockSpec(block, lambda i: (order, 0, chunk * packs + i, 0, 0))

    specs = [at(k) for k in range(1, orders)] + [at(orders - k) for k in range(1, orders)]
    size = xc * y_len * grid_len
    return pl.pallas_call(
        functools.partial(earlier_kernel, orders - 1),
        grid=(packs,),
        in_specs=specs,
        out_specs=pl.BlockSpec((3, pack, y_len, grid_len), lambda i: (0, i, 0, 0)),
        out_shape=jax.ShapeDtypeStruct((3, xc, y_len, grid_len), F32),
        compiler_params=params(),
        cost_estimate=SHORT,
        name="earlier_orders",
    )(*[velocity] * (orders - 1), *[vorticity] * (orders - 1))


def third_kernel(dims, place_ref, *refs):
    chunk, kz_len, cols, y_len, pack = dims
    b_ref, stored_refs = refs[0], refs[1:4]
    table_ref, out_ref, data, sem = refs[4:]
    grid_len = table_ref.shape[2]
    xc = data.shape[2]
    packs = xc // pack

    def copies(at):
        spot = pl.ds(at * pack, pack)
        far = pl.ds(chunk * xc + at * pack, pack)
        sources = [ref.at[0, :, far] for ref in stored_refs[:2]] + [stored_refs[2].at[:, spot]]
        return [
            pltpu.make_async_copy(source, data.at[idx, :, spot], sem.at[idx, at])
            for idx, source in enumerate(sources)
        ]

    for at in range(packs):
        for copy in copies(at):
            copy.start()

    def body(at, carry):
        def stack(field):
            return jnp.concatenate(
                [
                    b_ref[place_ref[2] ^ k, at, field * kz_len : (field + 1) * kz_len, :]
                    for k in range(cols)
                ],
                axis=0,
            ).T

        lines = jnp.concatenate([stack(field) for field in range(6)], axis=0)
        plain = dot_data_left(lines, table_ref[0], table_ref[1])
        slope = dot_data_left(lines[: 2 * LANES], table_ref[2], table_ref[3])
        new = [plain[f * LANES : (f + 1) * LANES] for f in range(6)]
        vel_new = new[:3]
        vort_new = [new[4] - slope[LANES:], slope[:LANES] + new[5], new[3]]
        for copy in copies(at):
            copy.wait()
        spot = pl.ds(at * pack, pack)
        flat = (pack * y_len, grid_len)
        vel, vort, base = [[data[idx, c, spot].reshape(flat) for c in range(3)] for idx in range(3)]
        one, two = cross(vel_new, vort), cross(vel, vort_new)
        total = [one[c] + two[c] + base[c] for c in range(3)]
        result = dot_data_right(table_ref[0], table_ref[1], jnp.concatenate(total, axis=0))
        for k in range(cols):
            for comp in range(3):
                out_ref[place_ref[2] ^ k, at, comp * kz_len : (comp + 1) * kz_len, :] = result[
                    k * kz_len : (k + 1) * kz_len, comp * LANES : (comp + 1) * LANES
                ]
        return carry

    lax.fori_loop(0, packs, body, 0)


def third(place, arrived, velocity, vorticity, base, table, chunk, dims):
    kz_len, cols, y_len, pack = dims
    packs = arrived.shape[1]
    grid_len = velocity.shape[-1]
    return pl.pallas_call(
        functools.partial(third_kernel, (chunk, *dims)),
        in_specs=[SMEM, VMEM] + [HBM] * 3 + [VMEM],
        out_specs=VMEM,
        out_shape=jax.ShapeDtypeStruct((cols, packs, 3 * kz_len, LANES), F32),
        scratch_shapes=[
            pltpu.VMEM((3, 3, packs * pack, y_len, grid_len), F32),
            pltpu.SemaphoreType.DMA((3, packs)),
        ],
        compiler_params=still(),
        cost_estimate=SHORT,
        name="third_dimension",
    )(place, arrived, velocity, vorticity, base, table)


def second_back_kernel(dims, place_ref, c_ref, table_ref, *refs):
    rows, xc, ky_len, kz_len, cols, y_len, pack = dims
    outs, all_ref = refs[:-1], refs[-1]
    width = 3 * kz_len
    high_pad = round_up(width, LANES)

    def body(at, carry):
        lines = []
        for part in range(pack):
            tiles = lane_pack(
                [c_ref[place_ref[2] ^ k, at] for k in range(cols)], y_len, part * y_len
            )
            lines.append(jnp.concatenate(tiles, axis=1))
            if high_pad > width:
                lines.append(jnp.zeros((high_pad - width, cols * y_len), F32))
        result = dot_data_right(table_ref[0], table_ref[1], jnp.concatenate(lines, axis=0))
        for part in range(pack):
            own = result[:, part * high_pad : (part + 1) * high_pad]
            tiles = lane_pack([own[ky * rows : (ky + 1) * rows] for ky in range(ky_len)], width)
            for idx, tile in enumerate(tiles):
                spot = idx * xc + at * pack + part
                all_ref[pl.ds(spot, rows, stride=len(tiles) * xc), :] = tile
        return carry

    lax.fori_loop(0, xc // pack, body, 0)
    size = all_ref.shape[0] // len(outs)
    for k, out in enumerate(outs):
        out[...] = all_ref[pl.ds(pl.multiple_of((place_ref[0] ^ k) * size, 8), size), :]


def second_back(place, arrived, table, dims):
    rows, xc, ky_len, kz_len, cols, y_len, pack = dims
    size = round_up(ky_len * 3 * kz_len, LANES) // LANES * xc
    groups = rows // 2
    return pl.pallas_call(
        functools.partial(second_back_kernel, dims),
        in_specs=[SMEM, VMEM, VMEM],
        out_specs=[VMEM] * groups,
        out_shape=[jax.ShapeDtypeStruct((2 * size, LANES), F32)] * groups,
        scratch_shapes=[pltpu.VMEM((rows * size, LANES), F32)],
        compiler_params=still(),
        cost_estimate=SHORT,
        name="second_back",
    )(place, arrived, table)


def first_back_kernel(dims, place_ref, *refs):
    count, xc, own = dims
    parts, table_ref, out_ref = refs[:count], refs[count], refs[count + 1]
    size = parts[0].shape[0] // 2
    core = place_ref[1] if own else 1 - place_ref[1]
    for tile in range(size // xc):
        spot = pl.ds(pl.multiple_of(core * size + tile * xc, 8), xc)
        found = jnp.concatenate([part[spot, :] for part in parts], axis=0)
        out_ref[:, tile * LANES : (tile + 1) * LANES] = dot_data_right(
            table_ref[0], table_ref[1], found, NN
        )


def first_back(place, parts, table, xc, own):
    count = len(parts)
    size = parts[0].shape[0] // 2
    return pl.pallas_call(
        functools.partial(first_back_kernel, (count, xc, own)),
        in_specs=[SMEM] + [VMEM] * (count + 1),
        out_specs=VMEM,
        out_shape=jax.ShapeDtypeStruct((table.shape[1], size // xc * LANES), F32),
        compiler_params=still(),
        cost_estimate=SHORT,
        name="first_back",
    )(place, *parts, table)


def last_kernel(dims, *refs):
    kz_len, modes, scale = dims
    wave_y_ref, own_ref, other_ref, wave_x_ref, wave_z_ref, out_ref, rows = refs
    pair = 2 * 3 * kz_len
    at = pl.program_id(0)

    @pl.when(at == 0)
    def _():
        for tile in range(rows.shape[0] // LANES):
            lanes = slice(tile * LANES, (tile + 1) * LANES)
            rows[lanes, 0:modes] = (own_ref[:, lanes] + other_ref[:, lanes]).T

    spec = rows[pl.ds(pl.multiple_of(at * pair, 8), pair), :]
    wide = spec.shape[1]
    wave_x = jnp.broadcast_to(wave_x_ref[0:1, :], (kz_len, wide))
    wave_z = wave_z_ref[...]
    wave_y = wave_y_ref[at]
    even_x = lax.broadcasted_iota(jnp.int32, (kz_len, wide), 1) % 2 == 0
    even_z = lax.broadcasted_iota(jnp.int32, (kz_len, wide), 0) % 2 == 0

    def slope_x(value):
        return jnp.where(even_x, turn(value, -1), -turn(value, 1)) * wave_x

    def slope_z(value):
        return (
            jnp.where(
                even_z,
                pltpu.roll(value, kz_len - 1, axis=0),
                -pltpu.roll(value, 1, axis=0),
            )
            * wave_z
        )

    s = [
        [spec[(y * 3 + c) * kz_len : (y * 3 + c + 1) * kz_len] for c in range(3)] for y in range(2)
    ]
    square = wave_x * wave_x + wave_z * wave_z + wave_y * wave_y
    positive = square > 0
    safe = jnp.where(positive, square, 1.0)
    potential = []
    for y in range(2):
        along_y = s[1 - y][1] * (wave_y if y == 0 else -wave_y)
        divergence = slope_x(s[y][0]) + along_y + slope_z(s[y][2])
        potential.append(jnp.where(positive, divergence / safe, 0.0))
    for y in range(2):
        along_y = potential[1 - y] * (wave_y if y == 0 else -wave_y)
        found = [
            s[y][0] + slope_x(potential[y]),
            s[y][1] + along_y,
            s[y][2] + slope_z(potential[y]),
        ]
        for comp in range(3):
            out_ref[comp, y] = (found[comp] * scale)[:, :modes]


def last(own, other, wave_y, wave_x, wave_z, ky_len, kz_len, scale):
    modes, lanes = own.shape
    return pl.pallas_call(
        functools.partial(last_kernel, (kz_len, modes, scale)),
        grid=(ky_len // 2,),
        in_specs=[SMEM, *[whole(a) for a in (own, other, wave_x, wave_z)]],
        out_specs=pl.BlockSpec((3, 2, kz_len, modes), lambda i: (0, i, 0, 0)),
        out_shape=jax.ShapeDtypeStruct((3, ky_len, kz_len, modes), F32),
        scratch_shapes=[pltpu.VMEM((lanes, wave_x.shape[1]), F32)],
        compiler_params=params(),
        cost_estimate=SHORT,
        name="last_projection",
    )(wave_y, own, other, wave_x, wave_z)


def after(value, *earlier_values):
    return lax.optimization_barrier((value, earlier_values))[0]


def shards(new_velocity, stored_velocity, stored_vorticity):
    rows = lax.axis_size("row")
    cols = lax.axis_size("col")
    _, ky_len, kz_own, modes = new_velocity.shape
    orders, _, x_len, y_len, grid_len = stored_velocity.shape
    kz_len = round_up(kz_own, 8)
    kmax = modes // 2 - 1
    xc = min(XC, x_len)
    chunks = x_len // xc
    pack = LANES // y_len
    packs = xc // pack
    wide = round_up(modes, LANES)
    group = 5 * kz_len
    lanes = round_up(ky_len * group, 256)

    basis = synth_np(grid_len, modes)
    slope = slope_np(basis, kmax)
    y_order = (np.arange(rows)[None, :] * ky_len + np.arange(ky_len)[:, None]).reshape(-1)

    groups = rows // 2
    row, col = lax.axis_index("row"), lax.axis_index("col")
    place = jnp.stack([row // 2, row % 2, col]).astype(jnp.int32)

    def own_table(tables, axis):
        return lax.dynamic_index_in_dim(jnp.asarray(np.stack(tables)), lax.axis_index(axis), 0, False)

    def x_points(row):
        owner = np.array([row ^ (2 * k) for k in range(groups)])
        return (
            owner[None, :, None] * x_len
            + np.arange(chunks)[:, None, None] * xc
            + np.arange(xc)[None, None, :]
        ).reshape(-1)

    def halves_of(plain, sloped):
        return np.stack([part for table in (plain, sloped) for part in halves(table)])

    def y_table(col):
        points = np.concatenate([(col ^ k) * y_len + np.arange(y_len) for k in range(cols)])
        return halves_of(basis[points].T[y_order], slope[points].T[y_order])

    def z_table(col):
        def spread(table):
            parts = table.T.reshape(cols, kz_own, grid_len)[[col ^ k for k in range(cols)]]
            parts = np.pad(parts, ((0, 0), (0, kz_len - kz_own), (0, 0)))
            return parts.reshape(cols * kz_len, grid_len)

        return halves_of(spread(basis), spread(slope))

    table_x = own_table(
        [halves_of(basis[x_points(row)].T, slope[x_points(row)].T) for row in range(rows)], "row"
    )
    table_y = own_table([y_table(col) for col in range(cols)], "col")
    table_z = own_table([z_table(col) for col in range(cols)], "col")

    def wave_of(index):
        return (index // 2).astype(F32) / kmax

    mode = jnp.arange(wide, dtype=jnp.int32)
    wave_x = jnp.broadcast_to(jnp.where(mode < modes, wave_of(mode), 0.0)[None, :], (8, wide))
    ky_first = lax.axis_index("row") * ky_len + 2 * jnp.arange(ky_len // 2, dtype=jnp.int32)
    wave_y = wave_of(ky_first)
    kz = lax.axis_index("col") * kz_own + jnp.arange(kz_len, dtype=jnp.int32)
    wave_z = jnp.broadcast_to(wave_of(kz)[:, None], (kz_len, wide))

    coeffs = new_velocity
    if kz_len > kz_own:
        coeffs = jnp.pad(coeffs, ((0, 0), (0, 0), (0, kz_len - kz_own), (0, 0)))

    def col_swap(value):
        return lax.all_to_all(value, "col", split_axis=0, concat_axis=0, tiled=True)

    def core_swap(value):
        return lax.ppermute(value, "row", [(src, src ^ 1) for src in range(rows)])

    dims = (rows, xc, ky_len, kz_len, cols, y_len, pack)
    sent = first_synth(place, coeffs, core_swap(coeffs), table_x, (chunks, groups, xc), lanes)
    latest = sent[0][0]

    def ordered(kernel, operands, *others):
        nonlocal latest
        operands = after(operands, latest)
        found = kernel(operands, *others)
        latest = found[0] if isinstance(found, (list, tuple)) else found
        return found

    stored = (stored_velocity, stored_vorticity)

    def run_earlier(chunk):
        return ordered(lambda values: earlier(*values, chunk, xc, pack), stored)

    def z_exchange(values, *gates):
        found = [values[0]]
        for k in range(1, groups):
            value = after(values[k], *gates) if gates else values[k]
            found.append(lax.ppermute(value, "row", [(src, src ^ (2 * k)) for src in range(rows)]))
        return found

    first, second, middle, back, base = {}, {}, {}, {}, {}
    first[0] = z_exchange(sent[0])
    for chunk in range(min(2, chunks)):
        base[chunk] = run_earlier(chunk)
    z_last = first[0]
    for step in range(chunks + 2):
        if step + 1 < chunks:
            z_last = first[step + 1] = z_exchange(sent[step + 1], z_last)
        if step < chunks:
            found = ordered(lambda values: second_synth(place, values, table_y, dims), first[step])
            second[step] = col_swap(found)
        at = step - 1
        if 0 <= at < chunks:
            found = ordered(
                lambda values: third(place, values, *stored, base[at], table_z, at, dims[3:]),
                second[at],
            )
            middle[at] = col_swap(found)
        if step + 2 < chunks:
            base[step + 2] = run_earlier(step + 2)
        at = step - 2
        if 0 <= at < chunks:
            found = ordered(lambda values: second_back(place, values, table_y, dims), middle[at])
            z_last = back[at] = z_exchange(found, z_last)
    parts = [value for chunk in range(chunks) for value in back[chunk]]
    away = first_back(place, parts, table_x, xc, False)
    home = first_back(place, parts, after(table_x, away), xc, True)
    result = last(home, core_swap(away), wave_y, wave_x, wave_z, ky_len, kz_len, 1.0 / (orders + 1))
    return result[:, :, :kz_own] if kz_len > kz_own else result


def solution(mesh):
    return jax.shard_map(
        shards,
        mesh=mesh,
        in_specs=(
            P(None, "row", "col", None),
            P(None, None, "row", "col", None),
            P(None, None, "row", "col", None),
        ),
        out_specs=P(None, "row", "col", None),
        check_vma=False,
    )
```

```python
import functools
import math

import jax
import jax.numpy as jnp
import ml_dtypes
import numpy as np
from jax import lax
from jax.experimental import pallas as pl
from jax.experimental.pallas import tpu as pltpu
from jax.sharding import PartitionSpec as P

LANES = 128
XC = 16
BF16 = jnp.bfloat16
F32 = jnp.float32
NN = (((1,), (0,)), ((), ()))
NT = (((1,), (1,)), ((), ()))


def round_up(value, step):
    return -(-value // step) * step


def synth_np(grid_len, mode_count):
    points = np.arange(grid_len)[:, None]
    mode_index = np.arange(mode_count)[None, :]
    wave_index = np.where(mode_index == 1, grid_len // 2, mode_index // 2)
    angles = (points * wave_index % grid_len) * (2.0 * math.pi / grid_len)
    trig = np.where((mode_index % 2 == 0) | (mode_index == 1), np.cos(angles), np.sin(angles))
    weight = np.where(mode_index < 2, 1.0, 2.0) / grid_len
    return np.where(mode_index == 1, 0.0, trig * np.sqrt(weight))


def slope_np(table, kmax):
    paired = table.reshape(table.shape[0], -1, 2)
    wavenum = np.arange(paired.shape[1]) / kmax
    return np.stack([-wavenum * paired[:, :, 1], wavenum * paired[:, :, 0]], -1).reshape(table.shape)


def halves(table):
    high = table.astype(ml_dtypes.bfloat16)
    low = (table - high.astype(np.float64)).astype(ml_dtypes.bfloat16)
    return high, low


def pieces_of(values):
    high = values.astype(BF16)
    return high, (values - high.astype(F32)).astype(BF16)


def dot(left, right, dims):
    return lax.dot_general(left, right, dims, preferred_element_type=F32)


def dot_data_left(values, high, low, dims=NN):
    top, rest = pieces_of(values)
    return dot(top, high, dims) + (dot(top, low, dims) + dot(rest, high, dims))


def dot_data_right(high, low, values, dims=NT):
    top, rest = pieces_of(values)
    return dot(high, top, dims) + (dot(low, top, dims) + dot(high, rest, dims))


def turn(values, shift):
    shift = shift % values.shape[-1]
    return values if shift == 0 else pltpu.roll(values, shift, axis=values.ndim - 1)


def lane_pack(parts, width, source_lane=0):
    tiles = []
    lane = lax.broadcasted_iota(jnp.int32, parts[0].shape, 1)
    for tile in range(-(-len(parts) * width // LANES)):
        start = tile * LANES
        acc = None
        for idx in range(start // width, min(len(parts) - 1, (start + LANES - 1) // width) + 1):
            moved = turn(parts[idx], idx * width - source_lane)
            acc = moved if acc is None else jnp.where(lane >= idx * width - start, moved, acc)
        tiles.append(acc)
    return tiles


VMEM_LIMIT = 32 * 1024 * 1024
VMEM_MOST = 60 * 1024 * 1024
SHORT = pl.CostEstimate(flops=1024, bytes_accessed=1024, transcendentals=0)
ANY = pl.BlockSpec(memory_space=pl.ANY)
HBM = pl.BlockSpec(memory_space=pltpu.HBM)
SMEM = pl.BlockSpec(memory_space=pltpu.SMEM)
VMEM = pl.BlockSpec(memory_space=pltpu.VMEM)


def params():
    return pltpu.CompilerParams(dimension_semantics=("arbitrary",), vmem_limit_bytes=VMEM_LIMIT)


def still(limit=VMEM_LIMIT):
    return pltpu.CompilerParams(vmem_limit_bytes=limit)


def finish(held, out_refs, sem):
    for at in range(held.shape[1]):
        for k, out in enumerate(out_refs):
            pltpu.make_async_copy(held.at[k, at], out.at[at], sem.at[k, at]).wait()


def both_passes(values, high_low, high):
    top, rest = pieces_of(values)
    wide = dot(top, high_low, NN)
    half = high.shape[1]
    return wide[:, :half] + (wide[:, half:] + dot(rest, high, NN))


def whole(array):
    rank = len(array.shape)
    return pl.BlockSpec(array.shape, lambda *_: (0,) * rank)


def first_synth_kernel(dims, place_ref, own_ref, other_ref, table_ref, *rest):
    chunks, dests, xc = dims
    outs = rest[: chunks * dests]
    own_data, other_data, rows, held, sem, out_sem = rest[chunks * dests :]
    _, ky_len, kz_len, _ = own_data.shape
    group = 5 * kz_len
    half = rows.shape[0] // 2
    copies = [
        pltpu.make_async_copy(ref.at[comp], data.at[comp], sem.at[side, comp])
        for side, (ref, data) in enumerate(((own_ref, own_data), (other_ref, other_data)))
        for comp in range(3)
    ]
    for copy in copies:
        copy.start()
    if ky_len * group < half:
        for core in range(2):
            rows[core * half + ky_len * group : (core + 1) * half, :] = jnp.zeros(
                (half - ky_len * group, LANES), F32
            )
    plain = jnp.concatenate([table_ref[0], table_ref[1]], axis=1)
    slope = jnp.concatenate([table_ref[2], table_ref[3]], axis=1)
    step = 4 if ky_len % 4 == 0 else 2

    for side, data in enumerate((own_data, other_data)):
        for copy in copies[3 * side : 3 * side + 3]:
            copy.wait()
        core = place_ref[1] if side == 0 else 1 - place_ref[1]

        def body(idx, carry):
            first = idx * step
            lines = [[data[comp, first + k] for comp in range(3)] for k in range(step)]
            found = both_passes(
                jnp.concatenate([v for line in lines for v in line], axis=0), plain, table_ref[0]
            )
            sloped = both_passes(
                jnp.concatenate([v for line in lines for v in line[1:]], axis=0), slope, table_ref[2]
            )
            for k in range(step):
                base = core * half + (first + k) * group
                rows[pl.ds(pl.multiple_of(base, 8), 3 * kz_len), :] = found[
                    3 * k * kz_len : 3 * (k + 1) * kz_len
                ]
                rows[pl.ds(pl.multiple_of(base + 3 * kz_len, 8), 2 * kz_len), :] = sloped[
                    2 * k * kz_len : 2 * (k + 1) * kz_len
                ]
            return carry

        lax.fori_loop(0, ky_len // step, body, 0)

    def flip(tile, carry):
        found = rows[pl.ds(pl.multiple_of(tile * LANES, LANES), LANES), :].T
        for idx in range(chunks * dests):
            held[idx, pl.ds(pl.multiple_of(tile * xc, 8), xc), :] = found[idx * xc : (idx + 1) * xc]
        return carry

    lax.fori_loop(0, 2 * half // LANES, flip, 0, unroll=2)
    copies = [pltpu.make_async_copy(held.at[k], out, out_sem.at[k]) for k, out in enumerate(outs)]
    for copy in copies:
        copy.start()
    for copy in copies:
        copy.wait()


def first_synth(place, own, other, table, dims, lanes):
    chunks, dests, xc = dims
    out = jax.ShapeDtypeStruct((2 * lanes // LANES * xc, LANES), F32)
    found = pl.pallas_call(
        functools.partial(first_synth_kernel, dims),
        in_specs=[SMEM, ANY, ANY, VMEM],
        out_specs=[HBM] * (chunks * dests),
        out_shape=[out] * (chunks * dests),
        scratch_shapes=[
            pltpu.VMEM(own.shape, F32),
            pltpu.VMEM(own.shape, F32),
            pltpu.VMEM((2 * lanes, LANES), F32),
            pltpu.VMEM((chunks * dests, *out.shape), F32),
            pltpu.SemaphoreType.DMA((2, 3)),
            pltpu.SemaphoreType.DMA((chunks * dests,)),
        ],
        compiler_params=still(VMEM_MOST),
        cost_estimate=SHORT,
        name="first_synth",
    )(place, own, other, table)
    return [list(found[k * dests : (k + 1) * dests]) for k in range(chunks)]


def second_synth_kernel(dims, place_ref, *refs):
    rows, xc, ky_len, kz_len, cols, y_len, pack = dims
    groups = rows // 2
    parts, table_ref, out_refs = refs[:groups], refs[groups], refs[groups + 1 : -3]
    a_ref, held, sem = refs[-3:]
    size = a_ref.shape[0] // groups
    for k, part in enumerate(parts):
        a_ref[pl.ds(pl.multiple_of((place_ref[0] ^ k) * size, 8), size), :] = part[...]
    group = 5 * kz_len
    wide = round_up(group, LANES)
    tiles = a_ref.shape[0] // (rows * xc)

    def body(at, carry):
        turned = []
        for part in range(pack):
            line = [
                a_ref[pl.ds(tile * xc + at * pack + part, rows, stride=tiles * xc), :]
                for tile in range(tiles)
            ]
            found = []
            for ky in range(ky_len):
                start = ky * group
                low, off = divmod(start, LANES)
                window = line[low : low + (wide // LANES) + (1 if off else 0)]
                found.append(turn(jnp.concatenate(window, axis=1), -off)[:, :wide])
            turned.append(jnp.concatenate(found, axis=0).T[:group])
        plain = dot_data_left(jnp.concatenate(turned, axis=0), table_ref[0], table_ref[1])
        slope_in = [t[c * kz_len : (c + 1) * kz_len] for t in turned for c in (0, 2)]
        slope = dot_data_left(jnp.concatenate(slope_in, axis=0), table_ref[2], table_ref[3])
        fields = []
        for part in range(pack):
            own = plain[part * group : (part + 1) * group]
            sl = slope[part * 2 * kz_len : (part + 1) * 2 * kz_len]
            fields.append(
                jnp.concatenate(
                    [
                        own[: 3 * kz_len],
                        own[3 * kz_len : 4 * kz_len] - sl[:kz_len],
                        sl[kz_len:],
                        -own[4 * kz_len :],
                    ],
                    axis=0,
                )
            )
        for dest in range(cols):
            tile, off = divmod(dest * y_len, LANES)
            held[dest, at] = lane_pack(
                [f[:, tile * LANES : (tile + 1) * LANES] for f in fields], y_len, off
            )[0]
            pltpu.make_async_copy(held.at[dest, at], out_refs[dest].at[at], sem.at[dest, at]).start()
        return carry

    lax.fori_loop(0, xc // pack, body, 0)
    finish(held, out_refs, sem)


def second_synth(place, arrived, table, dims):
    rows, xc, ky_len, kz_len, cols, y_len, pack = dims
    packs = xc // pack
    return pl.pallas_call(
        functools.partial(second_synth_kernel, dims),
        in_specs=[SMEM] + [VMEM] * (len(arrived) + 1),
        out_specs=[HBM] * cols,
        out_shape=[jax.ShapeDtypeStruct((packs, 6 * kz_len, LANES), F32)] * cols,
        scratch_shapes=[
            pltpu.VMEM((len(arrived) * arrived[0].shape[0], LANES), F32),
            pltpu.VMEM((cols, packs, 6 * kz_len, LANES), F32),
            pltpu.SemaphoreType.DMA((cols, packs)),
        ],
        compiler_params=still(),
        cost_estimate=SHORT,
        name="second_synth",
    )(place, *arrived, table)


def cross(left, right):
    return [
        left[1] * right[2] - left[2] * right[1],
        left[2] * right[0] - left[0] * right[2],
        left[0] * right[1] - left[1] * right[0],
    ]


def earlier_kernel(count, *refs):
    vels, vorts, out_ref = refs[:count], refs[count : 2 * count], refs[2 * count]
    pack, y_len = out_ref.shape[1:3]
    for part in range(pack):
        def body(step, carry):
            at = pl.ds(pl.multiple_of(step * 8, 8), 8)
            total = None
            for vel, vort in zip(vels, vorts):
                term = cross(
                    [vel[0, c, part, at, :] for c in range(3)],
                    [vort[0, c, part, at, :] for c in range(3)],
                )
                total = term if total is None else [a + b for a, b in zip(total, term)]
            for comp in range(3):
                out_ref[comp, part, at, :] = total[comp]
            return carry

        lax.fori_loop(0, y_len // 8, body, 0, unroll=2)


def earlier(velocity, vorticity, chunk, xc, pack):
    orders, _, _, y_len, grid_len = velocity.shape
    packs = xc // pack
    block = (1, 3, pack, y_len, grid_len)

    def at(order):
        return pl.BlockSpec(block, lambda i: (order, 0, chunk * packs + i, 0, 0))

    specs = [at(k) for k in range(1, orders)] + [at(orders - k) for k in range(1, orders)]
    size = xc * y_len * grid_len
    return pl.pallas_call(
        functools.partial(earlier_kernel, orders - 1),
        grid=(packs,),
        in_specs=specs,
        out_specs=pl.BlockSpec((3, pack, y_len, grid_len), lambda i: (0, i, 0, 0)),
        out_shape=jax.ShapeDtypeStruct((3, xc, y_len, grid_len), F32),
        compiler_params=params(),
        cost_estimate=SHORT,
        name="earlier_orders",
    )(*[velocity] * (orders - 1), *[vorticity] * (orders - 1))


def third_kernel(dims, place_ref, *refs):
    chunk, kz_len, cols, y_len, pack = dims
    b_refs, stored_refs, table_ref = refs[:cols], refs[cols : cols + 3], refs[cols + 3]
    data, sem, held, out_sem = refs[-4:]
    out_refs = refs[-4 - cols : -4]
    grid_len = table_ref.shape[2]
    xc = data.shape[2]
    packs = xc // pack

    def copies(at):
        spot = pl.ds(at * pack, pack)
        far = pl.ds(chunk * xc + at * pack, pack)
        sources = [ref.at[0, :, far] for ref in stored_refs[:2]] + [stored_refs[2].at[:, spot]]
        return [
            pltpu.make_async_copy(source, data.at[idx, :, spot], sem.at[idx, at])
            for idx, source in enumerate(sources)
        ]

    for at in range(packs):
        for copy in copies(at):
            copy.start()

    def body(at, carry):
        def stack(field):
            return jnp.concatenate(
                [b_refs[k][at, field * kz_len : (field + 1) * kz_len, :] for k in range(cols)], axis=0
            ).T

        lines = jnp.concatenate([stack(field) for field in range(6)], axis=0)
        plain = dot_data_left(lines, table_ref[0], table_ref[1])
        slope = dot_data_left(lines[: 2 * LANES], table_ref[2], table_ref[3])
        new = [plain[f * LANES : (f + 1) * LANES] for f in range(6)]
        vel_new = new[:3]
        vort_new = [new[4] - slope[LANES:], slope[:LANES] + new[5], new[3]]
        for copy in copies(at):
            copy.wait()
        spot = pl.ds(at * pack, pack)
        flat = (pack * y_len, grid_len)
        vel, vort, base = [[data[idx, c, spot].reshape(flat) for c in range(3)] for idx in range(3)]
        one, two = cross(vel_new, vort), cross(vel, vort_new)
        total = [one[c] + two[c] + base[c] for c in range(3)]
        result = dot_data_right(table_ref[0], table_ref[1], jnp.concatenate(total, axis=0))
        for k in range(cols):
            for comp in range(3):
                held[k, at, comp * kz_len : (comp + 1) * kz_len, :] = result[
                    k * kz_len : (k + 1) * kz_len, comp * LANES : (comp + 1) * LANES
                ]
            pltpu.make_async_copy(held.at[k, at], out_refs[k].at[at], out_sem.at[k, at]).start()
        return carry

    lax.fori_loop(0, packs, body, 0)
    finish(held, out_refs, out_sem)


def third(place, arrived, velocity, vorticity, base, table, chunk, dims):
    kz_len, cols, y_len, pack = dims
    packs = arrived[0].shape[0]
    grid_len = velocity.shape[-1]
    return pl.pallas_call(
        functools.partial(third_kernel, (chunk, *dims)),
        in_specs=[SMEM] + [VMEM] * cols + [ANY] * 3 + [VMEM],
        out_specs=[HBM] * cols,
        out_shape=[jax.ShapeDtypeStruct((packs, 3 * kz_len, LANES), F32)] * cols,
        scratch_shapes=[
            pltpu.VMEM((3, 3, packs * pack, y_len, grid_len), F32),
            pltpu.SemaphoreType.DMA((3, packs)),
            pltpu.VMEM((cols, packs, 3 * kz_len, LANES), F32),
            pltpu.SemaphoreType.DMA((cols, packs)),
        ],
        compiler_params=still(),
        cost_estimate=SHORT,
        name="third_dimension",
    )(place, *arrived, velocity, vorticity, base, table)


def second_back_kernel(dims, place_ref, *refs):
    rows, xc, ky_len, kz_len, cols, y_len, pack = dims
    c_refs, table_ref, outs = refs[:cols], refs[cols], refs[cols + 1 : -2]
    all_ref, sem = refs[-2:]
    width = 3 * kz_len
    high_pad = round_up(width, LANES)

    def body(at, carry):
        lines = []
        for part in range(pack):
            tiles = lane_pack(
                [c_ref[at] for c_ref in c_refs], y_len, part * y_len
            )
            lines.append(jnp.concatenate(tiles, axis=1))
            if high_pad > width:
                lines.append(jnp.zeros((high_pad - width, cols * y_len), F32))
        result = dot_data_right(table_ref[0], table_ref[1], jnp.concatenate(lines, axis=0))
        for part in range(pack):
            own = result[:, part * high_pad : (part + 1) * high_pad]
            tiles = lane_pack([own[ky * rows : (ky + 1) * rows] for ky in range(ky_len)], width)
            for idx, tile in enumerate(tiles):
                spot = idx * xc + at * pack + part
                all_ref[pl.ds(spot, rows, stride=len(tiles) * xc), :] = tile
        return carry

    lax.fori_loop(0, xc // pack, body, 0)
    size = all_ref.shape[0] // len(outs)
    copies = []
    for k, out in enumerate(outs):
        spot = pl.multiple_of((place_ref[0] ^ k) * size, 8)
        copies.append(pltpu.make_async_copy(all_ref.at[pl.ds(spot, size), :], out, sem.at[k]))
    for copy in copies:
        copy.start()
    for copy in copies:
        copy.wait()


def second_back(place, arrived, table, dims):
    rows, xc, ky_len, kz_len, cols, y_len, pack = dims
    size = round_up(ky_len * 3 * kz_len, LANES) // LANES * xc
    groups = rows // 2
    return pl.pallas_call(
        functools.partial(second_back_kernel, dims),
        in_specs=[SMEM] + [VMEM] * (cols + 1),
        out_specs=[HBM] * groups,
        out_shape=[jax.ShapeDtypeStruct((2 * size, LANES), F32)] * groups,
        scratch_shapes=[pltpu.VMEM((rows * size, LANES), F32), pltpu.SemaphoreType.DMA((groups,))],
        compiler_params=still(),
        cost_estimate=SHORT,
        name="second_back",
    )(place, *arrived, table)


def first_back_kernel(dims, place_ref, *refs):
    count, xc = dims
    parts, table_ref, outs = refs[:count], refs[count], refs[count + 1 : count + 3]
    data, sem = refs[-2:]
    copies = [pltpu.make_async_copy(part, data.at[k], sem.at[k]) for k, part in enumerate(parts)]
    for copy in copies:
        copy.start()
    for copy in copies:
        copy.wait()
    size = data.shape[1] // 2
    for out_ref, core in zip(outs, (1 - place_ref[1], place_ref[1])):
        for tile in range(size // xc):
            spot = pl.ds(pl.multiple_of(core * size + tile * xc, 8), xc)
            found = jnp.concatenate([data[k, spot, :] for k in range(count)], axis=0)
            out_ref[:, tile * LANES : (tile + 1) * LANES] = dot_data_right(
                table_ref[0], table_ref[1], found, NN
            )


def first_back(place, parts, table, xc):
    count = len(parts)
    size = parts[0].shape[0]
    out = jax.ShapeDtypeStruct((table.shape[1], size // (2 * xc) * LANES), F32)
    return pl.pallas_call(
        functools.partial(first_back_kernel, (count, xc)),
        in_specs=[SMEM] + [ANY] * count + [VMEM],
        out_shape=[out, out],
        scratch_shapes=[pltpu.VMEM((count, size, LANES), F32), pltpu.SemaphoreType.DMA((count,))],
        compiler_params=still(VMEM_MOST),
        cost_estimate=SHORT,
        name="first_back",
    )(place, *parts, table)


def last_kernel(dims, *refs):
    kz_len, modes, scale = dims
    wave_y_ref, own_ref, other_ref, wave_x_ref, wave_z_ref, out_ref, rows = refs
    pair = 2 * 3 * kz_len
    at = pl.program_id(0)

    @pl.when(at == 0)
    def _():
        for tile in range(rows.shape[0] // LANES):
            lanes = slice(tile * LANES, (tile + 1) * LANES)
            rows[lanes, 0:modes] = (own_ref[:, lanes] + other_ref[:, lanes]).T

    spec = rows[pl.ds(pl.multiple_of(at * pair, 8), pair), :]
    wide = spec.shape[1]
    wave_x = jnp.broadcast_to(wave_x_ref[0:1, :], (kz_len, wide))
    wave_z = wave_z_ref[...]
    wave_y = wave_y_ref[at]
    even_x = lax.broadcasted_iota(jnp.int32, (kz_len, wide), 1) % 2 == 0
    even_z = lax.broadcasted_iota(jnp.int32, (kz_len, wide), 0) % 2 == 0

    def slope_x(value):
        return jnp.where(even_x, turn(value, -1), -turn(value, 1)) * wave_x

    def slope_z(value):
        return (
            jnp.where(
                even_z,
                pltpu.roll(value, kz_len - 1, axis=0),
                -pltpu.roll(value, 1, axis=0),
            )
            * wave_z
        )

    s = [
        [spec[(y * 3 + c) * kz_len : (y * 3 + c + 1) * kz_len] for c in range(3)] for y in range(2)
    ]
    square = wave_x * wave_x + wave_z * wave_z + wave_y * wave_y
    positive = square > 0
    safe = jnp.where(positive, square, 1.0)
    potential = []
    for y in range(2):
        along_y = s[1 - y][1] * (wave_y if y == 0 else -wave_y)
        divergence = slope_x(s[y][0]) + along_y + slope_z(s[y][2])
        potential.append(jnp.where(positive, divergence / safe, 0.0))
    for y in range(2):
        along_y = potential[1 - y] * (wave_y if y == 0 else -wave_y)
        found = [
            s[y][0] + slope_x(potential[y]),
            s[y][1] + along_y,
            s[y][2] + slope_z(potential[y]),
        ]
        for comp in range(3):
            out_ref[comp, y] = (found[comp] * scale)[:, :modes]


def last(own, other, wave_y, wave_x, wave_z, ky_len, kz_len, scale):
    modes, lanes = own.shape
    return pl.pallas_call(
        functools.partial(last_kernel, (kz_len, modes, scale)),
        grid=(ky_len // 2,),
        in_specs=[SMEM, *[whole(a) for a in (own, other, wave_x, wave_z)]],
        out_specs=pl.BlockSpec((3, 2, kz_len, modes), lambda i: (0, i, 0, 0)),
        out_shape=jax.ShapeDtypeStruct((3, ky_len, kz_len, modes), F32),
        scratch_shapes=[pltpu.VMEM((lanes, wave_x.shape[1]), F32)],
        compiler_params=params(),
        cost_estimate=SHORT,
        name="last_projection",
    )(wave_y, own, other, wave_x, wave_z)


def after(value, *earlier_values):
    return lax.optimization_barrier((value, earlier_values))[0]


def shards(new_velocity, stored_velocity, stored_vorticity):
    rows = lax.axis_size("row")
    cols = lax.axis_size("col")
    _, ky_len, kz_own, modes = new_velocity.shape
    orders, _, x_len, y_len, grid_len = stored_velocity.shape
    kz_len = round_up(kz_own, 8)
    kmax = modes // 2 - 1
    xc = min(XC, x_len)
    chunks = x_len // xc
    pack = LANES // y_len
    packs = xc // pack
    wide = round_up(modes, LANES)
    group = 5 * kz_len
    lanes = round_up(ky_len * group, 256)

    basis = synth_np(grid_len, modes)
    slope = slope_np(basis, kmax)
    y_order = (np.arange(rows)[None, :] * ky_len + np.arange(ky_len)[:, None]).reshape(-1)

    groups = rows // 2
    row, col = lax.axis_index("row"), lax.axis_index("col")
    place = jnp.stack([row // 2, row % 2, col]).astype(jnp.int32)

    def own_table(tables, axis):
        return lax.dynamic_index_in_dim(jnp.asarray(np.stack(tables)), lax.axis_index(axis), 0, False)

    def x_points(row):
        owner = np.array([row ^ (2 * k) for k in range(groups)])
        return (
            owner[None, :, None] * x_len
            + np.arange(chunks)[:, None, None] * xc
            + np.arange(xc)[None, None, :]
        ).reshape(-1)

    def halves_of(plain, sloped):
        return np.stack([part for table in (plain, sloped) for part in halves(table)])

    def y_table(col):
        points = np.concatenate([(col ^ k) * y_len + np.arange(y_len) for k in range(cols)])
        return halves_of(basis[points].T[y_order], slope[points].T[y_order])

    def z_table(col):
        def spread(table):
            parts = table.T.reshape(cols, kz_own, grid_len)[[col ^ k for k in range(cols)]]
            parts = np.pad(parts, ((0, 0), (0, kz_len - kz_own), (0, 0)))
            return parts.reshape(cols * kz_len, grid_len)

        return halves_of(spread(basis), spread(slope))

    table_x = own_table(
        [halves_of(basis[x_points(row)].T, slope[x_points(row)].T) for row in range(rows)], "row"
    )
    table_y = own_table([y_table(col) for col in range(cols)], "col")
    table_z = own_table([z_table(col) for col in range(cols)], "col")

    def wave_of(index):
        return (index // 2).astype(F32) / kmax

    mode = jnp.arange(wide, dtype=jnp.int32)
    wave_x = jnp.broadcast_to(jnp.where(mode < modes, wave_of(mode), 0.0)[None, :], (8, wide))
    ky_first = lax.axis_index("row") * ky_len + 2 * jnp.arange(ky_len // 2, dtype=jnp.int32)
    wave_y = wave_of(ky_first)
    kz = lax.axis_index("col") * kz_own + jnp.arange(kz_len, dtype=jnp.int32)
    wave_z = jnp.broadcast_to(wave_of(kz)[:, None], (kz_len, wide))

    coeffs = new_velocity
    if kz_len > kz_own:
        coeffs = jnp.pad(coeffs, ((0, 0), (0, 0), (0, kz_len - kz_own), (0, 0)))

    def exchange(values, axis, shift, size):
        return [
            lax.ppermute(value, axis, [(src, src ^ (k << shift)) for src in range(size)]) if k else value
            for k, value in enumerate(values)
        ]

    def core_swap(value):
        return lax.ppermute(value, "row", [(src, src ^ 1) for src in range(rows)])

    dims = (rows, xc, ky_len, kz_len, cols, y_len, pack)
    sent = first_synth(place, coeffs, core_swap(coeffs), table_x, (chunks, groups, xc), lanes)
    latest = sent[0][0]

    def ordered(kernel, operands, *others):
        nonlocal latest
        operands = after(operands, latest)
        found = kernel(operands, *others)
        latest = found[0] if isinstance(found, (list, tuple)) else found
        return found

    stored = (stored_velocity, stored_vorticity)

    def run_earlier(chunk):
        return ordered(lambda values: earlier(*values, chunk, xc, pack), stored)

    def z_exchange(values, *gates):
        found = [values[0]]
        for k in range(1, groups):
            value = after(values[k], *gates) if gates else values[k]
            found.append(lax.ppermute(value, "row", [(src, src ^ (2 * k)) for src in range(rows)]))
        return found

    first, second, middle, back, base = {}, {}, {}, {}, {}
    first[0] = z_exchange(sent[0])
    for chunk in range(chunks):
        base[chunk] = run_earlier(chunk)
    for step in range(chunks):
        if step + 1 < chunks:
            first[step + 1] = z_exchange(sent[step + 1], first[step])
        found = ordered(lambda values: second_synth(place, values, table_y, dims), first[step])
        second[step] = exchange(found, "col", 0, cols)
    for step in range(chunks):
        middle[step] = ordered(
            lambda values: third(place, values, *stored, base[step], table_z, step, dims[3:]),
            second[step],
        )
    for step in range(chunks):
        found = exchange(middle[step], "col", 0, cols)
        found = ordered(lambda values: second_back(place, values, table_y, dims), found)
        back[step] = z_exchange(found, *([back[step - 1]] if step else []))
    parts = [value for step in range(chunks) for value in back[step]]
    away, home = first_back(place, parts, table_x, xc)
    result = last(home, core_swap(away), wave_y, wave_x, wave_z, ky_len, kz_len, 1.0 / (orders + 1))
    return result[:, :, :kz_own] if kz_len > kz_own else result


def solution(mesh):
    return jax.shard_map(
        shards,
        mesh=mesh,
        in_specs=(
            P(None, "row", "col", None),
            P(None, None, "row", "col", None),
            P(None, None, "row", "col", None),
        ),
        out_specs=P(None, "row", "col", None),
        check_vma=False,
    )
```

```python
import functools
import math

import jax
import jax.numpy as jnp
import ml_dtypes
import numpy as np
from jax import lax
from jax.experimental import pallas as pl
from jax.experimental.pallas import tpu as pltpu
from jax.sharding import PartitionSpec as P

LANES = 128
XC = 16
BF16 = jnp.bfloat16
F32 = jnp.float32
NN = (((1,), (0,)), ((), ()))
NT = (((1,), (1,)), ((), ()))


def round_up(value, step):
    return -(-value // step) * step


def synth_np(grid_len, mode_count):
    points = np.arange(grid_len)[:, None]
    mode_index = np.arange(mode_count)[None, :]
    wave_index = np.where(mode_index == 1, grid_len // 2, mode_index // 2)
    angles = (points * wave_index % grid_len) * (2.0 * math.pi / grid_len)
    trig = np.where((mode_index % 2 == 0) | (mode_index == 1), np.cos(angles), np.sin(angles))
    weight = np.where(mode_index < 2, 1.0, 2.0) / grid_len
    return np.where(mode_index == 1, 0.0, trig * np.sqrt(weight))


def slope_np(table, kmax):
    paired = table.reshape(table.shape[0], -1, 2)
    wavenum = np.arange(paired.shape[1]) / kmax
    return np.stack([-wavenum * paired[:, :, 1], wavenum * paired[:, :, 0]], -1).reshape(table.shape)


def halves(table):
    high = table.astype(ml_dtypes.bfloat16)
    low = (table - high.astype(np.float64)).astype(ml_dtypes.bfloat16)
    return high, low


def pieces_of(values):
    high = values.astype(BF16)
    return high, (values - high.astype(F32)).astype(BF16)


def dot(left, right, dims):
    return lax.dot_general(left, right, dims, preferred_element_type=F32)


def dot_data_left(values, high, low, dims=NN):
    top, rest = pieces_of(values)
    return dot(top, high, dims) + (dot(top, low, dims) + dot(rest, high, dims))


def dot_data_right(high, low, values, dims=NT):
    top, rest = pieces_of(values)
    return dot(high, top, dims) + (dot(low, top, dims) + dot(high, rest, dims))


def turn(values, shift):
    shift = shift % values.shape[-1]
    return values if shift == 0 else pltpu.roll(values, shift, axis=values.ndim - 1)


def lane_pack(parts, width, source_lane=0):
    tiles = []
    lane = lax.broadcasted_iota(jnp.int32, parts[0].shape, 1)
    for tile in range(-(-len(parts) * width // LANES)):
        start = tile * LANES
        acc = None
        for idx in range(start // width, min(len(parts) - 1, (start + LANES - 1) // width) + 1):
            moved = turn(parts[idx], idx * width - source_lane)
            acc = moved if acc is None else jnp.where(lane >= idx * width - start, moved, acc)
        tiles.append(acc)
    return tiles


VMEM_LIMIT = 32 * 1024 * 1024
VMEM_MOST = 60 * 1024 * 1024
SHORT = pl.CostEstimate(flops=1024, bytes_accessed=1024, transcendentals=0)
ANY = pl.BlockSpec(memory_space=pl.ANY)
HBM = pl.BlockSpec(memory_space=pltpu.HBM)
SMEM = pl.BlockSpec(memory_space=pltpu.SMEM)
VMEM = pl.BlockSpec(memory_space=pltpu.VMEM)


def params():
    return pltpu.CompilerParams(dimension_semantics=("arbitrary",), vmem_limit_bytes=VMEM_LIMIT)


def still(limit=VMEM_LIMIT):
    return pltpu.CompilerParams(vmem_limit_bytes=limit)


def finish(held, out_refs, sem):
    for at in range(held.shape[1]):
        for k, out in enumerate(out_refs):
            pltpu.make_async_copy(held.at[k, at], out.at[at], sem.at[k, at]).wait()


def both_passes(values, high_low, high):
    top, rest = pieces_of(values)
    wide = dot(top, high_low, NN)
    half = high.shape[1]
    return wide[:, :half] + (wide[:, half:] + dot(rest, high, NN))


def whole(array):
    rank = len(array.shape)
    return pl.BlockSpec(array.shape, lambda *_: (0,) * rank)


def first_synth_kernel(dims, place_ref, data_ref, table_ref, *rest):
    chunks, dests, xc, own = dims
    count = chunks * dests
    outs = rest[-count - 5 : -5]
    data, rows, held, sem, out_sem = rest[-5:]
    _, ky_len, kz_len, _ = data.shape
    group = 5 * kz_len
    size = held.shape[1]
    copies = [
        pltpu.make_async_copy(data_ref.at[comp], data.at[comp], sem.at[comp]) for comp in range(3)
    ]
    for copy in copies:
        copy.start()
    if ky_len * group < rows.shape[0]:
        rows[ky_len * group :, :] = jnp.zeros((rows.shape[0] - ky_len * group, LANES), F32)
    plain = jnp.concatenate([table_ref[0], table_ref[1]], axis=1)
    slope = jnp.concatenate([table_ref[2], table_ref[3]], axis=1)
    step = 4 if ky_len % 4 == 0 else 2
    for copy in copies:
        copy.wait()

    def body(idx, carry):
        first = idx * step
        lines = [[data[comp, first + k] for comp in range(3)] for k in range(step)]
        found = both_passes(
            jnp.concatenate([v for line in lines for v in line], axis=0), plain, table_ref[0]
        )
        sloped = both_passes(
            jnp.concatenate([v for line in lines for v in line[1:]], axis=0), slope, table_ref[2]
        )
        for k in range(step):
            base = (first + k) * group
            rows[pl.ds(pl.multiple_of(base, 8), 3 * kz_len), :] = found[
                3 * k * kz_len : 3 * (k + 1) * kz_len
            ]
            rows[pl.ds(pl.multiple_of(base + 3 * kz_len, 8), 2 * kz_len), :] = sloped[
                2 * k * kz_len : 2 * (k + 1) * kz_len
            ]
        return carry

    lax.fori_loop(0, ky_len // step, body, 0)

    def flip(tile, carry):
        found = rows[pl.ds(pl.multiple_of(tile * LANES, LANES), LANES), :].T
        for idx in range(count):
            held[idx, pl.ds(pl.multiple_of(tile * xc, 8), xc), :] = found[idx * xc : (idx + 1) * xc]
        return carry

    lax.fori_loop(0, rows.shape[0] // LANES, flip, 0, unroll=2)
    core = place_ref[1] if own else 1 - place_ref[1]
    spot = pl.ds(pl.multiple_of(core * size, 8), size)
    copies = [
        pltpu.make_async_copy(held.at[k], out.at[spot, :], out_sem.at[k]) for k, out in enumerate(outs)
    ]
    for copy in copies:
        copy.start()
    for copy in copies:
        copy.wait()


def first_synth(place, coeffs, table, dims, lanes, half):
    chunks, dests, xc = dims
    size = lanes // LANES * xc
    count = chunks * dests
    return pl.pallas_call(
        functools.partial(first_synth_kernel, (*dims, not half)),
        in_specs=[SMEM, ANY, VMEM] + [HBM] * len(half),
        out_specs=[HBM] * count,
        out_shape=[jax.ShapeDtypeStruct((2 * size, LANES), F32)] * count,
        input_output_aliases={3 + k: k for k in range(len(half))},
        scratch_shapes=[
            pltpu.VMEM(coeffs.shape, F32),
            pltpu.VMEM((lanes, LANES), F32),
            pltpu.VMEM((count, size, LANES), F32),
            pltpu.SemaphoreType.DMA((3,)),
            pltpu.SemaphoreType.DMA((count,)),
        ],
        compiler_params=still(),
        cost_estimate=SHORT,
        name="first_synth",
    )(place, coeffs, table, *half)


def second_synth_kernel(dims, place_ref, *refs):
    rows, xc, ky_len, kz_len, cols, y_len, pack = dims
    groups = rows // 2
    parts, table_ref, out_refs = refs[:groups], refs[groups], refs[groups + 1 : -3]
    a_ref, held, sem = refs[-3:]
    size = parts[0].shape[0] // 2
    stride = a_ref.shape[0] // rows
    for k, part in enumerate(parts):
        for core in range(2):
            spot = pl.multiple_of(((place_ref[0] ^ k) * 2 + core) * stride, 8)
            a_ref[pl.ds(spot, size), :] = part[core * size : (core + 1) * size, :]
    group = 5 * kz_len
    wide = round_up(group, LANES)
    tiles = size // xc

    def body(at, carry):
        turned = []
        for part in range(pack):
            line = [
                a_ref[pl.ds(tile * xc + at * pack + part, rows, stride=stride), :]
                for tile in range(tiles)
            ]
            found = []
            for ky in range(ky_len):
                start = ky * group
                low, off = divmod(start, LANES)
                window = line[low : low + (wide // LANES) + (1 if off else 0)]
                found.append(turn(jnp.concatenate(window, axis=1), -off)[:, :wide])
            turned.append(jnp.concatenate(found, axis=0).T[:group])
        plain = dot_data_left(jnp.concatenate(turned, axis=0), table_ref[0], table_ref[1])
        slope_in = [t[c * kz_len : (c + 1) * kz_len] for t in turned for c in (0, 2)]
        slope = dot_data_left(jnp.concatenate(slope_in, axis=0), table_ref[2], table_ref[3])
        fields = []
        for part in range(pack):
            own = plain[part * group : (part + 1) * group]
            sl = slope[part * 2 * kz_len : (part + 1) * 2 * kz_len]
            fields.append(
                jnp.concatenate(
                    [
                        own[: 3 * kz_len],
                        own[3 * kz_len : 4 * kz_len] - sl[:kz_len],
                        sl[kz_len:],
                        -own[4 * kz_len :],
                    ],
                    axis=0,
                )
            )
        for dest in range(cols):
            tile, off = divmod(dest * y_len, LANES)
            held[dest, at] = lane_pack(
                [f[:, tile * LANES : (tile + 1) * LANES] for f in fields], y_len, off
            )[0]
            pltpu.make_async_copy(held.at[dest, at], out_refs[dest].at[at], sem.at[dest, at]).start()
        return carry

    lax.fori_loop(0, xc // pack, body, 0)
    finish(held, out_refs, sem)


def second_synth(place, arrived, table, dims):
    rows, xc, ky_len, kz_len, cols, y_len, pack = dims
    packs = xc // pack
    return pl.pallas_call(
        functools.partial(second_synth_kernel, dims),
        in_specs=[SMEM] + [VMEM] * (len(arrived) + 1),
        out_specs=[HBM] * cols,
        out_shape=[jax.ShapeDtypeStruct((packs, 6 * kz_len, LANES), F32)] * cols,
        scratch_shapes=[
            pltpu.VMEM((rows * (arrived[0].shape[0] // 2 + 8), LANES), F32),
            pltpu.VMEM((cols, packs, 6 * kz_len, LANES), F32),
            pltpu.SemaphoreType.DMA((cols, packs)),
        ],
        compiler_params=still(),
        cost_estimate=SHORT,
        name="second_synth",
    )(place, *arrived, table)


def cross(left, right):
    return [
        left[1] * right[2] - left[2] * right[1],
        left[2] * right[0] - left[0] * right[2],
        left[0] * right[1] - left[1] * right[0],
    ]


def earlier_kernel(count, *refs):
    vels, vorts, out_ref = refs[:count], refs[count : 2 * count], refs[2 * count]
    pack, y_len = out_ref.shape[1:3]
    for part in range(pack):
        def body(step, carry):
            at = pl.ds(pl.multiple_of(step * 8, 8), 8)
            total = None
            for vel, vort in zip(vels, vorts):
                term = cross(
                    [vel[0, c, part, at, :] for c in range(3)],
                    [vort[0, c, part, at, :] for c in range(3)],
                )
                total = term if total is None else [a + b for a, b in zip(total, term)]
            for comp in range(3):
                out_ref[comp, part, at, :] = total[comp]
            return carry

        lax.fori_loop(0, y_len // 8, body, 0, unroll=2)


def earlier(velocity, vorticity, chunk, xc, pack):
    orders, _, _, y_len, grid_len = velocity.shape
    packs = xc // pack
    block = (1, 3, pack, y_len, grid_len)

    def at(order):
        return pl.BlockSpec(block, lambda i: (order, 0, chunk * packs + i, 0, 0))

    specs = [at(k) for k in range(1, orders)] + [at(orders - k) for k in range(1, orders)]
    size = xc * y_len * grid_len
    return pl.pallas_call(
        functools.partial(earlier_kernel, orders - 1),
        grid=(packs,),
        in_specs=specs,
        out_specs=pl.BlockSpec((3, pack, y_len, grid_len), lambda i: (0, i, 0, 0)),
        out_shape=jax.ShapeDtypeStruct((3, xc, y_len, grid_len), F32),
        compiler_params=params(),
        cost_estimate=SHORT,
        name="earlier_orders",
    )(*[velocity] * (orders - 1), *[vorticity] * (orders - 1))


def third_kernel(dims, place_ref, *refs):
    chunk, kz_len, cols, y_len, pack = dims
    b_refs, stored_refs, table_ref = refs[:cols], refs[cols : cols + 3], refs[cols + 3]
    data, sem, held, out_sem = refs[-4:]
    out_refs = refs[-4 - cols : -4]
    grid_len = table_ref.shape[2]
    xc = data.shape[2]
    packs = xc // pack

    def copies(at):
        spot = pl.ds(at * pack, pack)
        far = pl.ds(chunk * xc + at * pack, pack)
        sources = [ref.at[0, :, far] for ref in stored_refs[:2]] + [stored_refs[2].at[:, spot]]
        return [
            pltpu.make_async_copy(source, data.at[idx, :, spot], sem.at[idx, at])
            for idx, source in enumerate(sources)
        ]

    for at in range(packs):
        for copy in copies(at):
            copy.start()

    def body(at, carry):
        def stack(field):
            return jnp.concatenate(
                [b_refs[k][at, field * kz_len : (field + 1) * kz_len, :] for k in range(cols)], axis=0
            ).T

        lines = jnp.concatenate([stack(field) for field in range(6)], axis=0)
        plain = dot_data_left(lines, table_ref[0], table_ref[1])
        slope = dot_data_left(lines[: 2 * LANES], table_ref[2], table_ref[3])
        new = [plain[f * LANES : (f + 1) * LANES] for f in range(6)]
        vel_new = new[:3]
        vort_new = [new[4] - slope[LANES:], slope[:LANES] + new[5], new[3]]
        for copy in copies(at):
            copy.wait()
        spot = pl.ds(at * pack, pack)
        flat = (pack * y_len, grid_len)
        vel, vort, base = [[data[idx, c, spot].reshape(flat) for c in range(3)] for idx in range(3)]
        one, two = cross(vel_new, vort), cross(vel, vort_new)
        total = [one[c] + two[c] + base[c] for c in range(3)]
        result = dot_data_right(table_ref[0], table_ref[1], jnp.concatenate(total, axis=0))
        for k in range(cols):
            for comp in range(3):
                held[k, at, comp * kz_len : (comp + 1) * kz_len, :] = result[
                    k * kz_len : (k + 1) * kz_len, comp * LANES : (comp + 1) * LANES
                ]
            pltpu.make_async_copy(held.at[k, at], out_refs[k].at[at], out_sem.at[k, at]).start()
        return carry

    lax.fori_loop(0, packs, body, 0)
    finish(held, out_refs, out_sem)


def third(place, arrived, velocity, vorticity, base, table, chunk, dims):
    kz_len, cols, y_len, pack = dims
    packs = arrived[0].shape[0]
    grid_len = velocity.shape[-1]
    return pl.pallas_call(
        functools.partial(third_kernel, (chunk, *dims)),
        in_specs=[SMEM] + [VMEM] * cols + [ANY] * 3 + [VMEM],
        out_specs=[HBM] * cols,
        out_shape=[jax.ShapeDtypeStruct((packs, 3 * kz_len, LANES), F32)] * cols,
        scratch_shapes=[
            pltpu.VMEM((3, 3, packs * pack, y_len, grid_len), F32),
            pltpu.SemaphoreType.DMA((3, packs)),
            pltpu.VMEM((cols, packs, 3 * kz_len, LANES), F32),
            pltpu.SemaphoreType.DMA((cols, packs)),
        ],
        compiler_params=still(),
        cost_estimate=SHORT,
        name="third_dimension",
    )(place, *arrived, velocity, vorticity, base, table)


def second_back_kernel(dims, place_ref, *refs):
    rows, xc, ky_len, kz_len, cols, y_len, pack = dims
    c_refs, table_ref, outs = refs[:cols], refs[cols], refs[cols + 1 : -2]
    all_ref, sem = refs[-2:]
    width = 3 * kz_len
    high_pad = round_up(width, LANES)

    def body(at, carry):
        lines = []
        for part in range(pack):
            tiles = lane_pack(
                [c_ref[at] for c_ref in c_refs], y_len, part * y_len
            )
            lines.append(jnp.concatenate(tiles, axis=1))
            if high_pad > width:
                lines.append(jnp.zeros((high_pad - width, cols * y_len), F32))
        result = dot_data_right(table_ref[0], table_ref[1], jnp.concatenate(lines, axis=0))
        for part in range(pack):
            own = result[:, part * high_pad : (part + 1) * high_pad]
            tiles = lane_pack([own[ky * rows : (ky + 1) * rows] for ky in range(ky_len)], width)
            for idx, tile in enumerate(tiles):
                spot = idx * xc + at * pack + part
                all_ref[pl.ds(spot, rows, stride=len(tiles) * xc), :] = tile
        return carry

    lax.fori_loop(0, xc // pack, body, 0)
    size = all_ref.shape[0] // len(outs)
    copies = []
    for k, out in enumerate(outs):
        spot = pl.multiple_of((place_ref[0] ^ k) * size, 8)
        copies.append(pltpu.make_async_copy(all_ref.at[pl.ds(spot, size), :], out, sem.at[k]))
    for copy in copies:
        copy.start()
    for copy in copies:
        copy.wait()


def second_back(place, arrived, table, dims):
    rows, xc, ky_len, kz_len, cols, y_len, pack = dims
    size = round_up(ky_len * 3 * kz_len, LANES) // LANES * xc
    groups = rows // 2
    return pl.pallas_call(
        functools.partial(second_back_kernel, dims),
        in_specs=[SMEM] + [VMEM] * (cols + 1),
        out_specs=[HBM] * groups,
        out_shape=[jax.ShapeDtypeStruct((2 * size, LANES), F32)] * groups,
        scratch_shapes=[pltpu.VMEM((rows * size, LANES), F32), pltpu.SemaphoreType.DMA((groups,))],
        compiler_params=still(),
        cost_estimate=SHORT,
        name="second_back",
    )(place, *arrived, table)


def first_back_kernel(dims, place_ref, *refs):
    count, xc, own = dims
    parts, table_ref, out_ref = refs[:count], refs[count], refs[count + 1]
    data, sem = refs[-2:]
    size = data.shape[1]
    core = place_ref[1] if own else 1 - place_ref[1]
    spot = pl.ds(pl.multiple_of(core * size, 8), size)
    copies = [
        pltpu.make_async_copy(part.at[spot, :], data.at[k], sem.at[k]) for k, part in enumerate(parts)
    ]
    for copy in copies:
        copy.start()
    for copy in copies:
        copy.wait()
    for tile in range(size // xc):
        found = jnp.concatenate([data[k, tile * xc : (tile + 1) * xc, :] for k in range(count)], axis=0)
        out_ref[:, tile * LANES : (tile + 1) * LANES] = dot_data_right(
            table_ref[0], table_ref[1], found, NN
        )


def first_back(place, parts, table, xc, own):
    count = len(parts)
    size = parts[0].shape[0] // 2
    return pl.pallas_call(
        functools.partial(first_back_kernel, (count, xc, own)),
        in_specs=[SMEM] + [HBM] * count + [VMEM],
        out_shape=jax.ShapeDtypeStruct((table.shape[1], size // xc * LANES), F32),
        scratch_shapes=[pltpu.VMEM((count, size, LANES), F32), pltpu.SemaphoreType.DMA((count,))],
        compiler_params=still(),
        cost_estimate=SHORT,
        name="first_back",
    )(place, *parts, table)


def last_kernel(dims, *refs):
    kz_len, modes, scale = dims
    wave_y_ref, wave_x_ref, wave_z_ref, *sums, out_ref, rows = refs
    pair = 2 * 3 * kz_len
    at = pl.program_id(0)

    @pl.when(at == 0)
    def _():
        for tile in range(rows.shape[0] // LANES):
            lanes = slice(tile * LANES, (tile + 1) * LANES)
            rows[lanes, 0:modes] = functools.reduce(jnp.add, [part[:, lanes] for part in sums]).T

    spec = rows[pl.ds(pl.multiple_of(at * pair, 8), pair), :]
    wide = spec.shape[1]
    wave_x = jnp.broadcast_to(wave_x_ref[0:1, :], (kz_len, wide))
    wave_z = wave_z_ref[...]
    wave_y = wave_y_ref[at]
    even_x = lax.broadcasted_iota(jnp.int32, (kz_len, wide), 1) % 2 == 0
    even_z = lax.broadcasted_iota(jnp.int32, (kz_len, wide), 0) % 2 == 0

    def slope_x(value):
        return jnp.where(even_x, turn(value, -1), -turn(value, 1)) * wave_x

    def slope_z(value):
        return (
            jnp.where(
                even_z,
                pltpu.roll(value, kz_len - 1, axis=0),
                -pltpu.roll(value, 1, axis=0),
            )
            * wave_z
        )

    s = [
        [spec[(y * 3 + c) * kz_len : (y * 3 + c + 1) * kz_len] for c in range(3)] for y in range(2)
    ]
    square = wave_x * wave_x + wave_z * wave_z + wave_y * wave_y
    positive = square > 0
    safe = jnp.where(positive, square, 1.0)
    potential = []
    for y in range(2):
        along_y = s[1 - y][1] * (wave_y if y == 0 else -wave_y)
        divergence = slope_x(s[y][0]) + along_y + slope_z(s[y][2])
        potential.append(jnp.where(positive, divergence / safe, 0.0))
    for y in range(2):
        along_y = potential[1 - y] * (wave_y if y == 0 else -wave_y)
        found = [
            s[y][0] + slope_x(potential[y]),
            s[y][1] + along_y,
            s[y][2] + slope_z(potential[y]),
        ]
        for comp in range(3):
            out_ref[comp, y] = (found[comp] * scale)[:, :modes]


def last(sums, wave_y, wave_x, wave_z, ky_len, kz_len, scale):
    modes, lanes = sums[0].shape
    return pl.pallas_call(
        functools.partial(last_kernel, (kz_len, modes, scale)),
        grid=(ky_len // 2,),
        in_specs=[SMEM, *[whole(a) for a in (wave_x, wave_z, *sums)]],
        out_specs=pl.BlockSpec((3, 2, kz_len, modes), lambda i: (0, i, 0, 0)),
        out_shape=jax.ShapeDtypeStruct((3, ky_len, kz_len, modes), F32),
        scratch_shapes=[pltpu.VMEM((lanes, wave_x.shape[1]), F32)],
        compiler_params=params(),
        cost_estimate=SHORT,
        name="last_projection",
    )(wave_y, wave_x, wave_z, *sums)


def after(value, *earlier_values):
    return lax.optimization_barrier((value, earlier_values))[0]


def shards(new_velocity, stored_velocity, stored_vorticity):
    rows = lax.axis_size("row")
    cols = lax.axis_size("col")
    _, ky_len, kz_own, modes = new_velocity.shape
    orders, _, x_len, y_len, grid_len = stored_velocity.shape
    kz_len = round_up(kz_own, 8)
    kmax = modes // 2 - 1
    xc = min(XC, x_len)
    chunks = x_len // xc
    pack = LANES // y_len
    packs = xc // pack
    wide = round_up(modes, LANES)
    group = 5 * kz_len
    lanes = round_up(ky_len * group, 256)

    basis = synth_np(grid_len, modes)
    slope = slope_np(basis, kmax)
    y_order = (np.arange(rows)[None, :] * ky_len + np.arange(ky_len)[:, None]).reshape(-1)

    groups = rows // 2
    row, col = lax.axis_index("row"), lax.axis_index("col")
    place = jnp.stack([row // 2, row % 2, col]).astype(jnp.int32)

    def own_table(tables, axis):
        return lax.dynamic_index_in_dim(jnp.asarray(np.stack(tables)), lax.axis_index(axis), 0, False)

    def x_points(row):
        owner = np.array([row ^ (2 * k) for k in range(groups)])
        return (
            owner[None, :, None] * x_len
            + np.arange(chunks)[:, None, None] * xc
            + np.arange(xc)[None, None, :]
        ).reshape(-1)

    def halves_of(plain, sloped):
        return np.stack([part for table in (plain, sloped) for part in halves(table)])

    def y_table(col):
        points = np.concatenate([(col ^ k) * y_len + np.arange(y_len) for k in range(cols)])
        return halves_of(basis[points].T[y_order], slope[points].T[y_order])

    def z_table(col):
        def spread(table):
            parts = table.T.reshape(cols, kz_own, grid_len)[[col ^ k for k in range(cols)]]
            parts = np.pad(parts, ((0, 0), (0, kz_len - kz_own), (0, 0)))
            return parts.reshape(cols * kz_len, grid_len)

        return halves_of(spread(basis), spread(slope))

    table_x = own_table(
        [halves_of(basis[x_points(row)].T, slope[x_points(row)].T) for row in range(rows)], "row"
    )
    table_y = own_table([y_table(col) for col in range(cols)], "col")
    table_z = own_table([z_table(col) for col in range(cols)], "col")

    def wave_of(index):
        return (index // 2).astype(F32) / kmax

    mode = jnp.arange(wide, dtype=jnp.int32)
    wave_x = jnp.broadcast_to(jnp.where(mode < modes, wave_of(mode), 0.0)[None, :], (8, wide))
    ky_first = lax.axis_index("row") * ky_len + 2 * jnp.arange(ky_len // 2, dtype=jnp.int32)
    wave_y = wave_of(ky_first)
    kz = lax.axis_index("col") * kz_own + jnp.arange(kz_len, dtype=jnp.int32)
    wave_z = jnp.broadcast_to(wave_of(kz)[:, None], (kz_len, wide))

    coeffs = new_velocity
    if kz_len > kz_own:
        coeffs = jnp.pad(coeffs, ((0, 0), (0, 0), (0, kz_len - kz_own), (0, 0)))

    def exchange(values, axis, shift, size):
        return [
            lax.ppermute(value, axis, [(src, src ^ (k << shift)) for src in range(size)]) if k else value
            for k, value in enumerate(values)
        ]

    def core_swap(value):
        return lax.ppermute(value, "row", [(src, src ^ 1) for src in range(rows)])

    dims = (rows, xc, ky_len, kz_len, cols, y_len, pack)
    shape = (chunks, groups, xc)
    other = core_swap(coeffs)
    sent = first_synth(place, coeffs, table_x, shape, lanes, ())
    sent = first_synth(place, other, table_x, shape, lanes, sent)
    sent = [list(sent[k * groups : (k + 1) * groups]) for k in range(chunks)]
    latest = sent[0][0]

    def ordered(kernel, operands, *others):
        nonlocal latest
        operands = after(operands, latest)
        found = kernel(operands, *others)
        latest = found[0] if isinstance(found, (list, tuple)) else found
        return found

    stored = (stored_velocity, stored_vorticity)

    def run_earlier(chunk):
        return ordered(lambda values: earlier(*values, chunk, xc, pack), stored)

    def z_exchange(values, *gates):
        found = [values[0]]
        for k in range(1, groups):
            value = after(values[k], *gates) if gates else values[k]
            found.append(lax.ppermute(value, "row", [(src, src ^ (2 * k)) for src in range(rows)]))
        return found

    first, second, middle, back, base = {}, {}, {}, {}, {}
    first[0] = z_exchange(sent[0])
    for chunk in range(chunks):
        base[chunk] = run_earlier(chunk)
    for step in range(chunks):
        if step + 1 < chunks:
            first[step + 1] = z_exchange(sent[step + 1], first[step])
        found = ordered(lambda values: second_synth(place, values, table_y, dims), first[step])
        second[step] = exchange(found, "col", 0, cols)
    for step in range(chunks):
        middle[step] = ordered(
            lambda values: third(place, values, *stored, base[step], table_z, step, dims[3:]),
            second[step],
        )
    for step in range(chunks):
        found = exchange(middle[step], "col", 0, cols)
        found = ordered(lambda values: second_back(place, values, table_y, dims), found)
        back[step] = z_exchange(found, *([back[step - 1]] if step else []))
    parts = [value for step in range(chunks) for value in back[step]]
    away = first_back(place, parts, table_x, xc, False)
    home = first_back(place, parts, after(table_x, away), xc, True)
    sums = [home, core_swap(away)]
    result = last(sums, wave_y, wave_x, wave_z, ky_len, kz_len, 1.0 / (orders + 1))
    return result[:, :, :kz_own] if kz_len > kz_own else result


def solution(mesh):
    return jax.shard_map(
        shards,
        mesh=mesh,
        in_specs=(
            P(None, "row", "col", None),
            P(None, None, "row", "col", None),
            P(None, None, "row", "col", None),
        ),
        out_specs=P(None, "row", "col", None),
        check_vma=False,
    )
```

```python
import functools
import math

import jax
import jax.numpy as jnp
import ml_dtypes
import numpy as np
from jax import lax
from jax.experimental import pallas as pl
from jax.experimental.pallas import tpu as pltpu
from jax.sharding import PartitionSpec as P

LANES = 128


def chunk_sizes(x_len):
    ends = 8
    return [ends, x_len - 2 * ends, ends] if x_len > 3 * ends else [ends] * (x_len // ends)

BF16 = jnp.bfloat16
F32 = jnp.float32
NN = (((1,), (0,)), ((), ()))
NT = (((1,), (1,)), ((), ()))


def round_up(value, step):
    return -(-value // step) * step


def synth_np(grid_len, mode_count):
    points = np.arange(grid_len)[:, None]
    mode_index = np.arange(mode_count)[None, :]
    wave_index = np.where(mode_index == 1, grid_len // 2, mode_index // 2)
    angles = (points * wave_index % grid_len) * (2.0 * math.pi / grid_len)
    trig = np.where((mode_index % 2 == 0) | (mode_index == 1), np.cos(angles), np.sin(angles))
    weight = np.where(mode_index < 2, 1.0, 2.0) / grid_len
    return np.where(mode_index == 1, 0.0, trig * np.sqrt(weight))


def slope_np(table, kmax):
    paired = table.reshape(table.shape[0], -1, 2)
    wavenum = np.arange(paired.shape[1]) / kmax
    return np.stack([-wavenum * paired[:, :, 1], wavenum * paired[:, :, 0]], -1).reshape(table.shape)


def halves(table):
    high = table.astype(ml_dtypes.bfloat16)
    low = (table - high.astype(np.float64)).astype(ml_dtypes.bfloat16)
    return high, low


def pieces_of(values):
    high = values.astype(BF16)
    return high, (values - high.astype(F32)).astype(BF16)


def dot(left, right, dims):
    return lax.dot_general(left, right, dims, preferred_element_type=F32)


def dot_data_left(values, high, low, dims=NN):
    top, rest = pieces_of(values)
    return dot(top, high, dims) + (dot(top, low, dims) + dot(rest, high, dims))


def dot_data_right(high, low, values, dims=NT):
    top, rest = pieces_of(values)
    return dot(high, top, dims) + (dot(low, top, dims) + dot(high, rest, dims))


def turn(values, shift):
    shift = shift % values.shape[-1]
    return values if shift == 0 else pltpu.roll(values, shift, axis=values.ndim - 1)


def lane_pack(parts, width, source_lane=0):
    tiles = []
    lane = lax.broadcasted_iota(jnp.int32, parts[0].shape, 1)
    for tile in range(-(-len(parts) * width // LANES)):
        start = tile * LANES
        acc = None
        for idx in range(start // width, min(len(parts) - 1, (start + LANES - 1) // width) + 1):
            moved = turn(parts[idx], idx * width - source_lane)
            acc = moved if acc is None else jnp.where(lane >= idx * width - start, moved, acc)
        tiles.append(acc)
    return tiles


VMEM_LIMIT = 32 * 1024 * 1024
VMEM_MOST = 60 * 1024 * 1024
SHORT = pl.CostEstimate(flops=1024, bytes_accessed=1024, transcendentals=0)
ANY = pl.BlockSpec(memory_space=pl.ANY)
HBM = pl.BlockSpec(memory_space=pltpu.HBM)
SMEM = pl.BlockSpec(memory_space=pltpu.SMEM)
VMEM = pl.BlockSpec(memory_space=pltpu.VMEM)


def params():
    return pltpu.CompilerParams(dimension_semantics=("arbitrary",), vmem_limit_bytes=VMEM_LIMIT)


def still(limit=VMEM_LIMIT):
    return pltpu.CompilerParams(vmem_limit_bytes=limit)


def both_passes(values, high_low, high):
    top, rest = pieces_of(values)
    wide = dot(top, high_low, NN)
    half = high.shape[1]
    return wide[:, :half] + (wide[:, half:] + dot(rest, high, NN))


def whole(array):
    rank = len(array.shape)
    return pl.BlockSpec(array.shape, lambda *_: (0,) * rank)


def first_synth_kernel(dims, place_ref, data_ref, table_ref, *rest):
    sizes, chosen, dests, own = dims
    outs = rest[-len(chosen) * dests - 3 : -3]
    data, rows, sem = rest[-3:]
    _, ky_len, kz_len, _ = data.shape
    group = 5 * kz_len
    copies = [
        pltpu.make_async_copy(data_ref.at[comp], data.at[comp], sem.at[comp]) for comp in range(3)
    ]
    for copy in copies:
        copy.start()
    if ky_len * group < rows.shape[0]:
        rows[ky_len * group :, :] = jnp.zeros((rows.shape[0] - ky_len * group, LANES), F32)
    plain = jnp.concatenate([table_ref[0], table_ref[1]], axis=1)
    slope = jnp.concatenate([table_ref[2], table_ref[3]], axis=1)
    step = 4 if ky_len % 4 == 0 else 2
    for copy in copies:
        copy.wait()

    def body(idx, carry):
        first = idx * step
        lines = [[data[comp, first + k] for comp in range(3)] for k in range(step)]
        found = both_passes(
            jnp.concatenate([v for line in lines for v in line], axis=0), plain, table_ref[0]
        )
        sloped = both_passes(
            jnp.concatenate([v for line in lines for v in line[1:]], axis=0), slope, table_ref[2]
        )
        for k in range(step):
            base = (first + k) * group
            rows[pl.ds(pl.multiple_of(base, 8), 3 * kz_len), :] = found[
                3 * k * kz_len : 3 * (k + 1) * kz_len
            ]
            rows[pl.ds(pl.multiple_of(base + 3 * kz_len, 8), 2 * kz_len), :] = sloped[
                2 * k * kz_len : 2 * (k + 1) * kz_len
            ]
        return carry

    lax.fori_loop(0, ky_len // step, body, 0)

    core = place_ref[1] if own else 1 - place_ref[1]

    def flip(tile, carry):
        found = rows[pl.ds(pl.multiple_of(tile * LANES, LANES), LANES), :].T
        for idx, out in enumerate(outs):
            chunk, k = chosen[idx // dests], idx % dests
            xc = sizes[chunk]
            at = sum(sizes[:chunk]) * dests + k * xc
            spot = core * (out.shape[0] // 2) + tile * xc
            out[pl.ds(pl.multiple_of(spot, 8), xc), :] = found[at : at + xc]
        return carry

    lax.fori_loop(0, rows.shape[0] // LANES, flip, 0, unroll=2)


def first_synth(place, coeffs, table, dims, chosen, lanes, half):
    sizes, dests = dims
    heights = [2 * (lanes // LANES) * sizes[chunk] for chunk in chosen for _ in range(dests)]
    return pl.pallas_call(
        functools.partial(first_synth_kernel, (sizes, chosen, dests, not half)),
        in_specs=[SMEM, ANY, VMEM] + [ANY] * len(half),
        out_specs=[VMEM] * len(heights),
        out_shape=[jax.ShapeDtypeStruct((h, LANES), F32) for h in heights],
        input_output_aliases={3 + k: k for k in range(len(half))},
        scratch_shapes=[
            pltpu.VMEM(coeffs.shape, F32),
            pltpu.VMEM((lanes, LANES), F32),
            pltpu.SemaphoreType.DMA((3,)),
        ],
        compiler_params=still(),
        cost_estimate=SHORT,
        name="first_synth",
    )(place, coeffs, table, *half)


def second_synth_kernel(dims, place_ref, *refs):
    rows, xc, ky_len, kz_len, cols, y_len, pack = dims
    groups = rows // 2
    parts, table_ref, out_refs = refs[:groups], refs[groups], refs[groups + 1 : -1]
    a_ref = refs[-1]
    size = parts[0].shape[0] // 2
    stride = a_ref.shape[0] // rows
    for k, part in enumerate(parts):
        for core in range(2):
            spot = pl.multiple_of(((place_ref[0] ^ k) * 2 + core) * stride, 8)
            a_ref[pl.ds(spot, size), :] = part[core * size : (core + 1) * size, :]
    group = 5 * kz_len
    wide = round_up(group, LANES)
    tiles = size // xc

    def body(at, carry):
        turned = []
        for part in range(pack):
            line = [
                a_ref[pl.ds(tile * xc + at * pack + part, rows, stride=stride), :]
                for tile in range(tiles)
            ]
            found = []
            for ky in range(ky_len):
                start = ky * group
                low, off = divmod(start, LANES)
                window = line[low : low + (wide // LANES) + (1 if off else 0)]
                found.append(turn(jnp.concatenate(window, axis=1), -off)[:, :wide])
            turned.append(jnp.concatenate(found, axis=0).T[:group])
        plain = dot_data_left(jnp.concatenate(turned, axis=0), table_ref[0], table_ref[1])
        slope_in = [t[c * kz_len : (c + 1) * kz_len] for t in turned for c in (0, 2)]
        slope = dot_data_left(jnp.concatenate(slope_in, axis=0), table_ref[2], table_ref[3])
        fields = []
        for part in range(pack):
            own = plain[part * group : (part + 1) * group]
            sl = slope[part * 2 * kz_len : (part + 1) * 2 * kz_len]
            fields.append(
                jnp.concatenate(
                    [
                        own[: 3 * kz_len],
                        own[3 * kz_len : 4 * kz_len] - sl[:kz_len],
                        sl[kz_len:],
                        -own[4 * kz_len :],
                    ],
                    axis=0,
                )
            )
        for dest in range(cols):
            tile, off = divmod(dest * y_len, LANES)
            out_refs[dest][at] = lane_pack(
                [f[:, tile * LANES : (tile + 1) * LANES] for f in fields], y_len, off
            )[0]
        return carry

    lax.fori_loop(0, xc // pack, body, 0)


def second_synth(place, arrived, table, dims):
    rows, xc, ky_len, kz_len, cols, y_len, pack = dims
    packs = xc // pack
    return pl.pallas_call(
        functools.partial(second_synth_kernel, dims),
        in_specs=[SMEM] + [VMEM] * (len(arrived) + 1),
        out_specs=[VMEM] * cols,
        out_shape=[jax.ShapeDtypeStruct((packs, 6 * kz_len, LANES), F32)] * cols,
        scratch_shapes=[
            pltpu.VMEM((rows * (arrived[0].shape[0] // 2 + 8), LANES), F32),
        ],
        compiler_params=still(),
        cost_estimate=SHORT,
        name="second_synth",
    )(place, *arrived, table)


def cross(left, right):
    return [
        left[1] * right[2] - left[2] * right[1],
        left[2] * right[0] - left[0] * right[2],
        left[0] * right[1] - left[1] * right[0],
    ]


def earlier_kernel(count, *refs):
    vels, vorts, out_ref = refs[:count], refs[count : 2 * count], refs[2 * count]
    pack, y_len = out_ref.shape[1:3]
    for part in range(pack):
        def body(step, carry):
            at = pl.ds(pl.multiple_of(step * 8, 8), 8)
            total = None
            for vel, vort in zip(vels, vorts):
                term = cross(
                    [vel[0, c, part, at, :] for c in range(3)],
                    [vort[0, c, part, at, :] for c in range(3)],
                )
                total = term if total is None else [a + b for a, b in zip(total, term)]
            for comp in range(3):
                out_ref[comp, part, at, :] = total[comp]
            return carry

        lax.fori_loop(0, y_len // 8, body, 0, unroll=2)


def earlier(velocity, vorticity, start, xc, pack):
    orders, _, _, y_len, grid_len = velocity.shape
    packs = xc // pack
    block = (1, 3, pack, y_len, grid_len)

    def at(order):
        return pl.BlockSpec(block, lambda i: (order, 0, start // pack + i, 0, 0))

    specs = [at(k) for k in range(1, orders)] + [at(orders - k) for k in range(1, orders)]
    size = xc * y_len * grid_len
    return pl.pallas_call(
        functools.partial(earlier_kernel, orders - 1),
        grid=(packs,),
        in_specs=specs,
        out_specs=pl.BlockSpec((3, pack, y_len, grid_len), lambda i: (0, i, 0, 0)),
        out_shape=jax.ShapeDtypeStruct((3, xc, y_len, grid_len), F32),
        compiler_params=params(),
        cost_estimate=SHORT,
        name="earlier_orders",
    )(*[velocity] * (orders - 1), *[vorticity] * (orders - 1))


def third_kernel(dims, place_ref, *refs):
    begin, kz_len, cols, y_len, pack = dims
    b_refs, stored_refs, table_ref = refs[:cols], refs[cols : cols + 3], refs[cols + 3]
    data, sem = refs[-2:]
    out_refs = refs[-2 - cols : -2]
    grid_len = table_ref.shape[2]
    xc = data.shape[2]
    packs = xc // pack

    def copies(at):
        spot = pl.ds(at * pack, pack)
        far = pl.ds(begin + at * pack, pack)
        sources = [ref.at[0, :, far] for ref in stored_refs[:2]] + [stored_refs[2].at[:, spot]]
        return [
            pltpu.make_async_copy(source, data.at[idx, :, spot], sem.at[idx, at])
            for idx, source in enumerate(sources)
        ]

    for at in range(packs):
        for copy in copies(at):
            copy.start()

    def body(at, carry):
        def stack(field):
            return jnp.concatenate(
                [b_refs[k][at, field * kz_len : (field + 1) * kz_len, :] for k in range(cols)], axis=0
            ).T

        lines = jnp.concatenate([stack(field) for field in range(6)], axis=0)
        plain = dot_data_left(lines, table_ref[0], table_ref[1])
        slope = dot_data_left(lines[: 2 * LANES], table_ref[2], table_ref[3])
        new = [plain[f * LANES : (f + 1) * LANES] for f in range(6)]
        vel_new = new[:3]
        vort_new = [new[4] - slope[LANES:], slope[:LANES] + new[5], new[3]]
        for copy in copies(at):
            copy.wait()
        spot = pl.ds(at * pack, pack)
        flat = (pack * y_len, grid_len)
        vel, vort, base = [[data[idx, c, spot].reshape(flat) for c in range(3)] for idx in range(3)]
        one, two = cross(vel_new, vort), cross(vel, vort_new)
        total = [one[c] + two[c] + base[c] for c in range(3)]
        result = dot_data_right(table_ref[0], table_ref[1], jnp.concatenate(total, axis=0))
        for k in range(cols):
            for comp in range(3):
                out_refs[k][at, comp * kz_len : (comp + 1) * kz_len, :] = result[
                    k * kz_len : (k + 1) * kz_len, comp * LANES : (comp + 1) * LANES
                ]
        return carry

    lax.fori_loop(0, packs, body, 0)


def third(place, arrived, velocity, vorticity, base, table, begin, dims):
    kz_len, cols, y_len, pack = dims
    packs = arrived[0].shape[0]
    grid_len = velocity.shape[-1]
    return pl.pallas_call(
        functools.partial(third_kernel, (begin, *dims)),
        in_specs=[SMEM] + [VMEM] * cols + [ANY] * 3 + [VMEM],
        out_specs=[VMEM] * cols,
        out_shape=[jax.ShapeDtypeStruct((packs, 3 * kz_len, LANES), F32)] * cols,
        scratch_shapes=[
            pltpu.VMEM((3, 3, packs * pack, y_len, grid_len), F32),
            pltpu.SemaphoreType.DMA((3, packs)),
        ],
        compiler_params=still(),
        cost_estimate=SHORT,
        name="third_dimension",
    )(place, *arrived, velocity, vorticity, base, table)


def second_back_kernel(dims, place_ref, *refs):
    rows, xc, ky_len, kz_len, cols, y_len, pack = dims
    c_refs, table_ref, outs, all_ref = refs[:cols], refs[cols], refs[cols + 1 : -1], refs[-1]
    width = 3 * kz_len
    high_pad = round_up(width, LANES)

    def body(at, carry):
        lines = []
        for part in range(pack):
            tiles = lane_pack(
                [c_ref[at] for c_ref in c_refs], y_len, part * y_len
            )
            lines.append(jnp.concatenate(tiles, axis=1))
            if high_pad > width:
                lines.append(jnp.zeros((high_pad - width, cols * y_len), F32))
        result = dot_data_right(table_ref[0], table_ref[1], jnp.concatenate(lines, axis=0))
        for part in range(pack):
            own = result[:, part * high_pad : (part + 1) * high_pad]
            tiles = lane_pack([own[ky * rows : (ky + 1) * rows] for ky in range(ky_len)], width)
            for idx, tile in enumerate(tiles):
                spot = idx * xc + at * pack + part
                all_ref[pl.ds(spot, rows, stride=len(tiles) * xc), :] = tile
        return carry

    lax.fori_loop(0, xc // pack, body, 0)
    size = all_ref.shape[0] // len(outs)
    for k, out in enumerate(outs):
        out[...] = all_ref[pl.ds(pl.multiple_of((place_ref[0] ^ k) * size, 8), size), :]


def second_back(place, arrived, table, dims):
    rows, xc, ky_len, kz_len, cols, y_len, pack = dims
    size = round_up(ky_len * 3 * kz_len, LANES) // LANES * xc
    groups = rows // 2
    return pl.pallas_call(
        functools.partial(second_back_kernel, dims),
        in_specs=[SMEM] + [VMEM] * (cols + 1),
        out_specs=[VMEM] * groups,
        out_shape=[jax.ShapeDtypeStruct((2 * size, LANES), F32)] * groups,
        scratch_shapes=[pltpu.VMEM((rows * size, LANES), F32)],
        compiler_params=still(),
        cost_estimate=SHORT,
        name="second_back",
    )(place, *arrived, table)


def first_back_kernel(dims, place_ref, *refs):
    count, sizes, own = dims
    parts, table_ref, out_ref = refs[:count], refs[count], refs[count + 1]
    groups = count // len(sizes)
    core = place_ref[1] if own else 1 - place_ref[1]
    for tile in range(out_ref.shape[1] // LANES):
        found = []
        for idx, part in enumerate(parts):
            xc = sizes[idx // groups]
            spot = pl.multiple_of(core * (part.shape[0] // 2) + tile * xc, 8)
            found.append(part[pl.ds(spot, xc), :])
        out_ref[:, tile * LANES : (tile + 1) * LANES] = dot_data_right(
            table_ref[0], table_ref[1], jnp.concatenate(found, axis=0), NN
        )


def first_back(place, parts, table, sizes, own):
    count = len(parts)
    tiles = parts[0].shape[0] // 2 // sizes[0]
    return pl.pallas_call(
        functools.partial(first_back_kernel, (count, tuple(sizes), own)),
        in_specs=[SMEM] + [VMEM] * (count + 1),
        out_specs=VMEM,
        out_shape=jax.ShapeDtypeStruct((table.shape[1], tiles * LANES), F32),
        compiler_params=still(),
        cost_estimate=SHORT,
        name="first_back",
    )(place, *parts, table)


def last_kernel(dims, *refs):
    kz_len, modes, scale = dims
    wave_y_ref, wave_x_ref, wave_z_ref, *sums, out_ref, rows = refs
    pair = 2 * 3 * kz_len
    at = pl.program_id(0)

    @pl.when(at == 0)
    def _():
        for tile in range(rows.shape[0] // LANES):
            lanes = slice(tile * LANES, (tile + 1) * LANES)
            rows[lanes, 0:modes] = functools.reduce(jnp.add, [part[:, lanes] for part in sums]).T

    spec = rows[pl.ds(pl.multiple_of(at * pair, 8), pair), :]
    wide = spec.shape[1]
    wave_x = jnp.broadcast_to(wave_x_ref[0:1, :], (kz_len, wide))
    wave_z = wave_z_ref[...]
    wave_y = wave_y_ref[at]
    even_x = lax.broadcasted_iota(jnp.int32, (kz_len, wide), 1) % 2 == 0
    even_z = lax.broadcasted_iota(jnp.int32, (kz_len, wide), 0) % 2 == 0

    def slope_x(value):
        return jnp.where(even_x, turn(value, -1), -turn(value, 1)) * wave_x

    def slope_z(value):
        return (
            jnp.where(
                even_z,
                pltpu.roll(value, kz_len - 1, axis=0),
                -pltpu.roll(value, 1, axis=0),
            )
            * wave_z
        )

    s = [
        [spec[(y * 3 + c) * kz_len : (y * 3 + c + 1) * kz_len] for c in range(3)] for y in range(2)
    ]
    square = wave_x * wave_x + wave_z * wave_z + wave_y * wave_y
    positive = square > 0
    safe = jnp.where(positive, square, 1.0)
    potential = []
    for y in range(2):
        along_y = s[1 - y][1] * (wave_y if y == 0 else -wave_y)
        divergence = slope_x(s[y][0]) + along_y + slope_z(s[y][2])
        potential.append(jnp.where(positive, divergence / safe, 0.0))
    for y in range(2):
        along_y = potential[1 - y] * (wave_y if y == 0 else -wave_y)
        found = [
            s[y][0] + slope_x(potential[y]),
            s[y][1] + along_y,
            s[y][2] + slope_z(potential[y]),
        ]
        for comp in range(3):
            out_ref[comp, y] = (found[comp] * scale)[:, :modes]


def last(sums, wave_y, wave_x, wave_z, ky_len, kz_len, scale):
    modes, lanes = sums[0].shape
    return pl.pallas_call(
        functools.partial(last_kernel, (kz_len, modes, scale)),
        grid=(ky_len // 2,),
        in_specs=[SMEM, *[whole(a) for a in (wave_x, wave_z, *sums)]],
        out_specs=pl.BlockSpec((3, 2, kz_len, modes), lambda i: (0, i, 0, 0)),
        out_shape=jax.ShapeDtypeStruct((3, ky_len, kz_len, modes), F32),
        scratch_shapes=[pltpu.VMEM((lanes, wave_x.shape[1]), F32)],
        compiler_params=params(),
        cost_estimate=SHORT,
        name="last_projection",
    )(wave_y, wave_x, wave_z, *sums)


def after(value, *earlier_values):
    return lax.optimization_barrier((value, earlier_values))[0]


def shards(new_velocity, stored_velocity, stored_vorticity):
    rows = lax.axis_size("row")
    cols = lax.axis_size("col")
    _, ky_len, kz_own, modes = new_velocity.shape
    orders, _, x_len, y_len, grid_len = stored_velocity.shape
    kz_len = round_up(kz_own, 8)
    kmax = modes // 2 - 1
    sizes = chunk_sizes(x_len)
    chunks = len(sizes)
    begins = [sum(sizes[:k]) for k in range(chunks)]
    pack = LANES // y_len
    wide = round_up(modes, LANES)
    group = 5 * kz_len
    lanes = round_up(ky_len * group, 256)

    basis = synth_np(grid_len, modes)
    slope = slope_np(basis, kmax)
    y_order = (np.arange(rows)[None, :] * ky_len + np.arange(ky_len)[:, None]).reshape(-1)

    groups = rows // 2
    row, col = lax.axis_index("row"), lax.axis_index("col")
    place = jnp.stack([row // 2, row % 2, col]).astype(jnp.int32)

    def own_table(tables, axis):
        return lax.dynamic_index_in_dim(jnp.asarray(np.stack(tables)), lax.axis_index(axis), 0, False)

    def x_points(row):
        owner = np.array([row ^ (2 * k) for k in range(groups)])
        return np.concatenate(
            [
                (owner[:, None] * x_len + begin + np.arange(xc)[None, :]).reshape(-1)
                for begin, xc in zip(begins, sizes)
            ]
        )

    def halves_of(plain, sloped):
        return np.stack([part for table in (plain, sloped) for part in halves(table)])

    def y_table(col):
        points = np.concatenate([(col ^ k) * y_len + np.arange(y_len) for k in range(cols)])
        return halves_of(basis[points].T[y_order], slope[points].T[y_order])

    def z_table(col):
        def spread(table):
            parts = table.T.reshape(cols, kz_own, grid_len)[[col ^ k for k in range(cols)]]
            parts = np.pad(parts, ((0, 0), (0, kz_len - kz_own), (0, 0)))
            return parts.reshape(cols * kz_len, grid_len)

        return halves_of(spread(basis), spread(slope))

    table_x = own_table(
        [halves_of(basis[x_points(row)].T, slope[x_points(row)].T) for row in range(rows)], "row"
    )
    table_y = own_table([y_table(col) for col in range(cols)], "col")
    table_z = own_table([z_table(col) for col in range(cols)], "col")

    def wave_of(index):
        return (index // 2).astype(F32) / kmax

    mode = jnp.arange(wide, dtype=jnp.int32)
    wave_x = jnp.broadcast_to(jnp.where(mode < modes, wave_of(mode), 0.0)[None, :], (8, wide))
    ky_first = lax.axis_index("row") * ky_len + 2 * jnp.arange(ky_len // 2, dtype=jnp.int32)
    wave_y = wave_of(ky_first)
    kz = lax.axis_index("col") * kz_own + jnp.arange(kz_len, dtype=jnp.int32)
    wave_z = jnp.broadcast_to(wave_of(kz)[:, None], (kz_len, wide))

    coeffs = new_velocity
    if kz_len > kz_own:
        coeffs = jnp.pad(coeffs, ((0, 0), (0, 0), (0, kz_len - kz_own), (0, 0)))

    def exchange(values, axis, shift, size):
        return [
            lax.ppermute(value, axis, [(src, src ^ (k << shift)) for src in range(size)]) if k else value
            for k, value in enumerate(values)
        ]

    def core_swap(value):
        return lax.ppermute(value, "row", [(src, src ^ 1) for src in range(rows)])

    dims = [(rows, xc, ky_len, kz_len, cols, y_len, pack) for xc in sizes]
    shape = (tuple(sizes), groups)
    other = core_swap(coeffs)
    small = (place, table_x, table_y, table_z, wave_x, wave_y, wave_z)
    place, table_x, table_y, table_z, wave_x, wave_y, wave_z = lax.optimization_barrier(small)

    def run_first(chosen, gate):
        own = coeffs if gate is None else after(coeffs, gate)
        found = first_synth(place, own, table_x, shape, chosen, lanes, ())
        found = first_synth(place, other, table_x, shape, chosen, lanes, found)
        return {chunk: list(found[k * groups : (k + 1) * groups]) for k, chunk in enumerate(chosen)}

    sent = run_first((0,), None)
    if chunks > 1:
        sent.update(run_first(tuple(range(1, chunks)), sent[0][0]))
    latest = sent[chunks - 1][0]

    def ordered(kernel, operands, *others):
        nonlocal latest
        operands = after(operands, latest)
        found = kernel(operands, *others)
        latest = found[0] if isinstance(found, (list, tuple)) else found
        return found

    stored = (stored_velocity, stored_vorticity)

    def run_earlier(chunk):
        return ordered(lambda values: earlier(*values, begins[chunk], sizes[chunk], pack), stored)

    def z_exchange(values, *gates):
        found = [values[0]]
        for k in range(1, groups):
            value = after(values[k], *gates) if gates else values[k]
            found.append(lax.ppermute(value, "row", [(src, src ^ (2 * k)) for src in range(rows)]))
        return found

    first, second, middle, back, base = {}, {}, {}, {}, {}
    for step in range(chunks):
        first[step] = z_exchange(sent[step], *([first[step - 1]] if step else []))

    def run_second(at):
        found = ordered(lambda values: second_synth(place, values, table_y, dims[at]), first[at])
        if at:
            found = [found[0]] + [after(value, second[at - 1]) for value in found[1:]]
        second[at] = exchange(found, "col", 0, cols)

    def run_third(at):
        found = ordered(
            lambda values: third(
                place, values, *stored, base[at], table_z, begins[at], dims[at][3:]
            ),
            second[at],
        )
        middle[at] = exchange(found, "col", 0, cols)

    def run_back(at):
        values = after(middle[at], back[at - 1]) if 0 < at < chunks - 1 else middle[at]
        found = ordered(lambda values: second_back(place, values, table_y, dims[at]), values)
        back[at] = z_exchange(found, *([back[at - 1]] if at else []))

    def run_base(at):
        base[at] = run_earlier(at)

    plan = [(run_base, 0), (run_second, 0), (run_base, 1), (run_third, 0), (run_base, 2), (run_second, 1)]
    plan += [(run_back, 0), (run_second, 2), (run_third, 1), (run_third, 2), (run_back, 1), (run_back, 2)]
    for action, at in plan:
        if at < chunks:
            action(at)
    parts = [value for step in range(chunks) for value in back[step]]
    away = first_back(place, parts, table_x, sizes, False)
    home = first_back(place, parts, after(table_x, away), sizes, True)
    sums = [home, core_swap(away)]
    result = last(sums, wave_y, wave_x, wave_z, ky_len, kz_len, 1.0 / (orders + 1))
    return result[:, :, :kz_own] if kz_len > kz_own else result


def solution(mesh):
    return jax.shard_map(
        shards,
        mesh=mesh,
        in_specs=(
            P(None, "row", "col", None),
            P(None, None, "row", "col", None),
            P(None, None, "row", "col", None),
        ),
        out_specs=P(None, "row", "col", None),
        check_vma=False,
    )
```

```python
import functools
import math

import jax
import jax.numpy as jnp
import ml_dtypes
import numpy as np
from jax import lax
from jax.experimental import pallas as pl
from jax.experimental.pallas import tpu as pltpu
from jax.sharding import PartitionSpec as P

LANES = 128


def chunk_sizes(x_len):
    ends = 8
    return [ends, x_len - 2 * ends, ends] if x_len > 3 * ends else [ends] * (x_len // ends)

BF16 = jnp.bfloat16
F32 = jnp.float32
NN = (((1,), (0,)), ((), ()))
NT = (((1,), (1,)), ((), ()))


def round_up(value, step):
    return -(-value // step) * step


def synth_np(grid_len, mode_count):
    points = np.arange(grid_len)[:, None]
    mode_index = np.arange(mode_count)[None, :]
    wave_index = np.where(mode_index == 1, grid_len // 2, mode_index // 2)
    angles = (points * wave_index % grid_len) * (2.0 * math.pi / grid_len)
    trig = np.where((mode_index % 2 == 0) | (mode_index == 1), np.cos(angles), np.sin(angles))
    weight = np.where(mode_index < 2, 1.0, 2.0) / grid_len
    return np.where(mode_index == 1, 0.0, trig * np.sqrt(weight))


def slope_np(table, kmax):
    paired = table.reshape(table.shape[0], -1, 2)
    wavenum = np.arange(paired.shape[1]) / kmax
    return np.stack([-wavenum * paired[:, :, 1], wavenum * paired[:, :, 0]], -1).reshape(table.shape)


def halves(table):
    high = table.astype(ml_dtypes.bfloat16)
    low = (table - high.astype(np.float64)).astype(ml_dtypes.bfloat16)
    return high, low


def pieces_of(values):
    high = values.astype(BF16)
    return high, (values - high.astype(F32)).astype(BF16)


def dot(left, right, dims):
    return lax.dot_general(left, right, dims, preferred_element_type=F32)


def dot_data_left(values, high, low, dims=NN):
    top, rest = pieces_of(values)
    return dot(top, high, dims) + (dot(top, low, dims) + dot(rest, high, dims))


def dot_data_right(high, low, values, dims=NT):
    top, rest = pieces_of(values)
    return dot(high, top, dims) + (dot(low, top, dims) + dot(high, rest, dims))


def turn(values, shift):
    shift = shift % values.shape[-1]
    return values if shift == 0 else pltpu.roll(values, shift, axis=values.ndim - 1)


def lane_pack(parts, width, source_lane=0):
    tiles = []
    lane = lax.broadcasted_iota(jnp.int32, parts[0].shape, 1)
    for tile in range(-(-len(parts) * width // LANES)):
        start = tile * LANES
        acc = None
        for idx in range(start // width, min(len(parts) - 1, (start + LANES - 1) // width) + 1):
            moved = turn(parts[idx], idx * width - source_lane)
            acc = moved if acc is None else jnp.where(lane >= idx * width - start, moved, acc)
        tiles.append(acc)
    return tiles


VMEM_LIMIT = 32 * 1024 * 1024
VMEM_MOST = 60 * 1024 * 1024
SHORT = pl.CostEstimate(flops=1024, bytes_accessed=1024, transcendentals=0)
ANY = pl.BlockSpec(memory_space=pl.ANY)
HBM = pl.BlockSpec(memory_space=pltpu.HBM)
SMEM = pl.BlockSpec(memory_space=pltpu.SMEM)
VMEM = pl.BlockSpec(memory_space=pltpu.VMEM)


def params():
    return pltpu.CompilerParams(dimension_semantics=("arbitrary",), vmem_limit_bytes=VMEM_LIMIT)


def still(limit=VMEM_LIMIT):
    return pltpu.CompilerParams(vmem_limit_bytes=limit)


def both_passes(values, high_low, high):
    top, rest = pieces_of(values)
    wide = dot(top, high_low, NN)
    half = high.shape[1]
    return wide[:, :half] + (wide[:, half:] + dot(rest, high, NN))


def whole(array):
    rank = len(array.shape)
    return pl.BlockSpec(array.shape, lambda *_: (0,) * rank)


def first_synth_kernel(dims, place_ref, data_ref, table_ref, *rest):
    sizes, chosen, dests, own = dims
    outs = rest[-len(chosen) * dests - 3 : -3]
    data, rows, sem = rest[-3:]
    _, ky_len, kz_len, _ = data.shape
    group = 5 * kz_len
    copies = [
        pltpu.make_async_copy(data_ref.at[comp], data.at[comp], sem.at[comp]) for comp in range(3)
    ]
    for copy in copies:
        copy.start()
    if ky_len * group < rows.shape[0]:
        rows[ky_len * group :, :] = jnp.zeros((rows.shape[0] - ky_len * group, LANES), F32)
    plain = jnp.concatenate([table_ref[0], table_ref[1]], axis=1)
    slope = jnp.concatenate([table_ref[2], table_ref[3]], axis=1)
    step = 4 if ky_len % 4 == 0 else 2
    for copy in copies:
        copy.wait()

    def body(idx, carry):
        first = idx * step
        lines = [[data[comp, first + k] for comp in range(3)] for k in range(step)]
        found = both_passes(
            jnp.concatenate([v for line in lines for v in line], axis=0), plain, table_ref[0]
        )
        sloped = both_passes(
            jnp.concatenate([v for line in lines for v in line[1:]], axis=0), slope, table_ref[2]
        )
        for k in range(step):
            base = (first + k) * group
            rows[pl.ds(pl.multiple_of(base, 8), 3 * kz_len), :] = found[
                3 * k * kz_len : 3 * (k + 1) * kz_len
            ]
            rows[pl.ds(pl.multiple_of(base + 3 * kz_len, 8), 2 * kz_len), :] = sloped[
                2 * k * kz_len : 2 * (k + 1) * kz_len
            ]
        return carry

    lax.fori_loop(0, ky_len // step, body, 0)

    core = place_ref[1] if own else 1 - place_ref[1]

    def flip(tile, carry):
        found = rows[pl.ds(pl.multiple_of(tile * LANES, LANES), LANES), :].T
        for idx, out in enumerate(outs):
            chunk, k = chosen[idx // dests], idx % dests
            xc = sizes[chunk]
            at = sum(sizes[:chunk]) * dests + k * xc
            spot = core * (out.shape[0] // 2) + tile * xc
            out[pl.ds(pl.multiple_of(spot, 8), xc), :] = found[at : at + xc]
        return carry

    lax.fori_loop(0, rows.shape[0] // LANES, flip, 0, unroll=2)


def first_synth(place, coeffs, table, dims, chosen, lanes, half):
    sizes, dests = dims
    heights = [2 * (lanes // LANES) * sizes[chunk] for chunk in chosen for _ in range(dests)]
    return pl.pallas_call(
        functools.partial(first_synth_kernel, (sizes, chosen, dests, not half)),
        in_specs=[SMEM, ANY, VMEM] + [ANY] * len(half),
        out_specs=[VMEM] * len(heights),
        out_shape=[jax.ShapeDtypeStruct((h, LANES), F32) for h in heights],
        input_output_aliases={3 + k: k for k in range(len(half))},
        scratch_shapes=[
            pltpu.VMEM(coeffs.shape, F32),
            pltpu.VMEM((lanes, LANES), F32),
            pltpu.SemaphoreType.DMA((3,)),
        ],
        compiler_params=still(),
        cost_estimate=SHORT,
        name="first_synth",
    )(place, coeffs, table, *half)


def second_synth_kernel(dims, place_ref, *refs):
    rows, xc, ky_len, kz_len, cols, y_len, pack = dims
    groups = rows // 2
    parts, table_ref, out_refs = refs[:groups], refs[groups], refs[groups + 1 : -1]
    a_ref = refs[-1]
    size = parts[0].shape[0] // 2
    stride = a_ref.shape[0] // rows
    for k, part in enumerate(parts):
        for core in range(2):
            spot = pl.multiple_of(((place_ref[0] ^ k) * 2 + core) * stride, 8)
            a_ref[pl.ds(spot, size), :] = part[core * size : (core + 1) * size, :]
    group = 5 * kz_len
    wide = round_up(group, LANES)
    tiles = size // xc

    def body(at, carry):
        turned = []
        for part in range(pack):
            line = [
                a_ref[pl.ds(tile * xc + at * pack + part, rows, stride=stride), :]
                for tile in range(tiles)
            ]
            found = []
            for ky in range(ky_len):
                start = ky * group
                low, off = divmod(start, LANES)
                window = line[low : low + (wide // LANES) + (1 if off else 0)]
                found.append(turn(jnp.concatenate(window, axis=1), -off)[:, :wide])
            turned.append(jnp.concatenate(found, axis=0).T[:group])
        plain = dot_data_left(jnp.concatenate(turned, axis=0), table_ref[0], table_ref[1])
        slope_in = [t[c * kz_len : (c + 1) * kz_len] for t in turned for c in (0, 2)]
        slope = dot_data_left(jnp.concatenate(slope_in, axis=0), table_ref[2], table_ref[3])
        fields = []
        for part in range(pack):
            own = plain[part * group : (part + 1) * group]
            sl = slope[part * 2 * kz_len : (part + 1) * 2 * kz_len]
            fields.append(
                jnp.concatenate(
                    [
                        own[: 3 * kz_len],
                        own[3 * kz_len : 4 * kz_len] - sl[:kz_len],
                        sl[kz_len:],
                        -own[4 * kz_len :],
                    ],
                    axis=0,
                )
            )
        for dest in range(cols):
            tile, off = divmod(dest * y_len, LANES)
            out_refs[dest][at] = lane_pack(
                [f[:, tile * LANES : (tile + 1) * LANES] for f in fields], y_len, off
            )[0]
        return carry

    lax.fori_loop(0, xc // pack, body, 0)


def second_synth(place, arrived, table, dims):
    rows, xc, ky_len, kz_len, cols, y_len, pack = dims
    packs = xc // pack
    return pl.pallas_call(
        functools.partial(second_synth_kernel, dims),
        in_specs=[SMEM] + [VMEM] * (len(arrived) + 1),
        out_specs=[VMEM] * cols,
        out_shape=[jax.ShapeDtypeStruct((packs, 6 * kz_len, LANES), F32)] * cols,
        scratch_shapes=[
            pltpu.VMEM((rows * (arrived[0].shape[0] // 2 + 8), LANES), F32),
        ],
        compiler_params=still(),
        cost_estimate=SHORT,
        name="second_synth",
    )(place, *arrived, table)


def cross(left, right):
    return [
        left[1] * right[2] - left[2] * right[1],
        left[2] * right[0] - left[0] * right[2],
        left[0] * right[1] - left[1] * right[0],
    ]


def earlier_kernel(count, *refs):
    vels, vorts, out_ref = refs[:count], refs[count : 2 * count], refs[2 * count]
    pack, y_len = out_ref.shape[1:3]
    for part in range(pack):
        def body(step, carry):
            at = pl.ds(pl.multiple_of(step * 8, 8), 8)
            total = None
            for vel, vort in zip(vels, vorts):
                term = cross(
                    [vel[0, c, part, at, :] for c in range(3)],
                    [vort[0, c, part, at, :] for c in range(3)],
                )
                total = term if total is None else [a + b for a, b in zip(total, term)]
            for comp in range(3):
                out_ref[comp, part, at, :] = total[comp]
            return carry

        lax.fori_loop(0, y_len // 8, body, 0, unroll=2)


def earlier(velocity, vorticity, start, xc, pack):
    orders, _, _, y_len, grid_len = velocity.shape
    packs = xc // pack
    block = (1, 3, pack, y_len, grid_len)

    def at(order):
        return pl.BlockSpec(block, lambda i: (order, 0, start // pack + i, 0, 0))

    specs = [at(k) for k in range(1, orders)] + [at(orders - k) for k in range(1, orders)]
    size = xc * y_len * grid_len
    return pl.pallas_call(
        functools.partial(earlier_kernel, orders - 1),
        grid=(packs,),
        in_specs=specs,
        out_specs=pl.BlockSpec((3, pack, y_len, grid_len), lambda i: (0, i, 0, 0)),
        out_shape=jax.ShapeDtypeStruct((3, xc, y_len, grid_len), F32),
        compiler_params=params(),
        cost_estimate=SHORT,
        name="earlier_orders",
    )(*[velocity] * (orders - 1), *[vorticity] * (orders - 1))


def third_kernel(dims, place_ref, *refs):
    begin, kz_len, cols, y_len, pack = dims
    b_refs, stored_refs, table_ref = refs[:cols], refs[cols : cols + 3], refs[cols + 3]
    data, sem = refs[-2:]
    out_refs = refs[-2 - cols : -2]
    grid_len = table_ref.shape[2]
    xc = data.shape[2]
    packs = xc // pack

    def copies(at):
        spot = pl.ds(at * pack, pack)
        far = pl.ds(begin + at * pack, pack)
        sources = [ref.at[0, :, far] for ref in stored_refs[:2]] + [stored_refs[2].at[:, spot]]
        return [
            pltpu.make_async_copy(source, data.at[idx, :, spot], sem.at[idx, at])
            for idx, source in enumerate(sources)
        ]

    for at in range(packs):
        for copy in copies(at):
            copy.start()

    def body(at, carry):
        def stack(field):
            return jnp.concatenate(
                [b_refs[k][at, field * kz_len : (field + 1) * kz_len, :] for k in range(cols)], axis=0
            ).T

        lines = jnp.concatenate([stack(field) for field in range(6)], axis=0)
        plain = dot_data_left(lines, table_ref[0], table_ref[1])
        slope = dot_data_left(lines[: 2 * LANES], table_ref[2], table_ref[3])
        new = [plain[f * LANES : (f + 1) * LANES] for f in range(6)]
        vel_new = new[:3]
        vort_new = [new[4] - slope[LANES:], slope[:LANES] + new[5], new[3]]
        for copy in copies(at):
            copy.wait()
        spot = pl.ds(at * pack, pack)
        flat = (pack * y_len, grid_len)
        vel, vort, base = [[data[idx, c, spot].reshape(flat) for c in range(3)] for idx in range(3)]
        one, two = cross(vel_new, vort), cross(vel, vort_new)
        total = [one[c] + two[c] + base[c] for c in range(3)]
        result = dot_data_right(table_ref[0], table_ref[1], jnp.concatenate(total, axis=0))
        for k in range(cols):
            for comp in range(3):
                out_refs[k][at, comp * kz_len : (comp + 1) * kz_len, :] = result[
                    k * kz_len : (k + 1) * kz_len, comp * LANES : (comp + 1) * LANES
                ]
        return carry

    lax.fori_loop(0, packs, body, 0)


def third(place, arrived, velocity, vorticity, base, table, begin, dims):
    kz_len, cols, y_len, pack = dims
    packs = arrived[0].shape[0]
    grid_len = velocity.shape[-1]
    return pl.pallas_call(
        functools.partial(third_kernel, (begin, *dims)),
        in_specs=[SMEM] + [VMEM] * cols + [ANY] * 3 + [VMEM],
        out_specs=[VMEM] * cols,
        out_shape=[jax.ShapeDtypeStruct((packs, 3 * kz_len, LANES), F32)] * cols,
        scratch_shapes=[
            pltpu.VMEM((3, 3, packs * pack, y_len, grid_len), F32),
            pltpu.SemaphoreType.DMA((3, packs)),
        ],
        compiler_params=still(),
        cost_estimate=SHORT,
        name="third_dimension",
    )(place, *arrived, velocity, vorticity, base, table)


def second_back_kernel(dims, place_ref, *refs):
    rows, xc, ky_len, kz_len, cols, y_len, pack = dims
    c_refs, table_ref, outs, all_ref = refs[:cols], refs[cols], refs[cols + 1 : -1], refs[-1]
    width = 3 * kz_len
    high_pad = round_up(width, LANES)

    def body(at, carry):
        lines = []
        for part in range(pack):
            tiles = lane_pack(
                [c_ref[at] for c_ref in c_refs], y_len, part * y_len
            )
            lines.append(jnp.concatenate(tiles, axis=1))
            if high_pad > width:
                lines.append(jnp.zeros((high_pad - width, cols * y_len), F32))
        result = dot_data_right(table_ref[0], table_ref[1], jnp.concatenate(lines, axis=0))
        for part in range(pack):
            own = result[:, part * high_pad : (part + 1) * high_pad]
            tiles = lane_pack([own[ky * rows : (ky + 1) * rows] for ky in range(ky_len)], width)
            for idx, tile in enumerate(tiles):
                spot = idx * xc + at * pack + part
                all_ref[pl.ds(spot, rows, stride=len(tiles) * xc), :] = tile
        return carry

    lax.fori_loop(0, xc // pack, body, 0)
    size = all_ref.shape[0] // len(outs)
    for k, out in enumerate(outs):
        out[...] = all_ref[pl.ds(pl.multiple_of((place_ref[0] ^ k) * size, 8), size), :]


def second_back(place, arrived, table, dims):
    rows, xc, ky_len, kz_len, cols, y_len, pack = dims
    size = round_up(ky_len * 3 * kz_len, LANES) // LANES * xc
    groups = rows // 2
    return pl.pallas_call(
        functools.partial(second_back_kernel, dims),
        in_specs=[SMEM] + [VMEM] * (cols + 1),
        out_specs=[VMEM] * groups,
        out_shape=[jax.ShapeDtypeStruct((2 * size, LANES), F32)] * groups,
        scratch_shapes=[pltpu.VMEM((rows * size, LANES), F32)],
        compiler_params=still(),
        cost_estimate=SHORT,
        name="second_back",
    )(place, *arrived, table)


def first_back_kernel(dims, place_ref, *refs):
    count, sizes, own = dims
    parts, table_ref, out_ref = refs[:count], refs[count], refs[count + 1]
    groups = count // len(sizes)
    core = place_ref[1] if own else 1 - place_ref[1]
    for tile in range(out_ref.shape[1] // LANES):
        found = []
        for idx, part in enumerate(parts):
            xc = sizes[idx // groups]
            spot = pl.multiple_of(core * (part.shape[0] // 2) + tile * xc, 8)
            found.append(part[pl.ds(spot, xc), :])
        out_ref[:, tile * LANES : (tile + 1) * LANES] = dot_data_right(
            table_ref[0], table_ref[1], jnp.concatenate(found, axis=0), NN
        )


def first_back(place, parts, table, sizes, own):
    count = len(parts)
    tiles = parts[0].shape[0] // 2 // sizes[0]
    return pl.pallas_call(
        functools.partial(first_back_kernel, (count, tuple(sizes), own)),
        in_specs=[SMEM] + [VMEM] * (count + 1),
        out_specs=VMEM,
        out_shape=jax.ShapeDtypeStruct((table.shape[1], tiles * LANES), F32),
        compiler_params=still(),
        cost_estimate=SHORT,
        name="first_back",
    )(place, *parts, table)


def last_kernel(dims, *refs):
    kz_len, modes, scale = dims
    wave_y_ref, wave_x_ref, wave_z_ref, *sums, out_ref, rows = refs
    pair = 2 * 3 * kz_len
    at = pl.program_id(0)

    @pl.when(at == 0)
    def _():
        for tile in range(rows.shape[0] // LANES):
            lanes = slice(tile * LANES, (tile + 1) * LANES)
            rows[lanes, 0:modes] = functools.reduce(jnp.add, [part[:, lanes] for part in sums]).T

    spec = rows[pl.ds(pl.multiple_of(at * pair, 8), pair), :]
    wide = spec.shape[1]
    wave_x = jnp.broadcast_to(wave_x_ref[0:1, :], (kz_len, wide))
    wave_z = wave_z_ref[...]
    wave_y = wave_y_ref[at]
    even_x = lax.broadcasted_iota(jnp.int32, (kz_len, wide), 1) % 2 == 0
    even_z = lax.broadcasted_iota(jnp.int32, (kz_len, wide), 0) % 2 == 0

    def slope_x(value):
        return jnp.where(even_x, turn(value, -1), -turn(value, 1)) * wave_x

    def slope_z(value):
        return (
            jnp.where(
                even_z,
                pltpu.roll(value, kz_len - 1, axis=0),
                -pltpu.roll(value, 1, axis=0),
            )
            * wave_z
        )

    s = [
        [spec[(y * 3 + c) * kz_len : (y * 3 + c + 1) * kz_len] for c in range(3)] for y in range(2)
    ]
    square = wave_x * wave_x + wave_z * wave_z + wave_y * wave_y
    positive = square > 0
    safe = jnp.where(positive, square, 1.0)
    potential = []
    for y in range(2):
        along_y = s[1 - y][1] * (wave_y if y == 0 else -wave_y)
        divergence = slope_x(s[y][0]) + along_y + slope_z(s[y][2])
        potential.append(jnp.where(positive, divergence / safe, 0.0))
    for y in range(2):
        along_y = potential[1 - y] * (wave_y if y == 0 else -wave_y)
        found = [
            s[y][0] + slope_x(potential[y]),
            s[y][1] + along_y,
            s[y][2] + slope_z(potential[y]),
        ]
        for comp in range(3):
            out_ref[comp, y] = (found[comp] * scale)[:, :modes]


def last(sums, wave_y, wave_x, wave_z, ky_len, kz_len, scale):
    modes, lanes = sums[0].shape
    return pl.pallas_call(
        functools.partial(last_kernel, (kz_len, modes, scale)),
        grid=(ky_len // 2,),
        in_specs=[SMEM, *[whole(a) for a in (wave_x, wave_z, *sums)]],
        out_specs=pl.BlockSpec((3, 2, kz_len, modes), lambda i: (0, i, 0, 0)),
        out_shape=jax.ShapeDtypeStruct((3, ky_len, kz_len, modes), F32),
        scratch_shapes=[pltpu.VMEM((lanes, wave_x.shape[1]), F32)],
        compiler_params=params(),
        cost_estimate=SHORT,
        name="last_projection",
    )(wave_y, wave_x, wave_z, *sums)


def after(value, *earlier_values):
    return lax.optimization_barrier((value, earlier_values))[0]


def shards(new_velocity, stored_velocity, stored_vorticity):
    rows = lax.axis_size("row")
    cols = lax.axis_size("col")
    _, ky_len, kz_own, modes = new_velocity.shape
    orders, _, x_len, y_len, grid_len = stored_velocity.shape
    kz_len = round_up(kz_own, 8)
    kmax = modes // 2 - 1
    sizes = chunk_sizes(x_len)
    chunks = len(sizes)
    begins = [sum(sizes[:k]) for k in range(chunks)]
    pack = LANES // y_len
    wide = round_up(modes, LANES)
    group = 5 * kz_len
    lanes = round_up(ky_len * group, 256)

    basis = synth_np(grid_len, modes)
    slope = slope_np(basis, kmax)
    y_order = (np.arange(rows)[None, :] * ky_len + np.arange(ky_len)[:, None]).reshape(-1)

    groups = rows // 2
    row, col = lax.axis_index("row"), lax.axis_index("col")
    place = jnp.stack([row // 2, row % 2, col]).astype(jnp.int32)

    def own_table(tables, axis):
        return lax.dynamic_index_in_dim(jnp.asarray(np.stack(tables)), lax.axis_index(axis), 0, False)

    def x_points(row):
        owner = np.array([row ^ (2 * k) for k in range(groups)])
        return np.concatenate(
            [
                (owner[:, None] * x_len + begin + np.arange(xc)[None, :]).reshape(-1)
                for begin, xc in zip(begins, sizes)
            ]
        )

    def halves_of(plain, sloped):
        return np.stack([part for table in (plain, sloped) for part in halves(table)])

    def y_table(col):
        points = np.concatenate([(col ^ k) * y_len + np.arange(y_len) for k in range(cols)])
        return halves_of(basis[points].T[y_order], slope[points].T[y_order])

    def z_table(col):
        def spread(table):
            parts = table.T.reshape(cols, kz_own, grid_len)[[col ^ k for k in range(cols)]]
            parts = np.pad(parts, ((0, 0), (0, kz_len - kz_own), (0, 0)))
            return parts.reshape(cols * kz_len, grid_len)

        return halves_of(spread(basis), spread(slope))

    table_x = own_table(
        [halves_of(basis[x_points(row)].T, slope[x_points(row)].T) for row in range(rows)], "row"
    )
    table_y = own_table([y_table(col) for col in range(cols)], "col")
    table_z = own_table([z_table(col) for col in range(cols)], "col")

    def wave_of(index):
        return (index // 2).astype(F32) / kmax

    mode = jnp.arange(wide, dtype=jnp.int32)
    wave_x = jnp.broadcast_to(jnp.where(mode < modes, wave_of(mode), 0.0)[None, :], (8, wide))
    ky_first = lax.axis_index("row") * ky_len + 2 * jnp.arange(ky_len // 2, dtype=jnp.int32)
    wave_y = wave_of(ky_first)
    kz = lax.axis_index("col") * kz_own + jnp.arange(kz_len, dtype=jnp.int32)
    wave_z = jnp.broadcast_to(wave_of(kz)[:, None], (kz_len, wide))

    coeffs = new_velocity
    if kz_len > kz_own:
        coeffs = jnp.pad(coeffs, ((0, 0), (0, 0), (0, kz_len - kz_own), (0, 0)))

    def exchange(values, axis, shift, size):
        return [
            lax.ppermute(value, axis, [(src, src ^ (k << shift)) for src in range(size)]) if k else value
            for k, value in enumerate(values)
        ]

    def core_swap(value):
        return lax.ppermute(value, "row", [(src, src ^ 1) for src in range(rows)])

    dims = [(rows, xc, ky_len, kz_len, cols, y_len, pack) for xc in sizes]
    shape = (tuple(sizes), groups)
    other = core_swap(coeffs)
    small = (place, table_x, table_y, table_z, wave_x, wave_y, wave_z)
    place, table_x, table_y, table_z, wave_x, wave_y, wave_z = lax.optimization_barrier(small)

    def run_first(chosen, gate):
        own = coeffs if gate is None else after(coeffs, gate)
        found = first_synth(place, own, table_x, shape, chosen, lanes, ())
        found = first_synth(place, other, table_x, shape, chosen, lanes, found)
        return {chunk: list(found[k * groups : (k + 1) * groups]) for k, chunk in enumerate(chosen)}

    sent = run_first((0,), None)
    if chunks > 1:
        sent.update(run_first(tuple(range(1, chunks)), sent[0][0]))
    latest = sent[chunks - 1][0]

    def ordered(kernel, operands, *others):
        nonlocal latest
        operands = after(operands, latest)
        found = kernel(operands, *others)
        latest = found[0] if isinstance(found, (list, tuple)) else found
        return found

    stored = (stored_velocity, stored_vorticity)

    def run_earlier(chunk):
        return ordered(lambda values: earlier(*values, begins[chunk], sizes[chunk], pack), stored)

    def z_exchange(values, *gates, waves=True):
        found = [values[0]]
        for k in range(1, groups):
            value = values[k]
            if gates:
                value = after(value, found[1]) if waves and 2 * k > groups else after(value, *gates)
            found.append(lax.ppermute(value, "row", [(src, src ^ (2 * k)) for src in range(rows)]))
        return found

    first, second, middle, back, base = {}, {}, {}, {}, {}
    for step in range(min(2, chunks)):
        first[step] = z_exchange(sent[step], *([first[step - 1]] if step else []))

    def run_second(at):
        found = ordered(lambda values: second_synth(place, values, table_y, dims[at]), first[at])
        if at:
            found = [found[0]] + [after(value, second[at - 1]) for value in found[1:]]
        second[at] = exchange(found, "col", 0, cols)

    def run_third(at):
        found = ordered(
            lambda values: third(
                place, values, *stored, base[at], table_z, begins[at], dims[at][3:]
            ),
            second[at],
        )
        middle[at] = exchange(found, "col", 0, cols)

    def run_back(at):
        found = ordered(lambda values: second_back(place, values, table_y, dims[at]), middle[at])
        back[at] = z_exchange(found, back[at - 1] if at else first[min(1, chunks - 1)], waves=at == 0)
        if at == 0 and chunks > 2:
            first[2] = z_exchange(sent[2], back[0])

    def run_base(at):
        base[at] = run_earlier(at)

    plan = [(run_base, 0), (run_second, 0), (run_base, 1), (run_third, 0), (run_base, 2), (run_back, 0)]
    plan += [(run_second, 1), (run_second, 2), (run_third, 1), (run_third, 2), (run_back, 1), (run_back, 2)]
    for action, at in plan:
        if at < chunks:
            action(at)
    parts = [value for step in range(chunks) for value in back[step]]
    away = first_back(place, parts, table_x, sizes, False)
    home = first_back(place, parts, after(table_x, away), sizes, True)
    sums = [home, core_swap(away)]
    result = last(sums, wave_y, wave_x, wave_z, ky_len, kz_len, 1.0 / (orders + 1))
    return result[:, :, :kz_own] if kz_len > kz_own else result


def solution(mesh):
    return jax.shard_map(
        shards,
        mesh=mesh,
        in_specs=(
            P(None, "row", "col", None),
            P(None, None, "row", "col", None),
            P(None, None, "row", "col", None),
        ),
        out_specs=P(None, "row", "col", None),
        check_vma=False,
    )
```

```python
import functools
import math

import jax
import jax.numpy as jnp
import ml_dtypes
import numpy as np
from jax import lax
from jax.experimental import pallas as pl
from jax.experimental.pallas import tpu as pltpu
from jax.sharding import PartitionSpec as P

LANES = 128


def chunk_sizes(x_len):
    ends = 8
    return [ends, x_len - 2 * ends, ends] if x_len > 3 * ends else [ends] * (x_len // ends)

BF16 = jnp.bfloat16
F32 = jnp.float32
NN = (((1,), (0,)), ((), ()))
NT = (((1,), (1,)), ((), ()))


def round_up(value, step):
    return -(-value // step) * step


def synth_np(grid_len, mode_count):
    points = np.arange(grid_len)[:, None]
    mode_index = np.arange(mode_count)[None, :]
    wave_index = np.where(mode_index == 1, grid_len // 2, mode_index // 2)
    angles = (points * wave_index % grid_len) * (2.0 * math.pi / grid_len)
    trig = np.where((mode_index % 2 == 0) | (mode_index == 1), np.cos(angles), np.sin(angles))
    weight = np.where(mode_index < 2, 1.0, 2.0) / grid_len
    return np.where(mode_index == 1, 0.0, trig * np.sqrt(weight))


def slope_np(table, kmax):
    paired = table.reshape(table.shape[0], -1, 2)
    wavenum = np.arange(paired.shape[1]) / kmax
    return np.stack([-wavenum * paired[:, :, 1], wavenum * paired[:, :, 0]], -1).reshape(table.shape)


def halves(table):
    high = table.astype(ml_dtypes.bfloat16)
    low = (table - high.astype(np.float64)).astype(ml_dtypes.bfloat16)
    return high, low


def pieces_of(values):
    high = values.astype(BF16)
    return high, (values - high.astype(F32)).astype(BF16)


def dot(left, right, dims):
    return lax.dot_general(left, right, dims, preferred_element_type=F32)


def dot_data_left(values, high, low, dims=NN):
    top, rest = pieces_of(values)
    return dot(top, high, dims) + (dot(top, low, dims) + dot(rest, high, dims))


def dot_data_right(high, low, values, dims=NT):
    top, rest = pieces_of(values)
    return dot(high, top, dims) + (dot(low, top, dims) + dot(high, rest, dims))


def turn(values, shift):
    shift = shift % values.shape[-1]
    return values if shift == 0 else pltpu.roll(values, shift, axis=values.ndim - 1)


def lane_pack(parts, width, source_lane=0):
    tiles = []
    lane = lax.broadcasted_iota(jnp.int32, parts[0].shape, 1)
    for tile in range(-(-len(parts) * width // LANES)):
        start = tile * LANES
        acc = None
        for idx in range(start // width, min(len(parts) - 1, (start + LANES - 1) // width) + 1):
            moved = turn(parts[idx], idx * width - source_lane)
            acc = moved if acc is None else jnp.where(lane >= idx * width - start, moved, acc)
        tiles.append(acc)
    return tiles


VMEM_LIMIT = 32 * 1024 * 1024
VMEM_MOST = 60 * 1024 * 1024
SHORT = pl.CostEstimate(flops=1024, bytes_accessed=1024, transcendentals=0)
ANY = pl.BlockSpec(memory_space=pl.ANY)
HBM = pl.BlockSpec(memory_space=pltpu.HBM)
SMEM = pl.BlockSpec(memory_space=pltpu.SMEM)
VMEM = pl.BlockSpec(memory_space=pltpu.VMEM)


def params():
    return pltpu.CompilerParams(dimension_semantics=("arbitrary",), vmem_limit_bytes=VMEM_LIMIT)


def still(limit=VMEM_LIMIT):
    return pltpu.CompilerParams(vmem_limit_bytes=limit)


def both_passes(values, high_low, high):
    top, rest = pieces_of(values)
    wide = dot(top, high_low, NN)
    half = high.shape[1]
    return wide[:, :half] + (wide[:, half:] + dot(rest, high, NN))


def whole(array):
    rank = len(array.shape)
    return pl.BlockSpec(array.shape, lambda *_: (0,) * rank)


def first_synth_kernel(dims, place_ref, data, table_ref, *rest):
    sizes, chosen, dests, own = dims
    outs, rows = rest[-len(chosen) * dests - 1 : -1], rest[-1]
    _, ky_len, kz_len, _ = data.shape
    group = 5 * kz_len
    if ky_len * group < rows.shape[0]:
        rows[ky_len * group :, :] = jnp.zeros((rows.shape[0] - ky_len * group, LANES), F32)
    plain = jnp.concatenate([table_ref[0], table_ref[1]], axis=1)
    slope = jnp.concatenate([table_ref[2], table_ref[3]], axis=1)
    step = 4 if ky_len % 4 == 0 else 2

    def body(idx, carry):
        first = idx * step
        lines = [[data[comp, first + k] for comp in range(3)] for k in range(step)]
        found = both_passes(
            jnp.concatenate([v for line in lines for v in line], axis=0), plain, table_ref[0]
        )
        sloped = both_passes(
            jnp.concatenate([v for line in lines for v in line[1:]], axis=0), slope, table_ref[2]
        )
        for k in range(step):
            base = (first + k) * group
            rows[pl.ds(pl.multiple_of(base, 8), 3 * kz_len), :] = found[
                3 * k * kz_len : 3 * (k + 1) * kz_len
            ]
            rows[pl.ds(pl.multiple_of(base + 3 * kz_len, 8), 2 * kz_len), :] = sloped[
                2 * k * kz_len : 2 * (k + 1) * kz_len
            ]
        return carry

    lax.fori_loop(0, ky_len // step, body, 0)

    core = place_ref[1] if own else 1 - place_ref[1]

    def flip(tile, carry):
        found = rows[pl.ds(pl.multiple_of(tile * LANES, LANES), LANES), :].T
        for idx, out in enumerate(outs):
            chunk, k = chosen[idx // dests], idx % dests
            xc = sizes[chunk]
            at = sum(sizes[:chunk]) * dests + k * xc
            spot = core * (out.shape[0] // 2) + tile * xc
            out[pl.ds(pl.multiple_of(spot, 8), xc), :] = found[at : at + xc]
        return carry

    lax.fori_loop(0, rows.shape[0] // LANES, flip, 0, unroll=2)


def first_synth(place, coeffs, table, dims, chosen, lanes, half):
    sizes, dests = dims
    heights = [2 * (lanes // LANES) * sizes[chunk] for chunk in chosen for _ in range(dests)]
    return pl.pallas_call(
        functools.partial(first_synth_kernel, (sizes, chosen, dests, not half)),
        in_specs=[SMEM, VMEM, VMEM] + [ANY] * len(half),
        out_specs=[VMEM] * len(heights),
        out_shape=[jax.ShapeDtypeStruct((h, LANES), F32) for h in heights],
        input_output_aliases={3 + k: k for k in range(len(half))},
        scratch_shapes=[pltpu.VMEM((lanes, LANES), F32)],
        compiler_params=still(),
        cost_estimate=SHORT,
        name="first_synth",
    )(place, coeffs, table, *half)


def second_synth_kernel(dims, place_ref, *refs):
    rows, xc, ky_len, kz_len, cols, y_len, pack = dims
    groups = rows // 2
    parts, table_ref, out_refs = refs[:groups], refs[groups], refs[groups + 1 : -1]
    a_ref = refs[-1]
    size = parts[0].shape[0] // 2
    stride = a_ref.shape[0] // rows
    for k, part in enumerate(parts):
        for core in range(2):
            spot = pl.multiple_of(((place_ref[0] ^ k) * 2 + core) * stride, 8)
            a_ref[pl.ds(spot, size), :] = part[core * size : (core + 1) * size, :]
    group = 5 * kz_len
    wide = round_up(group, LANES)
    tiles = size // xc

    def body(at, carry):
        turned = []
        for part in range(pack):
            line = [
                a_ref[pl.ds(tile * xc + at * pack + part, rows, stride=stride), :]
                for tile in range(tiles)
            ]
            found = []
            for ky in range(ky_len):
                start = ky * group
                low, off = divmod(start, LANES)
                window = line[low : low + (wide // LANES) + (1 if off else 0)]
                found.append(turn(jnp.concatenate(window, axis=1), -off)[:, :wide])
            turned.append(jnp.concatenate(found, axis=0).T[:group])
        plain = dot_data_left(jnp.concatenate(turned, axis=0), table_ref[0], table_ref[1])
        slope_in = [t[c * kz_len : (c + 1) * kz_len] for t in turned for c in (0, 2)]
        slope = dot_data_left(jnp.concatenate(slope_in, axis=0), table_ref[2], table_ref[3])
        fields = []
        for part in range(pack):
            own = plain[part * group : (part + 1) * group]
            sl = slope[part * 2 * kz_len : (part + 1) * 2 * kz_len]
            fields.append(
                jnp.concatenate(
                    [
                        own[: 3 * kz_len],
                        own[3 * kz_len : 4 * kz_len] - sl[:kz_len],
                        sl[kz_len:],
                        -own[4 * kz_len :],
                    ],
                    axis=0,
                )
            )
        for dest in range(cols):
            tile, off = divmod(dest * y_len, LANES)
            out_refs[dest][at] = lane_pack(
                [f[:, tile * LANES : (tile + 1) * LANES] for f in fields], y_len, off
            )[0]
        return carry

    lax.fori_loop(0, xc // pack, body, 0)


def second_synth(place, arrived, table, dims):
    rows, xc, ky_len, kz_len, cols, y_len, pack = dims
    packs = xc // pack
    return pl.pallas_call(
        functools.partial(second_synth_kernel, dims),
        in_specs=[SMEM] + [VMEM] * (len(arrived) + 1),
        out_specs=[VMEM] * cols,
        out_shape=[jax.ShapeDtypeStruct((packs, 6 * kz_len, LANES), F32)] * cols,
        scratch_shapes=[
            pltpu.VMEM((rows * (arrived[0].shape[0] // 2 + 8), LANES), F32),
        ],
        compiler_params=still(),
        cost_estimate=SHORT,
        name="second_synth",
    )(place, *arrived, table)


def cross(left, right):
    return [
        left[1] * right[2] - left[2] * right[1],
        left[2] * right[0] - left[0] * right[2],
        left[0] * right[1] - left[1] * right[0],
    ]


def earlier_kernel(count, *refs):
    vels, vorts, out_ref = refs[:count], refs[count : 2 * count], refs[2 * count]
    pack, y_len = out_ref.shape[1:3]
    for part in range(pack):
        def body(step, carry):
            at = pl.ds(pl.multiple_of(step * 8, 8), 8)
            total = None
            for vel, vort in zip(vels, vorts):
                term = cross(
                    [vel[0, c, part, at, :] for c in range(3)],
                    [vort[0, c, part, at, :] for c in range(3)],
                )
                total = term if total is None else [a + b for a, b in zip(total, term)]
            for comp in range(3):
                out_ref[comp, part, at, :] = total[comp]
            return carry

        lax.fori_loop(0, y_len // 8, body, 0, unroll=2)


def earlier(velocity, vorticity, start, xc, pack):
    orders, _, _, y_len, grid_len = velocity.shape
    packs = xc // pack
    block = (1, 3, pack, y_len, grid_len)

    def at(order):
        return pl.BlockSpec(block, lambda i: (order, 0, start // pack + i, 0, 0))

    specs = [at(k) for k in range(1, orders)] + [at(orders - k) for k in range(1, orders)]
    size = xc * y_len * grid_len
    return pl.pallas_call(
        functools.partial(earlier_kernel, orders - 1),
        grid=(packs,),
        in_specs=specs,
        out_specs=pl.BlockSpec((3, pack, y_len, grid_len), lambda i: (0, i, 0, 0)),
        out_shape=jax.ShapeDtypeStruct((3, xc, y_len, grid_len), F32),
        compiler_params=params(),
        cost_estimate=SHORT,
        name="earlier_orders",
    )(*[velocity] * (orders - 1), *[vorticity] * (orders - 1))


def third_kernel(dims, place_ref, *refs):
    begin, kz_len, cols, y_len, pack = dims
    b_refs, stored_refs, table_ref = refs[:cols], refs[cols : cols + 3], refs[cols + 3]
    data, sem = refs[-2:]
    out_refs = refs[-2 - cols : -2]
    grid_len = table_ref.shape[2]
    xc = data.shape[2]
    packs = xc // pack

    def copies(at):
        spot = pl.ds(at * pack, pack)
        far = pl.ds(begin + at * pack, pack)
        sources = [ref.at[0, :, far] for ref in stored_refs[:2]] + [stored_refs[2].at[:, spot]]
        return [
            pltpu.make_async_copy(source, data.at[idx, :, spot], sem.at[idx, at])
            for idx, source in enumerate(sources)
        ]

    for at in range(packs):
        for copy in copies(at):
            copy.start()

    def body(at, carry):
        def stack(field):
            return jnp.concatenate(
                [b_refs[k][at, field * kz_len : (field + 1) * kz_len, :] for k in range(cols)], axis=0
            ).T

        lines = jnp.concatenate([stack(field) for field in range(6)], axis=0)
        plain = dot_data_left(lines, table_ref[0], table_ref[1])
        slope = dot_data_left(lines[: 2 * LANES], table_ref[2], table_ref[3])
        new = [plain[f * LANES : (f + 1) * LANES] for f in range(6)]
        vel_new = new[:3]
        vort_new = [new[4] - slope[LANES:], slope[:LANES] + new[5], new[3]]
        for copy in copies(at):
            copy.wait()
        spot = pl.ds(at * pack, pack)
        flat = (pack * y_len, grid_len)
        vel, vort, base = [[data[idx, c, spot].reshape(flat) for c in range(3)] for idx in range(3)]
        one, two = cross(vel_new, vort), cross(vel, vort_new)
        total = [one[c] + two[c] + base[c] for c in range(3)]
        result = dot_data_right(table_ref[0], table_ref[1], jnp.concatenate(total, axis=0))
        for k in range(cols):
            for comp in range(3):
                out_refs[k][at, comp * kz_len : (comp + 1) * kz_len, :] = result[
                    k * kz_len : (k + 1) * kz_len, comp * LANES : (comp + 1) * LANES
                ]
        return carry

    lax.fori_loop(0, packs, body, 0)


def third(place, arrived, velocity, vorticity, base, table, begin, dims):
    kz_len, cols, y_len, pack = dims
    packs = arrived[0].shape[0]
    grid_len = velocity.shape[-1]
    return pl.pallas_call(
        functools.partial(third_kernel, (begin, *dims)),
        in_specs=[SMEM] + [VMEM] * cols + [ANY] * 3 + [VMEM],
        out_specs=[VMEM] * cols,
        out_shape=[jax.ShapeDtypeStruct((packs, 3 * kz_len, LANES), F32)] * cols,
        scratch_shapes=[
            pltpu.VMEM((3, 3, packs * pack, y_len, grid_len), F32),
            pltpu.SemaphoreType.DMA((3, packs)),
        ],
        compiler_params=still(),
        cost_estimate=SHORT,
        name="third_dimension",
    )(place, *arrived, velocity, vorticity, base, table)


def second_back_kernel(dims, place_ref, *refs):
    rows, xc, ky_len, kz_len, cols, y_len, pack = dims
    c_refs, table_ref, outs, all_ref = refs[:cols], refs[cols], refs[cols + 1 : -1], refs[-1]
    width = 3 * kz_len
    high_pad = round_up(width, LANES)

    def body(at, carry):
        lines = []
        for part in range(pack):
            tiles = lane_pack(
                [c_ref[at] for c_ref in c_refs], y_len, part * y_len
            )
            lines.append(jnp.concatenate(tiles, axis=1))
            if high_pad > width:
                lines.append(jnp.zeros((high_pad - width, cols * y_len), F32))
        result = dot_data_right(table_ref[0], table_ref[1], jnp.concatenate(lines, axis=0))
        for part in range(pack):
            own = result[:, part * high_pad : (part + 1) * high_pad]
            tiles = lane_pack([own[ky * rows : (ky + 1) * rows] for ky in range(ky_len)], width)
            for idx, tile in enumerate(tiles):
                spot = idx * xc + at * pack + part
                all_ref[pl.ds(spot, rows, stride=len(tiles) * xc), :] = tile
        return carry

    lax.fori_loop(0, xc // pack, body, 0)
    size = all_ref.shape[0] // len(outs)
    for k, out in enumerate(outs):
        out[...] = all_ref[pl.ds(pl.multiple_of((place_ref[0] ^ k) * size, 8), size), :]


def second_back(place, arrived, table, dims):
    rows, xc, ky_len, kz_len, cols, y_len, pack = dims
    size = round_up(ky_len * 3 * kz_len, LANES) // LANES * xc
    groups = rows // 2
    return pl.pallas_call(
        functools.partial(second_back_kernel, dims),
        in_specs=[SMEM] + [VMEM] * (cols + 1),
        out_specs=[VMEM] * groups,
        out_shape=[jax.ShapeDtypeStruct((2 * size, LANES), F32)] * groups,
        scratch_shapes=[pltpu.VMEM((rows * size, LANES), F32)],
        compiler_params=still(),
        cost_estimate=SHORT,
        name="second_back",
    )(place, *arrived, table)


def first_back_kernel(dims, place_ref, *refs):
    count, sizes, own = dims
    parts, table_ref, out_ref = refs[:count], refs[count], refs[count + 1]
    groups = count // len(sizes)
    core = place_ref[1] if own else 1 - place_ref[1]
    for tile in range(out_ref.shape[1] // LANES):
        found = []
        for idx, part in enumerate(parts):
            xc = sizes[idx // groups]
            spot = pl.multiple_of(core * (part.shape[0] // 2) + tile * xc, 8)
            found.append(part[pl.ds(spot, xc), :])
        out_ref[:, tile * LANES : (tile + 1) * LANES] = dot_data_right(
            table_ref[0], table_ref[1], jnp.concatenate(found, axis=0), NN
        )


def first_back(place, parts, table, sizes, own):
    count = len(parts)
    tiles = parts[0].shape[0] // 2 // sizes[0]
    return pl.pallas_call(
        functools.partial(first_back_kernel, (count, tuple(sizes), own)),
        in_specs=[SMEM] + [VMEM] * (count + 1),
        out_specs=VMEM,
        out_shape=jax.ShapeDtypeStruct((table.shape[1], tiles * LANES), F32),
        compiler_params=still(),
        cost_estimate=SHORT,
        name="first_back",
    )(place, *parts, table)


def last_kernel(dims, *refs):
    kz_len, modes, scale = dims
    wave_y_ref, wave_x_ref, wave_z_ref, *sums, out_ref, rows, held, sem = refs
    pair = 2 * 3 * kz_len
    for tile in range(rows.shape[0] // LANES):
        lanes = slice(tile * LANES, (tile + 1) * LANES)
        rows[lanes, 0:modes] = functools.reduce(jnp.add, [part[:, lanes] for part in sums]).T

    def copy(at):
        spot = pl.ds(2 * at, 2)
        return pltpu.make_async_copy(held.at[:, spot], out_ref.at[:, spot], sem.at[at])

    def body(at, carry):
        project(at)
        copy(at).start()
        return carry

    def finish(at, carry):
        copy(at).wait()
        return carry

    def project(at):
        spec = rows[pl.ds(pl.multiple_of(at * pair, 8), pair), :]
        wide = spec.shape[1]
        wave_x = jnp.broadcast_to(wave_x_ref[0:1, :], (kz_len, wide))
        wave_z = wave_z_ref[...]
        wave_y = wave_y_ref[at]
        even_x = lax.broadcasted_iota(jnp.int32, (kz_len, wide), 1) % 2 == 0
        even_z = lax.broadcasted_iota(jnp.int32, (kz_len, wide), 0) % 2 == 0

        def slope_x(value):
            return jnp.where(even_x, turn(value, -1), -turn(value, 1)) * wave_x

        def slope_z(value):
            return (
                jnp.where(
                    even_z,
                    pltpu.roll(value, kz_len - 1, axis=0),
                    -pltpu.roll(value, 1, axis=0),
                )
                * wave_z
            )

        s = [
            [spec[(y * 3 + c) * kz_len : (y * 3 + c + 1) * kz_len] for c in range(3)] for y in range(2)
        ]
        square = wave_x * wave_x + wave_z * wave_z + wave_y * wave_y
        positive = square > 0
        safe = jnp.where(positive, square, 1.0)
        potential = []
        for y in range(2):
            along_y = s[1 - y][1] * (wave_y if y == 0 else -wave_y)
            divergence = slope_x(s[y][0]) + along_y + slope_z(s[y][2])
            potential.append(jnp.where(positive, divergence / safe, 0.0))
        for y in range(2):
            along_y = potential[1 - y] * (wave_y if y == 0 else -wave_y)
            found = [
                s[y][0] + slope_x(potential[y]),
                s[y][1] + along_y,
                s[y][2] + slope_z(potential[y]),
            ]
            for comp in range(3):
                held[comp, 2 * at + y] = (found[comp] * scale)[:, :modes]

    steps = held.shape[1] // 2
    lax.fori_loop(0, steps, body, 0)
    lax.fori_loop(0, steps, finish, 0)


def last(sums, wave_y, wave_x, wave_z, ky_len, kz_len, scale):
    modes, lanes = sums[0].shape
    return pl.pallas_call(
        functools.partial(last_kernel, (kz_len, modes, scale)),
        in_specs=[SMEM] + [VMEM] * (2 + len(sums)),
        out_specs=ANY,
        out_shape=jax.ShapeDtypeStruct((3, ky_len, kz_len, modes), F32),
        scratch_shapes=[
            pltpu.VMEM((lanes, wave_x.shape[1]), F32),
            pltpu.VMEM((3, ky_len, kz_len, modes), F32),
            pltpu.SemaphoreType.DMA((ky_len // 2,)),
        ],
        compiler_params=still(),
        cost_estimate=SHORT,
        name="last_projection",
    )(wave_y, wave_x, wave_z, *sums)


def after(value, *earlier_values):
    return lax.optimization_barrier((value, earlier_values))[0]


def shards(new_velocity, stored_velocity, stored_vorticity):
    rows = lax.axis_size("row")
    cols = lax.axis_size("col")
    _, ky_len, kz_own, modes = new_velocity.shape
    orders, _, x_len, y_len, grid_len = stored_velocity.shape
    kz_len = round_up(kz_own, 8)
    kmax = modes // 2 - 1
    sizes = chunk_sizes(x_len)
    chunks = len(sizes)
    begins = [sum(sizes[:k]) for k in range(chunks)]
    pack = LANES // y_len
    wide = round_up(modes, LANES)
    group = 5 * kz_len
    lanes = round_up(ky_len * group, 256)

    basis = synth_np(grid_len, modes)
    slope = slope_np(basis, kmax)
    y_order = (np.arange(rows)[None, :] * ky_len + np.arange(ky_len)[:, None]).reshape(-1)

    groups = rows // 2
    row, col = lax.axis_index("row"), lax.axis_index("col")
    place = jnp.stack([row // 2, row % 2, col]).astype(jnp.int32)

    def own_table(tables, axis):
        return lax.dynamic_index_in_dim(jnp.asarray(np.stack(tables)), lax.axis_index(axis), 0, False)

    def x_points(row):
        owner = np.array([row ^ (2 * k) for k in range(groups)])
        return np.concatenate(
            [
                (owner[:, None] * x_len + begin + np.arange(xc)[None, :]).reshape(-1)
                for begin, xc in zip(begins, sizes)
            ]
        )

    def halves_of(plain, sloped):
        return np.stack([part for table in (plain, sloped) for part in halves(table)])

    def y_table(col):
        points = np.concatenate([(col ^ k) * y_len + np.arange(y_len) for k in range(cols)])
        return halves_of(basis[points].T[y_order], slope[points].T[y_order])

    def z_table(col):
        def spread(table):
            parts = table.T.reshape(cols, kz_own, grid_len)[[col ^ k for k in range(cols)]]
            parts = np.pad(parts, ((0, 0), (0, kz_len - kz_own), (0, 0)))
            return parts.reshape(cols * kz_len, grid_len)

        return halves_of(spread(basis), spread(slope))

    table_x = own_table(
        [halves_of(basis[x_points(row)].T, slope[x_points(row)].T) for row in range(rows)], "row"
    )
    table_y = own_table([y_table(col) for col in range(cols)], "col")
    table_z = own_table([z_table(col) for col in range(cols)], "col")

    def wave_of(index):
        return (index // 2).astype(F32) / kmax

    mode = jnp.arange(wide, dtype=jnp.int32)
    wave_x = jnp.broadcast_to(jnp.where(mode < modes, wave_of(mode), 0.0)[None, :], (8, wide))
    ky_first = lax.axis_index("row") * ky_len + 2 * jnp.arange(ky_len // 2, dtype=jnp.int32)
    wave_y = wave_of(ky_first)
    kz = lax.axis_index("col") * kz_own + jnp.arange(kz_len, dtype=jnp.int32)
    wave_z = jnp.broadcast_to(wave_of(kz)[:, None], (kz_len, wide))

    coeffs = new_velocity
    if kz_len > kz_own:
        coeffs = jnp.pad(coeffs, ((0, 0), (0, 0), (0, kz_len - kz_own), (0, 0)))

    def exchange(values, axis, shift, size):
        return [
            lax.ppermute(value, axis, [(src, src ^ (k << shift)) for src in range(size)]) if k else value
            for k, value in enumerate(values)
        ]

    def core_swap(value):
        return lax.ppermute(value, "row", [(src, src ^ 1) for src in range(rows)])

    dims = [(rows, xc, ky_len, kz_len, cols, y_len, pack) for xc in sizes]
    shape = (tuple(sizes), groups)
    other = core_swap(coeffs)
    small = (place, table_x, table_y, table_z, wave_x, wave_y, wave_z)
    place, table_x, table_y, table_z, wave_x, wave_y, wave_z = lax.optimization_barrier(small)

    def run_first(chosen, gate):
        own = coeffs if gate is None else after(coeffs, gate)
        found = first_synth(place, own, table_x, shape, chosen, lanes, ())
        found = first_synth(place, other, table_x, shape, chosen, lanes, found)
        return {chunk: list(found[k * groups : (k + 1) * groups]) for k, chunk in enumerate(chosen)}

    sent = run_first((0,), None)
    if chunks > 1:
        sent.update(run_first(tuple(range(1, chunks)), sent[0][0]))
    latest = sent[chunks - 1][0]

    def ordered(kernel, operands, *others):
        nonlocal latest
        operands = after(operands, latest)
        found = kernel(operands, *others)
        latest = found[0] if isinstance(found, (list, tuple)) else found
        return found

    stored = (stored_velocity, stored_vorticity)

    def run_earlier(chunk):
        return ordered(lambda values: earlier(*values, begins[chunk], sizes[chunk], pack), stored)

    def z_exchange(values, *gates, waves=True):
        found = [values[0]]
        for k in range(1, groups):
            value = values[k]
            if gates:
                value = after(value, found[1]) if waves and 2 * k > groups else after(value, *gates)
            found.append(lax.ppermute(value, "row", [(src, src ^ (2 * k)) for src in range(rows)]))
        return found

    first, second, middle, back, base = {}, {}, {}, {}, {}
    for step in range(min(2, chunks)):
        first[step] = z_exchange(sent[step], *([first[step - 1]] if step else []))

    def run_second(at):
        found = ordered(lambda values: second_synth(place, values, table_y, dims[at]), first[at])
        if at:
            found = [found[0]] + [after(value, second[at - 1]) for value in found[1:]]
        second[at] = exchange(found, "col", 0, cols)

    def run_third(at):
        found = ordered(
            lambda values: third(
                place, values, *stored, base[at], table_z, begins[at], dims[at][3:]
            ),
            second[at],
        )
        middle[at] = exchange(found, "col", 0, cols)

    def run_back(at):
        found = ordered(lambda values: second_back(place, values, table_y, dims[at]), middle[at])
        back[at] = z_exchange(found, back[at - 1] if at else first[min(1, chunks - 1)], waves=at == 0)
        if at == 0 and chunks > 2:
            first[2] = z_exchange(sent[2], back[0])

    def run_base(at):
        base[at] = run_earlier(at)

    plan = [(run_second, 0), (run_base, 0), (run_base, 1), (run_third, 0), (run_base, 2), (run_back, 0)]
    plan += [(run_second, 1), (run_second, 2), (run_third, 1), (run_third, 2), (run_back, 1), (run_back, 2)]
    for action, at in plan:
        if at < chunks:
            action(at)
    parts = [value for step in range(chunks) for value in back[step]]
    away = first_back(place, parts, table_x, sizes, False)
    home = first_back(place, parts, after(table_x, away), sizes, True)
    sums = [home, core_swap(away)]
    result = last(sums, wave_y, wave_x, wave_z, ky_len, kz_len, 1.0 / (orders + 1))
    return result[:, :, :kz_own] if kz_len > kz_own else result


def solution(mesh):
    return jax.shard_map(
        shards,
        mesh=mesh,
        in_specs=(
            P(None, "row", "col", None),
            P(None, None, "row", "col", None),
            P(None, None, "row", "col", None),
        ),
        out_specs=P(None, "row", "col", None),
        check_vma=False,
    )
```

```python
import functools
import math

import jax
import jax.numpy as jnp
import ml_dtypes
import numpy as np
from jax import lax
from jax.experimental import pallas as pl
from jax.experimental.pallas import tpu as pltpu
from jax.sharding import PartitionSpec as P

LANES = 128


def chunk_sizes(x_len):
    short = 8
    return [short, short, x_len - 2 * short] if x_len > 3 * short else [short] * (x_len // short)

BF16 = jnp.bfloat16
F32 = jnp.float32
NN = (((1,), (0,)), ((), ()))
NT = (((1,), (1,)), ((), ()))


def round_up(value, step):
    return -(-value // step) * step


def synth_np(grid_len, mode_count):
    points = np.arange(grid_len)[:, None]
    mode_index = np.arange(mode_count)[None, :]
    wave_index = np.where(mode_index == 1, grid_len // 2, mode_index // 2)
    angles = (points * wave_index % grid_len) * (2.0 * math.pi / grid_len)
    trig = np.where((mode_index % 2 == 0) | (mode_index == 1), np.cos(angles), np.sin(angles))
    weight = np.where(mode_index < 2, 1.0, 2.0) / grid_len
    return np.where(mode_index == 1, 0.0, trig * np.sqrt(weight))


def slope_np(table, kmax):
    paired = table.reshape(table.shape[0], -1, 2)
    wavenum = np.arange(paired.shape[1]) / kmax
    return np.stack([-wavenum * paired[:, :, 1], wavenum * paired[:, :, 0]], -1).reshape(table.shape)


def halves(table):
    high = table.astype(ml_dtypes.bfloat16)
    low = (table - high.astype(np.float64)).astype(ml_dtypes.bfloat16)
    return high, low


def pieces_of(values):
    high = values.astype(BF16)
    return high, (values - high.astype(F32)).astype(BF16)


def dot(left, right, dims):
    return lax.dot_general(left, right, dims, preferred_element_type=F32)


def dot_data_left(values, high, low, dims=NN):
    top, rest = pieces_of(values)
    return dot(top, high, dims) + (dot(top, low, dims) + dot(rest, high, dims))


def dot_data_right(high, low, values, dims=NT):
    top, rest = pieces_of(values)
    return dot(high, top, dims) + (dot(low, top, dims) + dot(high, rest, dims))


def turn(values, shift):
    shift = shift % values.shape[-1]
    return values if shift == 0 else pltpu.roll(values, shift, axis=values.ndim - 1)


def lane_pack(parts, width, source_lane=0):
    tiles = []
    lane = lax.broadcasted_iota(jnp.int32, parts[0].shape, 1)
    for tile in range(-(-len(parts) * width // LANES)):
        start = tile * LANES
        acc = None
        for idx in range(start // width, min(len(parts) - 1, (start + LANES - 1) // width) + 1):
            moved = turn(parts[idx], idx * width - source_lane)
            acc = moved if acc is None else jnp.where(lane >= idx * width - start, moved, acc)
        tiles.append(acc)
    return tiles


VMEM_LIMIT = 32 * 1024 * 1024
VMEM_MOST = 60 * 1024 * 1024
SHORT = pl.CostEstimate(flops=1024, bytes_accessed=1024, transcendentals=0)
ANY = pl.BlockSpec(memory_space=pl.ANY)
HBM = pl.BlockSpec(memory_space=pltpu.HBM)
SMEM = pl.BlockSpec(memory_space=pltpu.SMEM)
VMEM = pl.BlockSpec(memory_space=pltpu.VMEM)


def params():
    return pltpu.CompilerParams(dimension_semantics=("arbitrary",), vmem_limit_bytes=VMEM_LIMIT)


def still(limit=VMEM_LIMIT):
    return pltpu.CompilerParams(vmem_limit_bytes=limit)


def both_passes(values, high_low, high):
    top, rest = pieces_of(values)
    wide = dot(top, high_low, NN)
    half = high.shape[1]
    return wide[:, :half] + (wide[:, half:] + dot(rest, high, NN))


def whole(array):
    rank = len(array.shape)
    return pl.BlockSpec(array.shape, lambda *_: (0,) * rank)


def first_synth_kernel(dims, place_ref, data, table_ref, *rest):
    sizes, chosen, dests, own = dims
    outs, rows = rest[-len(chosen) * dests - 1 : -1], rest[-1]
    _, ky_len, kz_len, _ = data.shape
    group = 5 * kz_len
    if ky_len * group < rows.shape[0]:
        rows[ky_len * group :, :] = jnp.zeros((rows.shape[0] - ky_len * group, LANES), F32)
    plain = jnp.concatenate([table_ref[0], table_ref[1]], axis=1)
    slope = jnp.concatenate([table_ref[2], table_ref[3]], axis=1)
    step = 4 if ky_len % 4 == 0 else 2

    def body(idx, carry):
        first = idx * step
        lines = [[data[comp, first + k] for comp in range(3)] for k in range(step)]
        found = both_passes(
            jnp.concatenate([v for line in lines for v in line], axis=0), plain, table_ref[0]
        )
        sloped = both_passes(
            jnp.concatenate([v for line in lines for v in line[1:]], axis=0), slope, table_ref[2]
        )
        for k in range(step):
            base = (first + k) * group
            rows[pl.ds(pl.multiple_of(base, 8), 3 * kz_len), :] = found[
                3 * k * kz_len : 3 * (k + 1) * kz_len
            ]
            rows[pl.ds(pl.multiple_of(base + 3 * kz_len, 8), 2 * kz_len), :] = sloped[
                2 * k * kz_len : 2 * (k + 1) * kz_len
            ]
        return carry

    lax.fori_loop(0, ky_len // step, body, 0)

    core = place_ref[1] if own else 1 - place_ref[1]

    def flip(tile, carry):
        found = rows[pl.ds(pl.multiple_of(tile * LANES, LANES), LANES), :].T
        for idx, out in enumerate(outs):
            chunk, k = chosen[idx // dests], idx % dests
            xc = sizes[chunk]
            at = sum(sizes[:chunk]) * dests + k * xc
            spot = core * (out.shape[0] // 2) + tile * xc
            out[pl.ds(pl.multiple_of(spot, 8), xc), :] = found[at : at + xc]
        return carry

    lax.fori_loop(0, rows.shape[0] // LANES, flip, 0, unroll=2)


def first_synth(place, coeffs, table, dims, chosen, lanes, half):
    sizes, dests = dims
    heights = [2 * (lanes // LANES) * sizes[chunk] for chunk in chosen for _ in range(dests)]
    return pl.pallas_call(
        functools.partial(first_synth_kernel, (sizes, chosen, dests, not half)),
        in_specs=[SMEM, VMEM, VMEM] + [ANY] * len(half),
        out_specs=[VMEM] * len(heights),
        out_shape=[jax.ShapeDtypeStruct((h, LANES), F32) for h in heights],
        input_output_aliases={3 + k: k for k in range(len(half))},
        scratch_shapes=[pltpu.VMEM((lanes, LANES), F32)],
        compiler_params=still(),
        cost_estimate=SHORT,
        name="first_synth",
    )(place, coeffs, table, *half)


def second_synth_kernel(dims, place_ref, *refs):
    rows, xc, ky_len, kz_len, cols, y_len, pack = dims
    groups = rows // 2
    parts, table_ref, out_refs = refs[:groups], refs[groups], refs[groups + 1 : -1]
    a_ref = refs[-1]
    size = parts[0].shape[0] // 2
    stride = a_ref.shape[0] // rows
    for k, part in enumerate(parts):
        for core in range(2):
            spot = pl.multiple_of(((place_ref[0] ^ k) * 2 + core) * stride, 8)
            a_ref[pl.ds(spot, size), :] = part[core * size : (core + 1) * size, :]
    group = 5 * kz_len
    wide = round_up(group, LANES)
    tiles = size // xc

    def body(at, carry):
        turned = []
        for part in range(pack):
            line = [
                a_ref[pl.ds(tile * xc + at * pack + part, rows, stride=stride), :]
                for tile in range(tiles)
            ]
            found = []
            for ky in range(ky_len):
                start = ky * group
                low, off = divmod(start, LANES)
                window = line[low : low + (wide // LANES) + (1 if off else 0)]
                found.append(turn(jnp.concatenate(window, axis=1), -off)[:, :wide])
            turned.append(jnp.concatenate(found, axis=0).T[:group])
        plain = dot_data_left(jnp.concatenate(turned, axis=0), table_ref[0], table_ref[1])
        slope_in = [t[c * kz_len : (c + 1) * kz_len] for t in turned for c in (0, 2)]
        slope = dot_data_left(jnp.concatenate(slope_in, axis=0), table_ref[2], table_ref[3])
        fields = []
        for part in range(pack):
            own = plain[part * group : (part + 1) * group]
            sl = slope[part * 2 * kz_len : (part + 1) * 2 * kz_len]
            fields.append(
                jnp.concatenate(
                    [
                        own[: 3 * kz_len],
                        own[3 * kz_len : 4 * kz_len] - sl[:kz_len],
                        sl[kz_len:],
                        -own[4 * kz_len :],
                    ],
                    axis=0,
                )
            )
        for dest in range(cols):
            tile, off = divmod(dest * y_len, LANES)
            out_refs[dest][at] = lane_pack(
                [f[:, tile * LANES : (tile + 1) * LANES] for f in fields], y_len, off
            )[0]
        return carry

    lax.fori_loop(0, xc // pack, body, 0)


def second_synth(place, arrived, table, dims):
    rows, xc, ky_len, kz_len, cols, y_len, pack = dims
    packs = xc // pack
    return pl.pallas_call(
        functools.partial(second_synth_kernel, dims),
        in_specs=[SMEM] + [VMEM] * (len(arrived) + 1),
        out_specs=[VMEM] * cols,
        out_shape=[jax.ShapeDtypeStruct((packs, 6 * kz_len, LANES), F32)] * cols,
        scratch_shapes=[
            pltpu.VMEM((rows * (arrived[0].shape[0] // 2 + 8), LANES), F32),
        ],
        compiler_params=still(),
        cost_estimate=SHORT,
        name="second_synth",
    )(place, *arrived, table)


def cross(left, right):
    return [
        left[1] * right[2] - left[2] * right[1],
        left[2] * right[0] - left[0] * right[2],
        left[0] * right[1] - left[1] * right[0],
    ]


def earlier_kernel(count, *refs):
    vels, vorts, out_ref = refs[:count], refs[count : 2 * count], refs[2 * count]
    pack, y_len = out_ref.shape[1:3]
    for part in range(pack):
        def body(step, carry):
            at = pl.ds(pl.multiple_of(step * 8, 8), 8)
            total = None
            for vel, vort in zip(vels, vorts):
                term = cross(
                    [vel[0, c, part, at, :] for c in range(3)],
                    [vort[0, c, part, at, :] for c in range(3)],
                )
                total = term if total is None else [a + b for a, b in zip(total, term)]
            for comp in range(3):
                out_ref[comp, part, at, :] = total[comp]
            return carry

        lax.fori_loop(0, y_len // 8, body, 0, unroll=2)


def earlier(velocity, vorticity, start, xc, pack):
    orders, _, _, y_len, grid_len = velocity.shape
    packs = xc // pack
    block = (1, 3, pack, y_len, grid_len)

    def at(order):
        return pl.BlockSpec(block, lambda i: (order, 0, start // pack + i, 0, 0))

    specs = [at(k) for k in range(1, orders)] + [at(orders - k) for k in range(1, orders)]
    size = xc * y_len * grid_len
    return pl.pallas_call(
        functools.partial(earlier_kernel, orders - 1),
        grid=(packs,),
        in_specs=specs,
        out_specs=pl.BlockSpec((3, pack, y_len, grid_len), lambda i: (0, i, 0, 0)),
        out_shape=jax.ShapeDtypeStruct((3, xc, y_len, grid_len), F32),
        compiler_params=params(),
        cost_estimate=SHORT,
        name="earlier_orders",
    )(*[velocity] * (orders - 1), *[vorticity] * (orders - 1))


def third_kernel(dims, place_ref, *refs):
    begin, kz_len, cols, y_len, pack = dims
    b_refs, stored_refs, table_ref = refs[:cols], refs[cols : cols + 3], refs[cols + 3]
    data, sem = refs[-2:]
    out_refs = refs[-2 - cols : -2]
    grid_len = table_ref.shape[2]
    xc = data.shape[2]
    packs = xc // pack

    def copies(at):
        spot = pl.ds(at * pack, pack)
        far = pl.ds(begin + at * pack, pack)
        sources = [ref.at[0, :, far] for ref in stored_refs[:2]] + [stored_refs[2].at[:, spot]]
        return [
            pltpu.make_async_copy(source, data.at[idx, :, spot], sem.at[idx, at])
            for idx, source in enumerate(sources)
        ]

    for at in range(packs):
        for copy in copies(at):
            copy.start()

    def body(at, carry):
        def stack(field):
            return jnp.concatenate(
                [b_refs[k][at, field * kz_len : (field + 1) * kz_len, :] for k in range(cols)], axis=0
            ).T

        lines = jnp.concatenate([stack(field) for field in range(6)], axis=0)
        plain = dot_data_left(lines, table_ref[0], table_ref[1])
        slope = dot_data_left(lines[: 2 * LANES], table_ref[2], table_ref[3])
        new = [plain[f * LANES : (f + 1) * LANES] for f in range(6)]
        vel_new = new[:3]
        vort_new = [new[4] - slope[LANES:], slope[:LANES] + new[5], new[3]]
        for copy in copies(at):
            copy.wait()
        spot = pl.ds(at * pack, pack)
        flat = (pack * y_len, grid_len)
        vel, vort, base = [[data[idx, c, spot].reshape(flat) for c in range(3)] for idx in range(3)]
        one, two = cross(vel_new, vort), cross(vel, vort_new)
        total = [one[c] + two[c] + base[c] for c in range(3)]
        result = dot_data_right(table_ref[0], table_ref[1], jnp.concatenate(total, axis=0))
        for k in range(cols):
            for comp in range(3):
                out_refs[k][at, comp * kz_len : (comp + 1) * kz_len, :] = result[
                    k * kz_len : (k + 1) * kz_len, comp * LANES : (comp + 1) * LANES
                ]
        return carry

    lax.fori_loop(0, packs, body, 0)


def third(place, arrived, velocity, vorticity, base, table, begin, dims):
    kz_len, cols, y_len, pack = dims
    packs = arrived[0].shape[0]
    grid_len = velocity.shape[-1]
    return pl.pallas_call(
        functools.partial(third_kernel, (begin, *dims)),
        in_specs=[SMEM] + [VMEM] * cols + [ANY] * 3 + [VMEM],
        out_specs=[VMEM] * cols,
        out_shape=[jax.ShapeDtypeStruct((packs, 3 * kz_len, LANES), F32)] * cols,
        scratch_shapes=[
            pltpu.VMEM((3, 3, packs * pack, y_len, grid_len), F32),
            pltpu.SemaphoreType.DMA((3, packs)),
        ],
        compiler_params=still(),
        cost_estimate=SHORT,
        name="third_dimension",
    )(place, *arrived, velocity, vorticity, base, table)


def second_back_kernel(dims, place_ref, *refs):
    rows, xc, ky_len, kz_len, cols, y_len, pack = dims
    c_refs, table_ref, outs, all_ref = refs[:cols], refs[cols], refs[cols + 1 : -1], refs[-1]
    width = 3 * kz_len
    high_pad = round_up(width, LANES)

    def body(at, carry):
        lines = []
        for part in range(pack):
            tiles = lane_pack(
                [c_ref[at] for c_ref in c_refs], y_len, part * y_len
            )
            lines.append(jnp.concatenate(tiles, axis=1))
            if high_pad > width:
                lines.append(jnp.zeros((high_pad - width, cols * y_len), F32))
        result = dot_data_right(table_ref[0], table_ref[1], jnp.concatenate(lines, axis=0))
        for part in range(pack):
            own = result[:, part * high_pad : (part + 1) * high_pad]
            tiles = lane_pack([own[ky * rows : (ky + 1) * rows] for ky in range(ky_len)], width)
            for idx, tile in enumerate(tiles):
                spot = idx * xc + at * pack + part
                all_ref[pl.ds(spot, rows, stride=len(tiles) * xc), :] = tile
        return carry

    lax.fori_loop(0, xc // pack, body, 0)
    size = all_ref.shape[0] // len(outs)
    for k, out in enumerate(outs):
        out[...] = all_ref[pl.ds(pl.multiple_of((place_ref[0] ^ k) * size, 8), size), :]


def second_back(place, arrived, table, dims):
    rows, xc, ky_len, kz_len, cols, y_len, pack = dims
    size = round_up(ky_len * 3 * kz_len, LANES) // LANES * xc
    groups = rows // 2
    return pl.pallas_call(
        functools.partial(second_back_kernel, dims),
        in_specs=[SMEM] + [VMEM] * (cols + 1),
        out_specs=[VMEM] * groups,
        out_shape=[jax.ShapeDtypeStruct((2 * size, LANES), F32)] * groups,
        scratch_shapes=[pltpu.VMEM((rows * size, LANES), F32)],
        compiler_params=still(),
        cost_estimate=SHORT,
        name="second_back",
    )(place, *arrived, table)


def first_back_kernel(dims, place_ref, *refs):
    count, sizes, own = dims
    parts, table_ref, out_ref = refs[:count], refs[count], refs[count + 1]
    groups = count // len(sizes)
    core = place_ref[1] if own else 1 - place_ref[1]
    for tile in range(out_ref.shape[1] // LANES):
        found = []
        for idx, part in enumerate(parts):
            xc = sizes[idx // groups]
            spot = pl.multiple_of(core * (part.shape[0] // 2) + tile * xc, 8)
            found.append(part[pl.ds(spot, xc), :])
        out_ref[:, tile * LANES : (tile + 1) * LANES] = dot_data_right(
            table_ref[0], table_ref[1], jnp.concatenate(found, axis=0), NN
        )


def first_back(place, parts, table, sizes, own):
    count = len(parts)
    tiles = parts[0].shape[0] // 2 // sizes[0]
    return pl.pallas_call(
        functools.partial(first_back_kernel, (count, tuple(sizes), own)),
        in_specs=[SMEM] + [VMEM] * (count + 1),
        out_specs=VMEM,
        out_shape=jax.ShapeDtypeStruct((table.shape[1], tiles * LANES), F32),
        compiler_params=still(),
        cost_estimate=SHORT,
        name="first_back",
    )(place, *parts, table)


def last_kernel(dims, *refs):
    kz_len, modes, scale = dims
    wave_y_ref, wave_x_ref, wave_z_ref, *sums, out_ref, rows, held, sem = refs
    pair = 2 * 3 * kz_len
    for tile in range(rows.shape[0] // LANES):
        lanes = slice(tile * LANES, (tile + 1) * LANES)
        rows[lanes, 0:modes] = functools.reduce(jnp.add, [part[:, lanes] for part in sums]).T

    def copy(at):
        spot = pl.ds(2 * at, 2)
        return pltpu.make_async_copy(held.at[:, spot], out_ref.at[:, spot], sem.at[at])

    def body(at, carry):
        project(at)
        copy(at).start()
        return carry

    def finish(at, carry):
        copy(at).wait()
        return carry

    def project(at):
        spec = rows[pl.ds(pl.multiple_of(at * pair, 8), pair), :]
        wide = spec.shape[1]
        wave_x = jnp.broadcast_to(wave_x_ref[0:1, :], (kz_len, wide))
        wave_z = wave_z_ref[...]
        wave_y = wave_y_ref[at]
        even_x = lax.broadcasted_iota(jnp.int32, (kz_len, wide), 1) % 2 == 0
        even_z = lax.broadcasted_iota(jnp.int32, (kz_len, wide), 0) % 2 == 0

        def slope_x(value):
            return jnp.where(even_x, turn(value, -1), -turn(value, 1)) * wave_x

        def slope_z(value):
            return (
                jnp.where(
                    even_z,
                    pltpu.roll(value, kz_len - 1, axis=0),
                    -pltpu.roll(value, 1, axis=0),
                )
                * wave_z
            )

        s = [
            [spec[(y * 3 + c) * kz_len : (y * 3 + c + 1) * kz_len] for c in range(3)] for y in range(2)
        ]
        square = wave_x * wave_x + wave_z * wave_z + wave_y * wave_y
        positive = square > 0
        safe = jnp.where(positive, square, 1.0)
        potential = []
        for y in range(2):
            along_y = s[1 - y][1] * (wave_y if y == 0 else -wave_y)
            divergence = slope_x(s[y][0]) + along_y + slope_z(s[y][2])
            potential.append(jnp.where(positive, divergence / safe, 0.0))
        for y in range(2):
            along_y = potential[1 - y] * (wave_y if y == 0 else -wave_y)
            found = [
                s[y][0] + slope_x(potential[y]),
                s[y][1] + along_y,
                s[y][2] + slope_z(potential[y]),
            ]
            for comp in range(3):
                held[comp, 2 * at + y] = (found[comp] * scale)[:, :modes]

    steps = held.shape[1] // 2
    lax.fori_loop(0, steps, body, 0)
    lax.fori_loop(0, steps, finish, 0)


def last(sums, wave_y, wave_x, wave_z, ky_len, kz_len, scale):
    modes, lanes = sums[0].shape
    return pl.pallas_call(
        functools.partial(last_kernel, (kz_len, modes, scale)),
        in_specs=[SMEM] + [VMEM] * (2 + len(sums)),
        out_specs=ANY,
        out_shape=jax.ShapeDtypeStruct((3, ky_len, kz_len, modes), F32),
        scratch_shapes=[
            pltpu.VMEM((lanes, wave_x.shape[1]), F32),
            pltpu.VMEM((3, ky_len, kz_len, modes), F32),
            pltpu.SemaphoreType.DMA((ky_len // 2,)),
        ],
        compiler_params=still(),
        cost_estimate=SHORT,
        name="last_projection",
    )(wave_y, wave_x, wave_z, *sums)


def after(value, *earlier_values):
    return lax.optimization_barrier((value, earlier_values))[0]


def shards(new_velocity, stored_velocity, stored_vorticity):
    rows = lax.axis_size("row")
    cols = lax.axis_size("col")
    _, ky_len, kz_own, modes = new_velocity.shape
    orders, _, x_len, y_len, grid_len = stored_velocity.shape
    kz_len = round_up(kz_own, 8)
    kmax = modes // 2 - 1
    sizes = chunk_sizes(x_len)
    chunks = len(sizes)
    begins = [sum(sizes[:k]) for k in range(chunks)]
    pack = LANES // y_len
    wide = round_up(modes, LANES)
    group = 5 * kz_len
    lanes = round_up(ky_len * group, 256)

    basis = synth_np(grid_len, modes)
    slope = slope_np(basis, kmax)
    y_order = (np.arange(rows)[None, :] * ky_len + np.arange(ky_len)[:, None]).reshape(-1)

    groups = rows // 2
    row, col = lax.axis_index("row"), lax.axis_index("col")
    place = jnp.stack([row // 2, row % 2, col]).astype(jnp.int32)

    def own_table(tables, axis):
        return lax.dynamic_index_in_dim(jnp.asarray(np.stack(tables)), lax.axis_index(axis), 0, False)

    def x_points(row):
        owner = np.array([row ^ (2 * k) for k in range(groups)])
        return np.concatenate(
            [
                (owner[:, None] * x_len + begin + np.arange(xc)[None, :]).reshape(-1)
                for begin, xc in zip(begins, sizes)
            ]
        )

    def halves_of(plain, sloped):
        return np.stack([part for table in (plain, sloped) for part in halves(table)])

    def y_table(col):
        points = np.concatenate([(col ^ k) * y_len + np.arange(y_len) for k in range(cols)])
        return halves_of(basis[points].T[y_order], slope[points].T[y_order])

    def z_table(col):
        def spread(table):
            parts = table.T.reshape(cols, kz_own, grid_len)[[col ^ k for k in range(cols)]]
            parts = np.pad(parts, ((0, 0), (0, kz_len - kz_own), (0, 0)))
            return parts.reshape(cols * kz_len, grid_len)

        return halves_of(spread(basis), spread(slope))

    table_x = own_table(
        [halves_of(basis[x_points(row)].T, slope[x_points(row)].T) for row in range(rows)], "row"
    )
    table_y = own_table([y_table(col) for col in range(cols)], "col")
    table_z = own_table([z_table(col) for col in range(cols)], "col")

    def wave_of(index):
        return (index // 2).astype(F32) / kmax

    mode = jnp.arange(wide, dtype=jnp.int32)
    wave_x = jnp.broadcast_to(jnp.where(mode < modes, wave_of(mode), 0.0)[None, :], (8, wide))
    ky_first = lax.axis_index("row") * ky_len + 2 * jnp.arange(ky_len // 2, dtype=jnp.int32)
    wave_y = wave_of(ky_first)
    kz = lax.axis_index("col") * kz_own + jnp.arange(kz_len, dtype=jnp.int32)
    wave_z = jnp.broadcast_to(wave_of(kz)[:, None], (kz_len, wide))

    coeffs = new_velocity
    if kz_len > kz_own:
        coeffs = jnp.pad(coeffs, ((0, 0), (0, 0), (0, kz_len - kz_own), (0, 0)))

    def exchange(values, axis, shift, size):
        return [
            lax.ppermute(value, axis, [(src, src ^ (k << shift)) for src in range(size)]) if k else value
            for k, value in enumerate(values)
        ]

    def core_swap(value):
        return lax.ppermute(value, "row", [(src, src ^ 1) for src in range(rows)])

    dims = [(rows, xc, ky_len, kz_len, cols, y_len, pack) for xc in sizes]
    shape = (tuple(sizes), groups)
    other = core_swap(coeffs)
    small = (place, table_x, table_y, table_z, wave_x, wave_y, wave_z)
    place, table_x, table_y, table_z, wave_x, wave_y, wave_z = lax.optimization_barrier(small)

    def run_first(chosen, gate):
        own = coeffs if gate is None else after(coeffs, gate)
        found = first_synth(place, own, table_x, shape, chosen, lanes, ())
        found = first_synth(place, other, table_x, shape, chosen, lanes, found)
        return {chunk: list(found[k * groups : (k + 1) * groups]) for k, chunk in enumerate(chosen)}

    sent = run_first((0,), None)
    if chunks > 1:
        sent.update(run_first(tuple(range(1, chunks)), sent[0][0]))
    latest = sent[chunks - 1][0]

    def ordered(kernel, operands, *others):
        nonlocal latest
        operands = after(operands, latest)
        found = kernel(operands, *others)
        latest = found[0] if isinstance(found, (list, tuple)) else found
        return found

    stored = (stored_velocity, stored_vorticity)

    def run_earlier(chunk):
        return ordered(lambda values: earlier(*values, begins[chunk], sizes[chunk], pack), stored)

    def z_exchange(values, *gates, waves=True):
        found = [values[0]]
        for k in range(1, groups):
            value = values[k]
            if gates:
                value = after(value, found[groups // 2]) if waves and 2 * k > groups else after(value, *gates)
            found.append(lax.ppermute(value, "row", [(src, src ^ (2 * k)) for src in range(rows)]))
        return found

    first, second, middle, back, base = {}, {}, {}, {}, {}
    for step in range(chunks):
        first[step] = z_exchange(sent[step], *([first[step - 1]] if step else []), waves=step > 1)

    def run_second(at):
        found = ordered(lambda values: second_synth(place, values, table_y, dims[at]), first[at])
        if at:
            gates = [second[at - 1]] + ([middle[at - 1]] if at - 1 in middle else [])
            found = [found[0]] + [after(value, *gates) for value in found[1:]]
        second[at] = exchange(found, "col", 0, cols)

    def run_third(at):
        found = ordered(
            lambda values: third(
                place, values, *stored, base[at], table_z, begins[at], dims[at][3:]
            ),
            second[at],
        )
        middle[at] = exchange(found, "col", 0, cols)

    def run_back(at):
        values = after(middle[at], back[0]) if at == 1 else middle[at]
        found = ordered(lambda values: second_back(place, values, table_y, dims[at]), values)
        gate = back[at - 1] if at else first[chunks - 1]
        back[at] = z_exchange(found, gate, waves=at == 0)

    def run_base(at):
        base[at] = run_earlier(at)

    plan = [(run_second, 0), (run_base, 0), (run_second, 1), (run_third, 0), (run_base, 1), (run_base, 2)]
    plan += [(run_third, 1), (run_back, 0), (run_second, 2), (run_back, 1), (run_third, 2), (run_back, 2)]
    for action, at in plan:
        if at < chunks:
            action(at)
    parts = [value for step in range(chunks) for value in back[step]]
    away = first_back(place, parts, table_x, sizes, False)
    home = first_back(place, parts, after(table_x, away), sizes, True)
    sums = [home, core_swap(away)]
    result = last(sums, wave_y, wave_x, wave_z, ky_len, kz_len, 1.0 / (orders + 1))
    return result[:, :, :kz_own] if kz_len > kz_own else result


def solution(mesh):
    return jax.shard_map(
        shards,
        mesh=mesh,
        in_specs=(
            P(None, "row", "col", None),
            P(None, None, "row", "col", None),
            P(None, None, "row", "col", None),
        ),
        out_specs=P(None, "row", "col", None),
        check_vma=False,
    )
```

```python
import functools
import math

import jax
import jax.numpy as jnp
import ml_dtypes
import numpy as np
from jax import lax
from jax.experimental import pallas as pl
from jax.experimental.pallas import tpu as pltpu
from jax.sharding import PartitionSpec as P

LANES = 128


def chunk_sizes(x_len):
    ends = 8
    return [ends, x_len - 2 * ends, ends] if x_len > 3 * ends else [ends] * (x_len // ends)

BF16 = jnp.bfloat16
F32 = jnp.float32
NN = (((1,), (0,)), ((), ()))
NT = (((1,), (1,)), ((), ()))


def round_up(value, step):
    return -(-value // step) * step


def synth_np(grid_len, mode_count):
    points = np.arange(grid_len)[:, None]
    mode_index = np.arange(mode_count)[None, :]
    wave_index = np.where(mode_index == 1, grid_len // 2, mode_index // 2)
    angles = (points * wave_index % grid_len) * (2.0 * math.pi / grid_len)
    trig = np.where((mode_index % 2 == 0) | (mode_index == 1), np.cos(angles), np.sin(angles))
    weight = np.where(mode_index < 2, 1.0, 2.0) / grid_len
    return np.where(mode_index == 1, 0.0, trig * np.sqrt(weight))


def slope_np(table, kmax):
    paired = table.reshape(table.shape[0], -1, 2)
    wavenum = np.arange(paired.shape[1]) / kmax
    return np.stack([-wavenum * paired[:, :, 1], wavenum * paired[:, :, 0]], -1).reshape(table.shape)


def halves(table):
    high = table.astype(ml_dtypes.bfloat16)
    low = (table - high.astype(np.float64)).astype(ml_dtypes.bfloat16)
    return high, low


def pieces_of(values):
    high = values.astype(BF16)
    return high, (values - high.astype(F32)).astype(BF16)


def dot(left, right, dims):
    return lax.dot_general(left, right, dims, preferred_element_type=F32)


def dot_data_left(values, high, low, dims=NN):
    top, rest = pieces_of(values)
    return dot(top, high, dims) + (dot(top, low, dims) + dot(rest, high, dims))


def dot_data_right(high, low, values, dims=NT):
    top, rest = pieces_of(values)
    return dot(high, top, dims) + (dot(low, top, dims) + dot(high, rest, dims))


def turn(values, shift):
    shift = shift % values.shape[-1]
    return values if shift == 0 else pltpu.roll(values, shift, axis=values.ndim - 1)


def lane_pack(parts, width, source_lane=0):
    tiles = []
    lane = lax.broadcasted_iota(jnp.int32, parts[0].shape, 1)
    for tile in range(-(-len(parts) * width // LANES)):
        start = tile * LANES
        acc = None
        for idx in range(start // width, min(len(parts) - 1, (start + LANES - 1) // width) + 1):
            moved = turn(parts[idx], idx * width - source_lane)
            acc = moved if acc is None else jnp.where(lane >= idx * width - start, moved, acc)
        tiles.append(acc)
    return tiles


VMEM_LIMIT = 32 * 1024 * 1024
VMEM_MOST = 60 * 1024 * 1024
SHORT = pl.CostEstimate(flops=1024, bytes_accessed=1024, transcendentals=0)
ANY = pl.BlockSpec(memory_space=pl.ANY)
HBM = pl.BlockSpec(memory_space=pltpu.HBM)
SMEM = pl.BlockSpec(memory_space=pltpu.SMEM)
VMEM = pl.BlockSpec(memory_space=pltpu.VMEM)


def params():
    return pltpu.CompilerParams(dimension_semantics=("arbitrary",), vmem_limit_bytes=VMEM_LIMIT)


def still(limit=VMEM_LIMIT):
    return pltpu.CompilerParams(vmem_limit_bytes=limit)


def both_passes(values, high_low, high):
    top, rest = pieces_of(values)
    wide = dot(top, high_low, NN)
    half = high.shape[1]
    return wide[:, :half] + (wide[:, half:] + dot(rest, high, NN))


def whole(array):
    rank = len(array.shape)
    return pl.BlockSpec(array.shape, lambda *_: (0,) * rank)


def first_synth_kernel(dims, place_ref, data, table_ref, *rest):
    sizes, chosen, dests, own = dims
    outs, rows = rest[-len(chosen) * dests - 1 : -1], rest[-1]
    _, ky_len, kz_len, _ = data.shape
    group = 5 * kz_len
    if ky_len * group < rows.shape[0]:
        rows[ky_len * group :, :] = jnp.zeros((rows.shape[0] - ky_len * group, LANES), F32)
    plain = jnp.concatenate([table_ref[0], table_ref[1]], axis=1)
    slope = jnp.concatenate([table_ref[2], table_ref[3]], axis=1)
    step = 4 if ky_len % 4 == 0 else 2

    def body(idx, carry):
        first = idx * step
        lines = [[data[comp, first + k] for comp in range(3)] for k in range(step)]
        found = both_passes(
            jnp.concatenate([v for line in lines for v in line], axis=0), plain, table_ref[0]
        )
        sloped = both_passes(
            jnp.concatenate([v for line in lines for v in line[1:]], axis=0), slope, table_ref[2]
        )
        for k in range(step):
            base = (first + k) * group
            rows[pl.ds(pl.multiple_of(base, 8), 3 * kz_len), :] = found[
                3 * k * kz_len : 3 * (k + 1) * kz_len
            ]
            rows[pl.ds(pl.multiple_of(base + 3 * kz_len, 8), 2 * kz_len), :] = sloped[
                2 * k * kz_len : 2 * (k + 1) * kz_len
            ]
        return carry

    lax.fori_loop(0, ky_len // step, body, 0)

    core = place_ref[1] if own else 1 - place_ref[1]

    def flip(tile, carry):
        found = rows[pl.ds(pl.multiple_of(tile * LANES, LANES), LANES), :].T
        for idx, out in enumerate(outs):
            chunk, k = chosen[idx // dests], idx % dests
            xc = sizes[chunk]
            at = sum(sizes[:chunk]) * dests + k * xc
            spot = core * (out.shape[0] // 2) + tile * xc
            out[pl.ds(pl.multiple_of(spot, 8), xc), :] = found[at : at + xc]
        return carry

    lax.fori_loop(0, rows.shape[0] // LANES, flip, 0, unroll=2)


def first_synth(place, coeffs, table, dims, chosen, lanes, half):
    sizes, dests = dims
    heights = [2 * (lanes // LANES) * sizes[chunk] for chunk in chosen for _ in range(dests)]
    return pl.pallas_call(
        functools.partial(first_synth_kernel, (sizes, chosen, dests, not half)),
        in_specs=[SMEM, VMEM, VMEM] + [ANY] * len(half),
        out_specs=[VMEM] * len(heights),
        out_shape=[jax.ShapeDtypeStruct((h, LANES), F32) for h in heights],
        input_output_aliases={3 + k: k for k in range(len(half))},
        scratch_shapes=[pltpu.VMEM((lanes, LANES), F32)],
        compiler_params=still(),
        cost_estimate=SHORT,
        name="first_synth",
    )(place, coeffs, table, *half)


def second_synth_kernel(dims, place_ref, *refs):
    rows, xc, ky_len, kz_len, cols, y_len, pack = dims
    groups = rows // 2
    parts, table_ref, out_refs = refs[:groups], refs[groups], refs[groups + 1 : -1]
    a_ref = refs[-1]
    size = parts[0].shape[0] // 2
    stride = a_ref.shape[0] // rows
    for k, part in enumerate(parts):
        for core in range(2):
            spot = pl.multiple_of(((place_ref[0] ^ k) * 2 + core) * stride, 8)
            a_ref[pl.ds(spot, size), :] = part[core * size : (core + 1) * size, :]
    group = 5 * kz_len
    wide = round_up(group, LANES)
    tiles = size // xc

    def body(at, carry):
        turned = []
        for part in range(pack):
            line = [
                a_ref[pl.ds(tile * xc + at * pack + part, rows, stride=stride), :]
                for tile in range(tiles)
            ]
            found = []
            for ky in range(ky_len):
                start = ky * group
                low, off = divmod(start, LANES)
                window = line[low : low + (wide // LANES) + (1 if off else 0)]
                found.append(turn(jnp.concatenate(window, axis=1), -off)[:, :wide])
            turned.append(jnp.concatenate(found, axis=0).T[:group])
        plain = dot_data_left(jnp.concatenate(turned, axis=0), table_ref[0], table_ref[1])
        slope_in = [t[c * kz_len : (c + 1) * kz_len] for t in turned for c in (0, 2)]
        slope = dot_data_left(jnp.concatenate(slope_in, axis=0), table_ref[2], table_ref[3])
        fields = []
        for part in range(pack):
            own = plain[part * group : (part + 1) * group]
            sl = slope[part * 2 * kz_len : (part + 1) * 2 * kz_len]
            fields.append(
                jnp.concatenate(
                    [
                        own[: 3 * kz_len],
                        own[3 * kz_len : 4 * kz_len] - sl[:kz_len],
                        sl[kz_len:],
                        -own[4 * kz_len :],
                    ],
                    axis=0,
                )
            )
        for dest in range(cols):
            tile, off = divmod(dest * y_len, LANES)
            out_refs[dest][at] = lane_pack(
                [f[:, tile * LANES : (tile + 1) * LANES] for f in fields], y_len, off
            )[0]
        return carry

    lax.fori_loop(0, xc // pack, body, 0)


def second_synth(place, arrived, table, dims):
    rows, xc, ky_len, kz_len, cols, y_len, pack = dims
    packs = xc // pack
    return pl.pallas_call(
        functools.partial(second_synth_kernel, dims),
        in_specs=[SMEM] + [VMEM] * (len(arrived) + 1),
        out_specs=[VMEM] * cols,
        out_shape=[jax.ShapeDtypeStruct((packs, 6 * kz_len, LANES), F32)] * cols,
        scratch_shapes=[
            pltpu.VMEM((rows * (arrived[0].shape[0] // 2 + 8), LANES), F32),
        ],
        compiler_params=still(),
        cost_estimate=SHORT,
        name="second_synth",
    )(place, *arrived, table)


def cross(left, right):
    return [
        left[1] * right[2] - left[2] * right[1],
        left[2] * right[0] - left[0] * right[2],
        left[0] * right[1] - left[1] * right[0],
    ]


def earlier_kernel(count, *refs):
    vels, vorts, out_ref = refs[:count], refs[count : 2 * count], refs[2 * count]
    pack, y_len = out_ref.shape[1:3]
    for part in range(pack):
        def body(step, carry):
            at = pl.ds(pl.multiple_of(step * 8, 8), 8)
            total = None
            for vel, vort in zip(vels, vorts):
                term = cross(
                    [vel[0, c, part, at, :] for c in range(3)],
                    [vort[0, c, part, at, :] for c in range(3)],
                )
                total = term if total is None else [a + b for a, b in zip(total, term)]
            for comp in range(3):
                out_ref[comp, part, at, :] = total[comp]
            return carry

        lax.fori_loop(0, y_len // 8, body, 0, unroll=2)


def earlier(velocity, vorticity, start, xc, pack):
    orders, _, _, y_len, grid_len = velocity.shape
    packs = xc // pack
    block = (1, 3, pack, y_len, grid_len)

    def at(order):
        return pl.BlockSpec(block, lambda i: (order, 0, start // pack + i, 0, 0))

    specs = [at(k) for k in range(1, orders)] + [at(orders - k) for k in range(1, orders)]
    size = xc * y_len * grid_len
    return pl.pallas_call(
        functools.partial(earlier_kernel, orders - 1),
        grid=(packs,),
        in_specs=specs,
        out_specs=pl.BlockSpec((3, pack, y_len, grid_len), lambda i: (0, i, 0, 0)),
        out_shape=jax.ShapeDtypeStruct((3, xc, y_len, grid_len), F32),
        compiler_params=params(),
        cost_estimate=SHORT,
        name="earlier_orders",
    )(*[velocity] * (orders - 1), *[vorticity] * (orders - 1))


def third_kernel(dims, place_ref, *refs):
    begin, kz_len, cols, y_len, pack = dims
    b_refs, stored_refs, table_ref = refs[:cols], refs[cols : cols + 3], refs[cols + 3]
    data, sem = refs[-2:]
    out_refs = refs[-2 - cols : -2]
    grid_len = table_ref.shape[2]
    xc = data.shape[2]
    packs = xc // pack

    def copies(at):
        spot = pl.ds(at * pack, pack)
        far = pl.ds(begin + at * pack, pack)
        sources = [ref.at[0, :, far] for ref in stored_refs[:2]] + [stored_refs[2].at[:, spot]]
        return [
            pltpu.make_async_copy(source, data.at[idx, :, spot], sem.at[idx, at])
            for idx, source in enumerate(sources)
        ]

    for at in range(packs):
        for copy in copies(at):
            copy.start()

    def body(at, carry):
        def stack(field):
            return jnp.concatenate(
                [b_refs[k][at, field * kz_len : (field + 1) * kz_len, :] for k in range(cols)], axis=0
            ).T

        lines = jnp.concatenate([stack(field) for field in range(6)], axis=0)
        plain = dot_data_left(lines, table_ref[0], table_ref[1])
        slope = dot_data_left(lines[: 2 * LANES], table_ref[2], table_ref[3])
        new = [plain[f * LANES : (f + 1) * LANES] for f in range(6)]
        vel_new = new[:3]
        vort_new = [new[4] - slope[LANES:], slope[:LANES] + new[5], new[3]]
        for copy in copies(at):
            copy.wait()
        spot = pl.ds(at * pack, pack)
        flat = (pack * y_len, grid_len)
        vel, vort, base = [[data[idx, c, spot].reshape(flat) for c in range(3)] for idx in range(3)]
        one, two = cross(vel_new, vort), cross(vel, vort_new)
        total = [one[c] + two[c] + base[c] for c in range(3)]
        result = dot_data_right(table_ref[0], table_ref[1], jnp.concatenate(total, axis=0))
        for k in range(cols):
            for comp in range(3):
                out_refs[k][at, comp * kz_len : (comp + 1) * kz_len, :] = result[
                    k * kz_len : (k + 1) * kz_len, comp * LANES : (comp + 1) * LANES
                ]
        return carry

    lax.fori_loop(0, packs, body, 0)


def third(place, arrived, velocity, vorticity, base, table, begin, dims):
    kz_len, cols, y_len, pack = dims
    packs = arrived[0].shape[0]
    grid_len = velocity.shape[-1]
    return pl.pallas_call(
        functools.partial(third_kernel, (begin, *dims)),
        in_specs=[SMEM] + [VMEM] * cols + [ANY] * 3 + [VMEM],
        out_specs=[VMEM] * cols,
        out_shape=[jax.ShapeDtypeStruct((packs, 3 * kz_len, LANES), F32)] * cols,
        scratch_shapes=[
            pltpu.VMEM((3, 3, packs * pack, y_len, grid_len), F32),
            pltpu.SemaphoreType.DMA((3, packs)),
        ],
        compiler_params=still(),
        cost_estimate=SHORT,
        name="third_dimension",
    )(place, *arrived, velocity, vorticity, base, table)


def second_back_kernel(dims, place_ref, *refs):
    rows, xc, ky_len, kz_len, cols, y_len, pack = dims
    c_refs, table_ref, outs, all_ref = refs[:cols], refs[cols], refs[cols + 1 : -1], refs[-1]
    width = 3 * kz_len
    high_pad = round_up(width, LANES)

    def body(at, carry):
        lines = []
        for part in range(pack):
            tiles = lane_pack(
                [c_ref[at] for c_ref in c_refs], y_len, part * y_len
            )
            lines.append(jnp.concatenate(tiles, axis=1))
            if high_pad > width:
                lines.append(jnp.zeros((high_pad - width, cols * y_len), F32))
        result = dot_data_right(table_ref[0], table_ref[1], jnp.concatenate(lines, axis=0))
        for part in range(pack):
            own = result[:, part * high_pad : (part + 1) * high_pad]
            tiles = lane_pack([own[ky * rows : (ky + 1) * rows] for ky in range(ky_len)], width)
            for idx, tile in enumerate(tiles):
                spot = idx * xc + at * pack + part
                all_ref[pl.ds(spot, rows, stride=len(tiles) * xc), :] = tile
        return carry

    lax.fori_loop(0, xc // pack, body, 0)
    size = all_ref.shape[0] // len(outs)
    for k, out in enumerate(outs):
        out[...] = all_ref[pl.ds(pl.multiple_of((place_ref[0] ^ k) * size, 8), size), :]


def second_back(place, arrived, table, dims):
    rows, xc, ky_len, kz_len, cols, y_len, pack = dims
    size = round_up(ky_len * 3 * kz_len, LANES) // LANES * xc
    groups = rows // 2
    return pl.pallas_call(
        functools.partial(second_back_kernel, dims),
        in_specs=[SMEM] + [VMEM] * (cols + 1),
        out_specs=[VMEM] * groups,
        out_shape=[jax.ShapeDtypeStruct((2 * size, LANES), F32)] * groups,
        scratch_shapes=[pltpu.VMEM((rows * size, LANES), F32)],
        compiler_params=still(),
        cost_estimate=SHORT,
        name="second_back",
    )(place, *arrived, table)


def first_back_kernel(dims, place_ref, *refs):
    count, sizes, own = dims
    parts, table_ref, out_ref = refs[:count], refs[count], refs[count + 1]
    groups = count // len(sizes)
    core = place_ref[1] if own else 1 - place_ref[1]
    for tile in range(out_ref.shape[1] // LANES):
        found = []
        for idx, part in enumerate(parts):
            xc = sizes[idx // groups]
            spot = pl.multiple_of(core * (part.shape[0] // 2) + tile * xc, 8)
            found.append(part[pl.ds(spot, xc), :])
        out_ref[:, tile * LANES : (tile + 1) * LANES] = dot_data_right(
            table_ref[0], table_ref[1], jnp.concatenate(found, axis=0), NN
        )


def first_back(place, parts, table, sizes, own):
    count = len(parts)
    tiles = parts[0].shape[0] // 2 // sizes[0]
    return pl.pallas_call(
        functools.partial(first_back_kernel, (count, tuple(sizes), own)),
        in_specs=[SMEM] + [VMEM] * (count + 1),
        out_specs=VMEM,
        out_shape=jax.ShapeDtypeStruct((table.shape[1], tiles * LANES), F32),
        compiler_params=still(),
        cost_estimate=SHORT,
        name="first_back",
    )(place, *parts, table)


def last_kernel(dims, *refs):
    kz_len, modes, scale = dims
    wave_y_ref, wave_x_ref, wave_z_ref, *sums, out_ref, rows, held, sem = refs
    pair = 2 * 3 * kz_len
    for tile in range(rows.shape[0] // LANES):
        lanes = slice(tile * LANES, (tile + 1) * LANES)
        rows[lanes, 0:modes] = functools.reduce(jnp.add, [part[:, lanes] for part in sums]).T

    def copy(at):
        spot = pl.ds(2 * at, 2)
        return pltpu.make_async_copy(held.at[:, spot], out_ref.at[:, spot], sem.at[at])

    def body(at, carry):
        project(at)
        copy(at).start()
        return carry

    def finish(at, carry):
        copy(at).wait()
        return carry

    def project(at):
        spec = rows[pl.ds(pl.multiple_of(at * pair, 8), pair), :]
        wide = spec.shape[1]
        wave_x = jnp.broadcast_to(wave_x_ref[0:1, :], (kz_len, wide))
        wave_z = wave_z_ref[...]
        wave_y = wave_y_ref[at]
        even_x = lax.broadcasted_iota(jnp.int32, (kz_len, wide), 1) % 2 == 0
        even_z = lax.broadcasted_iota(jnp.int32, (kz_len, wide), 0) % 2 == 0

        def slope_x(value):
            return jnp.where(even_x, turn(value, -1), -turn(value, 1)) * wave_x

        def slope_z(value):
            return (
                jnp.where(
                    even_z,
                    pltpu.roll(value, kz_len - 1, axis=0),
                    -pltpu.roll(value, 1, axis=0),
                )
                * wave_z
            )

        s = [
            [spec[(y * 3 + c) * kz_len : (y * 3 + c + 1) * kz_len] for c in range(3)] for y in range(2)
        ]
        square = wave_x * wave_x + wave_z * wave_z + wave_y * wave_y
        positive = square > 0
        safe = jnp.where(positive, square, 1.0)
        potential = []
        for y in range(2):
            along_y = s[1 - y][1] * (wave_y if y == 0 else -wave_y)
            divergence = slope_x(s[y][0]) + along_y + slope_z(s[y][2])
            potential.append(jnp.where(positive, divergence / safe, 0.0))
        for y in range(2):
            along_y = potential[1 - y] * (wave_y if y == 0 else -wave_y)
            found = [
                s[y][0] + slope_x(potential[y]),
                s[y][1] + along_y,
                s[y][2] + slope_z(potential[y]),
            ]
            for comp in range(3):
                held[comp, 2 * at + y] = (found[comp] * scale)[:, :modes]

    steps = held.shape[1] // 2
    lax.fori_loop(0, steps, body, 0)
    lax.fori_loop(0, steps, finish, 0)


def last(sums, wave_y, wave_x, wave_z, ky_len, kz_len, scale):
    modes, lanes = sums[0].shape
    return pl.pallas_call(
        functools.partial(last_kernel, (kz_len, modes, scale)),
        in_specs=[SMEM] + [VMEM] * (2 + len(sums)),
        out_specs=ANY,
        out_shape=jax.ShapeDtypeStruct((3, ky_len, kz_len, modes), F32),
        scratch_shapes=[
            pltpu.VMEM((lanes, wave_x.shape[1]), F32),
            pltpu.VMEM((3, ky_len, kz_len, modes), F32),
            pltpu.SemaphoreType.DMA((ky_len // 2,)),
        ],
        compiler_params=still(),
        cost_estimate=SHORT,
        name="last_projection",
    )(wave_y, wave_x, wave_z, *sums)


def after(value, *earlier_values):
    return lax.optimization_barrier((value, earlier_values))[0]


def shards(new_velocity, stored_velocity, stored_vorticity):
    rows = lax.axis_size("row")
    cols = lax.axis_size("col")
    _, ky_len, kz_own, modes = new_velocity.shape
    orders, _, x_len, y_len, grid_len = stored_velocity.shape
    kz_len = round_up(kz_own, 8)
    kmax = modes // 2 - 1
    sizes = chunk_sizes(x_len)
    chunks = len(sizes)
    begins = [sum(sizes[:k]) for k in range(chunks)]
    pack = LANES // y_len
    wide = round_up(modes, LANES)
    group = 5 * kz_len
    lanes = round_up(ky_len * group, 256)

    basis = synth_np(grid_len, modes)
    slope = slope_np(basis, kmax)
    y_order = (np.arange(rows)[None, :] * ky_len + np.arange(ky_len)[:, None]).reshape(-1)

    groups = rows // 2
    row, col = lax.axis_index("row"), lax.axis_index("col")
    place = jnp.stack([row // 2, row % 2, col]).astype(jnp.int32)

    def own_table(tables, axis):
        return lax.dynamic_index_in_dim(jnp.asarray(np.stack(tables)), lax.axis_index(axis), 0, False)

    def x_points(row):
        owner = np.array([row ^ (2 * k) for k in range(groups)])
        return np.concatenate(
            [
                (owner[:, None] * x_len + begin + np.arange(xc)[None, :]).reshape(-1)
                for begin, xc in zip(begins, sizes)
            ]
        )

    def halves_of(plain, sloped):
        return np.stack([part for table in (plain, sloped) for part in halves(table)])

    def y_table(col):
        points = np.concatenate([(col ^ k) * y_len + np.arange(y_len) for k in range(cols)])
        return halves_of(basis[points].T[y_order], slope[points].T[y_order])

    def z_table(col):
        def spread(table):
            parts = table.T.reshape(cols, kz_own, grid_len)[[col ^ k for k in range(cols)]]
            parts = np.pad(parts, ((0, 0), (0, kz_len - kz_own), (0, 0)))
            return parts.reshape(cols * kz_len, grid_len)

        return halves_of(spread(basis), spread(slope))

    table_x = own_table(
        [halves_of(basis[x_points(row)].T, slope[x_points(row)].T) for row in range(rows)], "row"
    )
    table_y = own_table([y_table(col) for col in range(cols)], "col")
    table_z = own_table([z_table(col) for col in range(cols)], "col")

    def wave_of(index):
        return (index // 2).astype(F32) / kmax

    mode = jnp.arange(wide, dtype=jnp.int32)
    wave_x = jnp.broadcast_to(jnp.where(mode < modes, wave_of(mode), 0.0)[None, :], (8, wide))
    ky_first = lax.axis_index("row") * ky_len + 2 * jnp.arange(ky_len // 2, dtype=jnp.int32)
    wave_y = wave_of(ky_first)
    kz = lax.axis_index("col") * kz_own + jnp.arange(kz_len, dtype=jnp.int32)
    wave_z = jnp.broadcast_to(wave_of(kz)[:, None], (kz_len, wide))

    coeffs = new_velocity
    if kz_len > kz_own:
        coeffs = jnp.pad(coeffs, ((0, 0), (0, 0), (0, kz_len - kz_own), (0, 0)))

    def exchange(values, axis, shift, size):
        return [
            lax.ppermute(value, axis, [(src, src ^ (k << shift)) for src in range(size)]) if k else value
            for k, value in enumerate(values)
        ]

    def core_swap(value):
        return lax.ppermute(value, "row", [(src, src ^ 1) for src in range(rows)])

    dims = [(rows, xc, ky_len, kz_len, cols, y_len, pack) for xc in sizes]
    shape = (tuple(sizes), groups)
    other = core_swap(coeffs)
    small = (place, table_x, table_y, table_z, wave_x, wave_y, wave_z)
    place, table_x, table_y, table_z, wave_x, wave_y, wave_z = lax.optimization_barrier(small)

    def run_first(chosen, gate):
        own = coeffs if gate is None else after(coeffs, gate)
        found = first_synth(place, own, table_x, shape, chosen, lanes, ())
        found = first_synth(place, other, table_x, shape, chosen, lanes, found)
        return {chunk: list(found[k * groups : (k + 1) * groups]) for k, chunk in enumerate(chosen)}

    sent = run_first((0,), None)
    if chunks > 1:
        sent.update(run_first(tuple(range(1, chunks)), sent[0][0]))
    latest = sent[chunks - 1][0]

    def ordered(kernel, operands, *others):
        nonlocal latest
        operands = after(operands, latest)
        found = kernel(operands, *others)
        latest = found[0] if isinstance(found, (list, tuple)) else found
        return found

    stored = (stored_velocity, stored_vorticity)

    def run_earlier(chunk):
        return ordered(lambda values: earlier(*values, begins[chunk], sizes[chunk], pack), stored)

    def z_exchange(values, *gates, waves=True, lead=1):
        found = [values[0]]
        for k in range(1, groups):
            value = values[k]
            if gates:
                value = after(value, found[lead]) if waves and 2 * k > groups else after(value, *gates)
            found.append(lax.ppermute(value, "row", [(src, src ^ (2 * k)) for src in range(rows)]))
        return found

    first, second, middle, back, base = {}, {}, {}, {}, {}
    for step in range(min(2, chunks)):
        first[step] = z_exchange(sent[step], *([first[step - 1]] if step else []), lead=groups // 2)

    def run_second(at):
        found = ordered(lambda values: second_synth(place, values, table_y, dims[at]), first[at])
        if at:
            found = [found[0]] + [after(value, second[at - 1]) for value in found[1:]]
        second[at] = exchange(found, "col", 0, cols)

    def run_third(at):
        found = ordered(
            lambda values: third(
                place, values, *stored, base[at], table_z, begins[at], dims[at][3:]
            ),
            second[at],
        )
        middle[at] = exchange(found, "col", 0, cols)

    def run_back(at):
        found = ordered(lambda values: second_back(place, values, table_y, dims[at]), middle[at])
        back[at] = z_exchange(found, back[at - 1] if at else first[min(1, chunks - 1)], waves=at == 0)

    def run_base(at):
        base[at] = run_earlier(at)
        if at == 1 and chunks > 2:
            first[2] = z_exchange(sent[2], back[0], base[1])

    plan = [(run_second, 0), (run_base, 0), (run_third, 0), (run_back, 0), (run_second, 1), (run_base, 1)]
    plan += [(run_base, 2), (run_second, 2), (run_third, 1), (run_third, 2), (run_back, 1), (run_back, 2)]
    for action, at in plan:
        if at < chunks:
            action(at)
    parts = [value for step in range(chunks) for value in back[step]]
    away = first_back(place, parts, table_x, sizes, False)
    home = first_back(place, parts, after(table_x, away), sizes, True)
    sums = [home, core_swap(away)]
    result = last(sums, wave_y, wave_x, wave_z, ky_len, kz_len, 1.0 / (orders + 1))
    return result[:, :, :kz_own] if kz_len > kz_own else result


def solution(mesh):
    return jax.shard_map(
        shards,
        mesh=mesh,
        in_specs=(
            P(None, "row", "col", None),
            P(None, None, "row", "col", None),
            P(None, None, "row", "col", None),
        ),
        out_specs=P(None, "row", "col", None),
        check_vma=False,
    )
```

```python
import functools
import math

import jax
import jax.numpy as jnp
import ml_dtypes
import numpy as np
from jax import lax
from jax.experimental import pallas as pl
from jax.experimental.pallas import tpu as pltpu
from jax.sharding import PartitionSpec as P

LANES = 128


def chunk_sizes(x_len):
    ends = 8
    return [ends, x_len - 2 * ends, ends] if x_len > 3 * ends else [ends] * (x_len // ends)

BF16 = jnp.bfloat16
F32 = jnp.float32
NN = (((1,), (0,)), ((), ()))
NT = (((1,), (1,)), ((), ()))


def round_up(value, step):
    return -(-value // step) * step


def synth_np(grid_len, mode_count):
    points = np.arange(grid_len)[:, None]
    mode_index = np.arange(mode_count)[None, :]
    wave_index = np.where(mode_index == 1, grid_len // 2, mode_index // 2)
    angles = (points * wave_index % grid_len) * (2.0 * math.pi / grid_len)
    trig = np.where((mode_index % 2 == 0) | (mode_index == 1), np.cos(angles), np.sin(angles))
    weight = np.where(mode_index < 2, 1.0, 2.0) / grid_len
    return np.where(mode_index == 1, 0.0, trig * np.sqrt(weight))


def slope_np(table, kmax):
    paired = table.reshape(table.shape[0], -1, 2)
    wavenum = np.arange(paired.shape[1]) / kmax
    return np.stack([-wavenum * paired[:, :, 1], wavenum * paired[:, :, 0]], -1).reshape(table.shape)


def halves(table):
    high = table.astype(ml_dtypes.bfloat16)
    low = (table - high.astype(np.float64)).astype(ml_dtypes.bfloat16)
    return high, low


def pieces_of(values):
    high = values.astype(BF16)
    return high, (values - high.astype(F32)).astype(BF16)


def dot(left, right, dims):
    return lax.dot_general(left, right, dims, preferred_element_type=F32)


def dot_data_left(values, high, low, dims=NN):
    top, rest = pieces_of(values)
    return dot(top, high, dims) + (dot(top, low, dims) + dot(rest, high, dims))


def dot_data_right(high, low, values, dims=NT):
    top, rest = pieces_of(values)
    return dot(high, top, dims) + (dot(low, top, dims) + dot(high, rest, dims))


def turn(values, shift):
    shift = shift % values.shape[-1]
    return values if shift == 0 else pltpu.roll(values, shift, axis=values.ndim - 1)


def lane_pack(parts, width, source_lane=0):
    tiles = []
    lane = lax.broadcasted_iota(jnp.int32, parts[0].shape, 1)
    for tile in range(-(-len(parts) * width // LANES)):
        start = tile * LANES
        acc = None
        for idx in range(start // width, min(len(parts) - 1, (start + LANES - 1) // width) + 1):
            moved = turn(parts[idx], idx * width - source_lane)
            acc = moved if acc is None else jnp.where(lane >= idx * width - start, moved, acc)
        tiles.append(acc)
    return tiles


VMEM_LIMIT = 32 * 1024 * 1024
VMEM_MOST = 60 * 1024 * 1024
SHORT = pl.CostEstimate(flops=1024, bytes_accessed=1024, transcendentals=0)
ANY = pl.BlockSpec(memory_space=pl.ANY)
HBM = pl.BlockSpec(memory_space=pltpu.HBM)
SMEM = pl.BlockSpec(memory_space=pltpu.SMEM)
VMEM = pl.BlockSpec(memory_space=pltpu.VMEM)


def params():
    return pltpu.CompilerParams(dimension_semantics=("arbitrary",), vmem_limit_bytes=VMEM_LIMIT)


def still(limit=VMEM_LIMIT):
    return pltpu.CompilerParams(vmem_limit_bytes=limit)


def both_passes(values, high_low, high):
    top, rest = pieces_of(values)
    wide = dot(top, high_low, NN)
    half = high.shape[1]
    return wide[:, :half] + (wide[:, half:] + dot(rest, high, NN))


def whole(array):
    rank = len(array.shape)
    return pl.BlockSpec(array.shape, lambda *_: (0,) * rank)


def first_synth_kernel(dims, place_ref, data, table_ref, *rest):
    sizes, chosen, dests, own = dims
    outs, rows = rest[-len(chosen) * dests - 1 : -1], rest[-1]
    _, ky_len, kz_len, _ = data.shape
    group = 5 * kz_len
    if ky_len * group < rows.shape[0]:
        rows[ky_len * group :, :] = jnp.zeros((rows.shape[0] - ky_len * group, LANES), F32)
    plain = jnp.concatenate([table_ref[0], table_ref[1]], axis=1)
    slope = jnp.concatenate([table_ref[2], table_ref[3]], axis=1)
    step = 4 if ky_len % 4 == 0 else 2

    def body(idx, carry):
        first = idx * step
        lines = [[data[comp, first + k] for comp in range(3)] for k in range(step)]
        found = both_passes(
            jnp.concatenate([v for line in lines for v in line], axis=0), plain, table_ref[0]
        )
        sloped = both_passes(
            jnp.concatenate([v for line in lines for v in line[1:]], axis=0), slope, table_ref[2]
        )
        for k in range(step):
            base = (first + k) * group
            rows[pl.ds(pl.multiple_of(base, 8), 3 * kz_len), :] = found[
                3 * k * kz_len : 3 * (k + 1) * kz_len
            ]
            rows[pl.ds(pl.multiple_of(base + 3 * kz_len, 8), 2 * kz_len), :] = sloped[
                2 * k * kz_len : 2 * (k + 1) * kz_len
            ]
        return carry

    lax.fori_loop(0, ky_len // step, body, 0)

    core = place_ref[1] if own else 1 - place_ref[1]

    def flip(tile, carry):
        found = rows[pl.ds(pl.multiple_of(tile * LANES, LANES), LANES), :].T
        for idx, out in enumerate(outs):
            chunk, k = chosen[idx // dests], idx % dests
            xc = sizes[chunk]
            at = sum(sizes[:chunk]) * dests + k * xc
            spot = core * (out.shape[0] // 2) + tile * xc
            out[pl.ds(pl.multiple_of(spot, 8), xc), :] = found[at : at + xc]
        return carry

    lax.fori_loop(0, rows.shape[0] // LANES, flip, 0, unroll=2)


def first_synth(place, coeffs, table, dims, chosen, lanes, half):
    sizes, dests = dims
    heights = [2 * (lanes // LANES) * sizes[chunk] for chunk in chosen for _ in range(dests)]
    return pl.pallas_call(
        functools.partial(first_synth_kernel, (sizes, chosen, dests, not half)),
        in_specs=[SMEM, VMEM, VMEM] + [ANY] * len(half),
        out_specs=[VMEM] * len(heights),
        out_shape=[jax.ShapeDtypeStruct((h, LANES), F32) for h in heights],
        input_output_aliases={3 + k: k for k in range(len(half))},
        scratch_shapes=[pltpu.VMEM((lanes, LANES), F32)],
        compiler_params=still(),
        cost_estimate=SHORT,
        name="first_synth",
    )(place, coeffs, table, *half)


def second_synth_kernel(dims, place_ref, *refs):
    rows, xc, ky_len, kz_len, cols, y_len, pack = dims
    groups = rows // 2
    parts, table_ref, out_refs = refs[:groups], refs[groups], refs[groups + 1 : -1]
    a_ref = refs[-1]
    size = parts[0].shape[0] // 2
    stride = a_ref.shape[0] // rows
    for k, part in enumerate(parts):
        for core in range(2):
            spot = pl.multiple_of(((place_ref[0] ^ k) * 2 + core) * stride, 8)
            a_ref[pl.ds(spot, size), :] = part[core * size : (core + 1) * size, :]
    group = 5 * kz_len
    wide = round_up(group, LANES)
    tiles = size // xc

    def body(at, carry):
        turned = []
        for part in range(pack):
            line = [
                a_ref[pl.ds(tile * xc + at * pack + part, rows, stride=stride), :]
                for tile in range(tiles)
            ]
            found = []
            for ky in range(ky_len):
                start = ky * group
                low, off = divmod(start, LANES)
                window = line[low : low + (wide // LANES) + (1 if off else 0)]
                found.append(turn(jnp.concatenate(window, axis=1), -off)[:, :wide])
            turned.append(jnp.concatenate(found, axis=0).T[:group])
        plain = dot_data_left(jnp.concatenate(turned, axis=0), table_ref[0], table_ref[1])
        slope_in = [t[c * kz_len : (c + 1) * kz_len] for t in turned for c in (0, 2)]
        slope = dot_data_left(jnp.concatenate(slope_in, axis=0), table_ref[2], table_ref[3])
        fields = []
        for part in range(pack):
            own = plain[part * group : (part + 1) * group]
            sl = slope[part * 2 * kz_len : (part + 1) * 2 * kz_len]
            fields.append(
                jnp.concatenate(
                    [
                        own[: 3 * kz_len],
                        own[3 * kz_len : 4 * kz_len] - sl[:kz_len],
                        sl[kz_len:],
                        -own[4 * kz_len :],
                    ],
                    axis=0,
                )
            )
        for dest in range(cols):
            tile, off = divmod(dest * y_len, LANES)
            out_refs[dest][at] = lane_pack(
                [f[:, tile * LANES : (tile + 1) * LANES] for f in fields], y_len, off
            )[0]
        return carry

    lax.fori_loop(0, xc // pack, body, 0)


def second_synth(place, arrived, table, dims):
    rows, xc, ky_len, kz_len, cols, y_len, pack = dims
    packs = xc // pack
    return pl.pallas_call(
        functools.partial(second_synth_kernel, dims),
        in_specs=[SMEM] + [VMEM] * (len(arrived) + 1),
        out_specs=[VMEM] * cols,
        out_shape=[jax.ShapeDtypeStruct((packs, 6 * kz_len, LANES), F32)] * cols,
        scratch_shapes=[
            pltpu.VMEM((rows * (arrived[0].shape[0] // 2 + 8), LANES), F32),
        ],
        compiler_params=still(),
        cost_estimate=SHORT,
        name="second_synth",
    )(place, *arrived, table)


def cross(left, right):
    return [
        left[1] * right[2] - left[2] * right[1],
        left[2] * right[0] - left[0] * right[2],
        left[0] * right[1] - left[1] * right[0],
    ]


def earlier_kernel(count, *refs):
    vels, vorts, out_ref = refs[:count], refs[count : 2 * count], refs[2 * count]
    pack, y_len = out_ref.shape[1:3]
    for part in range(pack):
        def body(step, carry):
            at = pl.ds(pl.multiple_of(step * 8, 8), 8)
            total = None
            for vel, vort in zip(vels, vorts):
                term = cross(
                    [vel[0, c, part, at, :] for c in range(3)],
                    [vort[0, c, part, at, :] for c in range(3)],
                )
                total = term if total is None else [a + b for a, b in zip(total, term)]
            for comp in range(3):
                out_ref[comp, part, at, :] = total[comp]
            return carry

        lax.fori_loop(0, y_len // 8, body, 0, unroll=2)


def earlier(velocity, vorticity, start, xc, pack):
    orders, _, _, y_len, grid_len = velocity.shape
    packs = xc // pack
    block = (1, 3, pack, y_len, grid_len)

    def at(order):
        return pl.BlockSpec(block, lambda i: (order, 0, start // pack + i, 0, 0))

    specs = [at(k) for k in range(1, orders)] + [at(orders - k) for k in range(1, orders)]
    size = xc * y_len * grid_len
    return pl.pallas_call(
        functools.partial(earlier_kernel, orders - 1),
        grid=(packs,),
        in_specs=specs,
        out_specs=pl.BlockSpec((3, pack, y_len, grid_len), lambda i: (0, i, 0, 0)),
        out_shape=jax.ShapeDtypeStruct((3, xc, y_len, grid_len), F32),
        compiler_params=params(),
        cost_estimate=SHORT,
        name="earlier_orders",
    )(*[velocity] * (orders - 1), *[vorticity] * (orders - 1))


def third_kernel(dims, place_ref, *refs):
    begin, kz_len, cols, y_len, pack = dims
    b_refs, stored_refs, table_ref = refs[:cols], refs[cols : cols + 3], refs[cols + 3]
    data, sem = refs[-2:]
    out_refs = refs[-2 - cols : -2]
    grid_len = table_ref.shape[2]
    xc = data.shape[2]
    packs = xc // pack

    def copies(at):
        spot = pl.ds(at * pack, pack)
        far = pl.ds(begin + at * pack, pack)
        sources = [ref.at[0, :, far] for ref in stored_refs[:2]] + [stored_refs[2].at[:, spot]]
        return [
            pltpu.make_async_copy(source, data.at[idx, :, spot], sem.at[idx, at])
            for idx, source in enumerate(sources)
        ]

    for at in range(packs):
        for copy in copies(at):
            copy.start()

    def body(at, carry):
        def stack(field):
            return jnp.concatenate(
                [b_refs[k][at, field * kz_len : (field + 1) * kz_len, :] for k in range(cols)], axis=0
            ).T

        lines = jnp.concatenate([stack(field) for field in range(6)], axis=0)
        plain = dot_data_left(lines, table_ref[0], table_ref[1])
        slope = dot_data_left(lines[: 2 * LANES], table_ref[2], table_ref[3])
        new = [plain[f * LANES : (f + 1) * LANES] for f in range(6)]
        vel_new = new[:3]
        vort_new = [new[4] - slope[LANES:], slope[:LANES] + new[5], new[3]]
        for copy in copies(at):
            copy.wait()
        spot = pl.ds(at * pack, pack)
        flat = (pack * y_len, grid_len)
        vel, vort, base = [[data[idx, c, spot].reshape(flat) for c in range(3)] for idx in range(3)]
        one, two = cross(vel_new, vort), cross(vel, vort_new)
        total = [one[c] + two[c] + base[c] for c in range(3)]
        result = dot_data_right(table_ref[0], table_ref[1], jnp.concatenate(total, axis=0))
        for k in range(cols):
            for comp in range(3):
                out_refs[k][at, comp * kz_len : (comp + 1) * kz_len, :] = result[
                    k * kz_len : (k + 1) * kz_len, comp * LANES : (comp + 1) * LANES
                ]
        return carry

    lax.fori_loop(0, packs, body, 0)


def third(place, arrived, velocity, vorticity, base, table, begin, dims):
    kz_len, cols, y_len, pack = dims
    packs = arrived[0].shape[0]
    grid_len = velocity.shape[-1]
    return pl.pallas_call(
        functools.partial(third_kernel, (begin, *dims)),
        in_specs=[SMEM] + [VMEM] * cols + [ANY] * 3 + [VMEM],
        out_specs=[VMEM] * cols,
        out_shape=[jax.ShapeDtypeStruct((packs, 3 * kz_len, LANES), F32)] * cols,
        scratch_shapes=[
            pltpu.VMEM((3, 3, packs * pack, y_len, grid_len), F32),
            pltpu.SemaphoreType.DMA((3, packs)),
        ],
        compiler_params=still(),
        cost_estimate=SHORT,
        name="third_dimension",
    )(place, *arrived, velocity, vorticity, base, table)


def second_back_kernel(dims, place_ref, *refs):
    rows, xc, ky_len, kz_len, cols, y_len, pack = dims
    c_refs, table_ref, outs, all_ref = refs[:cols], refs[cols], refs[cols + 1 : -1], refs[-1]
    width = 3 * kz_len
    high_pad = round_up(width, LANES)

    def body(at, carry):
        lines = []
        for part in range(pack):
            tiles = lane_pack(
                [c_ref[at] for c_ref in c_refs], y_len, part * y_len
            )
            lines.append(jnp.concatenate(tiles, axis=1))
            if high_pad > width:
                lines.append(jnp.zeros((high_pad - width, cols * y_len), F32))
        result = dot_data_right(table_ref[0], table_ref[1], jnp.concatenate(lines, axis=0))
        for part in range(pack):
            own = result[:, part * high_pad : (part + 1) * high_pad]
            tiles = lane_pack([own[ky * rows : (ky + 1) * rows] for ky in range(ky_len)], width)
            for idx, tile in enumerate(tiles):
                spot = idx * xc + at * pack + part
                all_ref[pl.ds(spot, rows, stride=len(tiles) * xc), :] = tile
        return carry

    lax.fori_loop(0, xc // pack, body, 0)
    size = all_ref.shape[0] // len(outs)
    for k, out in enumerate(outs):
        out[...] = all_ref[pl.ds(pl.multiple_of((place_ref[0] ^ k) * size, 8), size), :]


def second_back(place, arrived, table, dims):
    rows, xc, ky_len, kz_len, cols, y_len, pack = dims
    size = round_up(ky_len * 3 * kz_len, LANES) // LANES * xc
    groups = rows // 2
    return pl.pallas_call(
        functools.partial(second_back_kernel, dims),
        in_specs=[SMEM] + [VMEM] * (cols + 1),
        out_specs=[VMEM] * groups,
        out_shape=[jax.ShapeDtypeStruct((2 * size, LANES), F32)] * groups,
        scratch_shapes=[pltpu.VMEM((rows * size, LANES), F32)],
        compiler_params=still(),
        cost_estimate=SHORT,
        name="second_back",
    )(place, *arrived, table)


def first_back_kernel(dims, place_ref, *refs):
    count, sizes, own = dims
    parts, table_ref, out_ref = refs[:count], refs[count], refs[count + 1]
    groups = count // len(sizes)
    core = place_ref[1] if own else 1 - place_ref[1]
    for tile in range(out_ref.shape[1] // LANES):
        found = []
        for idx, part in enumerate(parts):
            xc = sizes[idx // groups]
            spot = pl.multiple_of(core * (part.shape[0] // 2) + tile * xc, 8)
            found.append(part[pl.ds(spot, xc), :])
        out_ref[:, tile * LANES : (tile + 1) * LANES] = dot_data_right(
            table_ref[0], table_ref[1], jnp.concatenate(found, axis=0), NN
        )


def first_back(place, parts, table, sizes, own):
    count = len(parts)
    tiles = parts[0].shape[0] // 2 // sizes[0]
    return pl.pallas_call(
        functools.partial(first_back_kernel, (count, tuple(sizes), own)),
        in_specs=[SMEM] + [VMEM] * (count + 1),
        out_specs=VMEM,
        out_shape=jax.ShapeDtypeStruct((table.shape[1], tiles * LANES), F32),
        compiler_params=still(),
        cost_estimate=SHORT,
        name="first_back",
    )(place, *parts, table)


def last_kernel(dims, *refs):
    kz_len, modes, scale = dims
    wave_y_ref, wave_x_ref, wave_z_ref, *sums, out_ref, rows, held, sem = refs
    pair = 2 * 3 * kz_len
    for tile in range(rows.shape[0] // LANES):
        lanes = slice(tile * LANES, (tile + 1) * LANES)
        rows[lanes, 0:modes] = functools.reduce(jnp.add, [part[:, lanes] for part in sums]).T

    def copy(at):
        spot = pl.ds(2 * at, 2)
        return pltpu.make_async_copy(held.at[:, spot], out_ref.at[:, spot], sem.at[at])

    def body(at, carry):
        project(at)
        copy(at).start()
        return carry

    def finish(at, carry):
        copy(at).wait()
        return carry

    def project(at):
        spec = rows[pl.ds(pl.multiple_of(at * pair, 8), pair), :]
        wide = spec.shape[1]
        wave_x = jnp.broadcast_to(wave_x_ref[0:1, :], (kz_len, wide))
        wave_z = wave_z_ref[...]
        wave_y = wave_y_ref[at]
        even_x = lax.broadcasted_iota(jnp.int32, (kz_len, wide), 1) % 2 == 0
        even_z = lax.broadcasted_iota(jnp.int32, (kz_len, wide), 0) % 2 == 0

        def slope_x(value):
            return jnp.where(even_x, turn(value, -1), -turn(value, 1)) * wave_x

        def slope_z(value):
            return (
                jnp.where(
                    even_z,
                    pltpu.roll(value, kz_len - 1, axis=0),
                    -pltpu.roll(value, 1, axis=0),
                )
                * wave_z
            )

        s = [
            [spec[(y * 3 + c) * kz_len : (y * 3 + c + 1) * kz_len] for c in range(3)] for y in range(2)
        ]
        square = wave_x * wave_x + wave_z * wave_z + wave_y * wave_y
        positive = square > 0
        safe = jnp.where(positive, square, 1.0)
        potential = []
        for y in range(2):
            along_y = s[1 - y][1] * (wave_y if y == 0 else -wave_y)
            divergence = slope_x(s[y][0]) + along_y + slope_z(s[y][2])
            potential.append(jnp.where(positive, divergence / safe, 0.0))
        for y in range(2):
            along_y = potential[1 - y] * (wave_y if y == 0 else -wave_y)
            found = [
                s[y][0] + slope_x(potential[y]),
                s[y][1] + along_y,
                s[y][2] + slope_z(potential[y]),
            ]
            for comp in range(3):
                held[comp, 2 * at + y] = (found[comp] * scale)[:, :modes]

    steps = held.shape[1] // 2
    lax.fori_loop(0, steps, body, 0)
    lax.fori_loop(0, steps, finish, 0)


def last(sums, wave_y, wave_x, wave_z, ky_len, kz_len, scale):
    modes, lanes = sums[0].shape
    return pl.pallas_call(
        functools.partial(last_kernel, (kz_len, modes, scale)),
        in_specs=[SMEM] + [VMEM] * (2 + len(sums)),
        out_specs=ANY,
        out_shape=jax.ShapeDtypeStruct((3, ky_len, kz_len, modes), F32),
        scratch_shapes=[
            pltpu.VMEM((lanes, wave_x.shape[1]), F32),
            pltpu.VMEM((3, ky_len, kz_len, modes), F32),
            pltpu.SemaphoreType.DMA((ky_len // 2,)),
        ],
        compiler_params=still(),
        cost_estimate=SHORT,
        name="last_projection",
    )(wave_y, wave_x, wave_z, *sums)


def after(value, *earlier_values):
    return lax.optimization_barrier((value, earlier_values))[0]


def shards(new_velocity, stored_velocity, stored_vorticity):
    rows = lax.axis_size("row")
    cols = lax.axis_size("col")
    _, ky_len, kz_own, modes = new_velocity.shape
    orders, _, x_len, y_len, grid_len = stored_velocity.shape
    kz_len = round_up(kz_own, 8)
    kmax = modes // 2 - 1
    sizes = chunk_sizes(x_len)
    chunks = len(sizes)
    begins = [sum(sizes[:k]) for k in range(chunks)]
    pack = LANES // y_len
    wide = round_up(modes, LANES)
    group = 5 * kz_len
    lanes = round_up(ky_len * group, 256)

    basis = synth_np(grid_len, modes)
    slope = slope_np(basis, kmax)
    y_order = (np.arange(rows)[None, :] * ky_len + np.arange(ky_len)[:, None]).reshape(-1)

    groups = rows // 2
    row, col = lax.axis_index("row"), lax.axis_index("col")
    place = jnp.stack([row // 2, row % 2, col]).astype(jnp.int32)

    def own_table(tables, axis):
        return lax.dynamic_index_in_dim(jnp.asarray(np.stack(tables)), lax.axis_index(axis), 0, False)

    def x_points(row):
        owner = np.array([row ^ (2 * k) for k in range(groups)])
        return np.concatenate(
            [
                (owner[:, None] * x_len + begin + np.arange(xc)[None, :]).reshape(-1)
                for begin, xc in zip(begins, sizes)
            ]
        )

    def halves_of(plain, sloped):
        return np.stack([part for table in (plain, sloped) for part in halves(table)])

    def y_table(col):
        points = np.concatenate([(col ^ k) * y_len + np.arange(y_len) for k in range(cols)])
        return halves_of(basis[points].T[y_order], slope[points].T[y_order])

    def z_table(col):
        def spread(table):
            parts = table.T.reshape(cols, kz_own, grid_len)[[col ^ k for k in range(cols)]]
            parts = np.pad(parts, ((0, 0), (0, kz_len - kz_own), (0, 0)))
            return parts.reshape(cols * kz_len, grid_len)

        return halves_of(spread(basis), spread(slope))

    table_x = own_table(
        [halves_of(basis[x_points(row)].T, slope[x_points(row)].T) for row in range(rows)], "row"
    )
    table_y = own_table([y_table(col) for col in range(cols)], "col")
    table_z = own_table([z_table(col) for col in range(cols)], "col")

    def wave_of(index):
        return (index // 2).astype(F32) / kmax

    mode = jnp.arange(wide, dtype=jnp.int32)
    wave_x = jnp.broadcast_to(jnp.where(mode < modes, wave_of(mode), 0.0)[None, :], (8, wide))
    ky_first = lax.axis_index("row") * ky_len + 2 * jnp.arange(ky_len // 2, dtype=jnp.int32)
    wave_y = wave_of(ky_first)
    kz = lax.axis_index("col") * kz_own + jnp.arange(kz_len, dtype=jnp.int32)
    wave_z = jnp.broadcast_to(wave_of(kz)[:, None], (kz_len, wide))

    coeffs = new_velocity
    if kz_len > kz_own:
        coeffs = jnp.pad(coeffs, ((0, 0), (0, 0), (0, kz_len - kz_own), (0, 0)))

    def exchange(values, axis, shift, size):
        return [
            lax.ppermute(value, axis, [(src, src ^ (k << shift)) for src in range(size)]) if k else value
            for k, value in enumerate(values)
        ]

    def core_swap(value):
        return lax.ppermute(value, "row", [(src, src ^ 1) for src in range(rows)])

    dims = [(rows, xc, ky_len, kz_len, cols, y_len, pack) for xc in sizes]
    shape = (tuple(sizes), groups)
    other = core_swap(coeffs)
    small = (place, table_x, table_y, table_z, wave_x, wave_y, wave_z)
    place, table_x, table_y, table_z, wave_x, wave_y, wave_z = lax.optimization_barrier(small)

    def run_first(chosen, gate):
        own = coeffs if gate is None else after(coeffs, gate)
        found = first_synth(place, own, table_x, shape, chosen, lanes, ())
        found = first_synth(place, other, table_x, shape, chosen, lanes, found)
        return {chunk: list(found[k * groups : (k + 1) * groups]) for k, chunk in enumerate(chosen)}

    sent = run_first((0,), None)
    if chunks > 1:
        sent.update(run_first(tuple(range(1, chunks)), sent[0][0]))
    latest = sent[chunks - 1][0]

    def ordered(kernel, operands, *others):
        nonlocal latest
        operands = after(operands, latest)
        found = kernel(operands, *others)
        latest = found[0] if isinstance(found, (list, tuple)) else found
        return found

    stored = (stored_velocity, stored_vorticity)

    def run_earlier(chunk):
        return ordered(lambda values: earlier(*values, begins[chunk], sizes[chunk], pack), stored)

    def z_exchange(values, *gates, waves=True):
        found = [values[0]]
        for k in range(1, groups):
            value = values[k]
            if gates:
                value = after(value, found[1]) if waves and 2 * k > groups else after(value, *gates)
            found.append(lax.ppermute(value, "row", [(src, src ^ (2 * k)) for src in range(rows)]))
        return found

    first, second, middle, back, base = {}, {}, {}, {}, {}
    for step in range(min(2, chunks)):
        first[step] = z_exchange(sent[step], *([first[step - 1]] if step else []))

    def run_second(at):
        found = ordered(lambda values: second_synth(place, values, table_y, dims[at]), first[at])
        if at:
            found = [found[0]] + [after(value, second[at - 1]) for value in found[1:]]
        second[at] = exchange(found, "col", 0, cols)

    def run_third(at):
        found = ordered(
            lambda values: third(
                place, values, *stored, base[at], table_z, begins[at], dims[at][3:]
            ),
            second[at],
        )
        middle[at] = exchange(found, "col", 0, cols)

    def run_back(at):
        found = ordered(lambda values: second_back(place, values, table_y, dims[at]), middle[at])
        gates = [back[0] if at else first[min(1, chunks - 1)]] if at < 2 else []
        back[at] = z_exchange(found, *gates, waves=at == 0)

    def run_base(at):
        base[at] = run_earlier(at)
        if at == 1 and chunks > 2:
            first[2] = z_exchange(sent[2], back[0], base[1])

    plan = [(run_second, 0), (run_base, 0), (run_third, 0), (run_back, 0), (run_second, 1), (run_base, 1)]
    plan += [(run_base, 2), (run_second, 2), (run_third, 1), (run_third, 2), (run_back, 1), (run_back, 2)]
    for action, at in plan:
        if at < chunks:
            action(at)
    parts = [value for step in range(chunks) for value in back[step]]
    away = first_back(place, parts, table_x, sizes, False)
    home = first_back(place, parts, after(table_x, away), sizes, True)
    sums = [home, core_swap(away)]
    result = last(sums, wave_y, wave_x, wave_z, ky_len, kz_len, 1.0 / (orders + 1))
    return result[:, :, :kz_own] if kz_len > kz_own else result


def solution(mesh):
    return jax.shard_map(
        shards,
        mesh=mesh,
        in_specs=(
            P(None, "row", "col", None),
            P(None, None, "row", "col", None),
            P(None, None, "row", "col", None),
        ),
        out_specs=P(None, "row", "col", None),
        check_vma=False,
    )
```

```python
import functools
import math

import jax
import jax.numpy as jnp
import ml_dtypes
import numpy as np
from jax import lax
from jax.experimental import pallas as pl
from jax.experimental.pallas import tpu as pltpu
from jax.sharding import PartitionSpec as P

LANES = 128


def chunk_sizes(x_len):
    ends = 8
    return [ends, x_len - 2 * ends, ends] if x_len > 3 * ends else [ends] * (x_len // ends)

BF16 = jnp.bfloat16
F32 = jnp.float32
NN = (((1,), (0,)), ((), ()))
NT = (((1,), (1,)), ((), ()))


def round_up(value, step):
    return -(-value // step) * step


def synth_np(grid_len, mode_count):
    points = np.arange(grid_len)[:, None]
    mode_index = np.arange(mode_count)[None, :]
    wave_index = np.where(mode_index == 1, grid_len // 2, mode_index // 2)
    angles = (points * wave_index % grid_len) * (2.0 * math.pi / grid_len)
    trig = np.where((mode_index % 2 == 0) | (mode_index == 1), np.cos(angles), np.sin(angles))
    weight = np.where(mode_index < 2, 1.0, 2.0) / grid_len
    return np.where(mode_index == 1, 0.0, trig * np.sqrt(weight))


def slope_np(table, kmax):
    paired = table.reshape(table.shape[0], -1, 2)
    wavenum = np.arange(paired.shape[1]) / kmax
    return np.stack([-wavenum * paired[:, :, 1], wavenum * paired[:, :, 0]], -1).reshape(table.shape)


def halves(table):
    high = table.astype(ml_dtypes.bfloat16)
    low = (table - high.astype(np.float64)).astype(ml_dtypes.bfloat16)
    return high, low


def pieces_of(values):
    high = values.astype(BF16)
    return high, (values - high.astype(F32)).astype(BF16)


def dot(left, right, dims):
    return lax.dot_general(left, right, dims, preferred_element_type=F32)


def dot_data_left(values, high, low, dims=NN):
    top, rest = pieces_of(values)
    return dot(top, high, dims) + (dot(top, low, dims) + dot(rest, high, dims))


def dot_data_right(high, low, values, dims=NT):
    top, rest = pieces_of(values)
    return dot(high, top, dims) + (dot(low, top, dims) + dot(high, rest, dims))


def turn(values, shift):
    shift = shift % values.shape[-1]
    return values if shift == 0 else pltpu.roll(values, shift, axis=values.ndim - 1)


def lane_pack(parts, width, source_lane=0):
    tiles = []
    lane = lax.broadcasted_iota(jnp.int32, parts[0].shape, 1)
    for tile in range(-(-len(parts) * width // LANES)):
        start = tile * LANES
        acc = None
        for idx in range(start // width, min(len(parts) - 1, (start + LANES - 1) // width) + 1):
            moved = turn(parts[idx], idx * width - source_lane)
            acc = moved if acc is None else jnp.where(lane >= idx * width - start, moved, acc)
        tiles.append(acc)
    return tiles


VMEM_LIMIT = 32 * 1024 * 1024
VMEM_MOST = 60 * 1024 * 1024
SHORT = pl.CostEstimate(flops=1024, bytes_accessed=1024, transcendentals=0)
ANY = pl.BlockSpec(memory_space=pl.ANY)
HBM = pl.BlockSpec(memory_space=pltpu.HBM)
SMEM = pl.BlockSpec(memory_space=pltpu.SMEM)
VMEM = pl.BlockSpec(memory_space=pltpu.VMEM)


def params():
    return pltpu.CompilerParams(dimension_semantics=("arbitrary",), vmem_limit_bytes=VMEM_LIMIT)


def still(limit=VMEM_LIMIT):
    return pltpu.CompilerParams(vmem_limit_bytes=limit)


def both_passes(values, high_low, high):
    top, rest = pieces_of(values)
    wide = dot(top, high_low, NN)
    half = high.shape[1]
    return wide[:, :half] + (wide[:, half:] + dot(rest, high, NN))


def whole(array):
    rank = len(array.shape)
    return pl.BlockSpec(array.shape, lambda *_: (0,) * rank)


def first_synth_kernel(dims, place_ref, data, table_ref, *rest):
    sizes, chosen, dests, own = dims
    outs, rows = rest[-len(chosen) * dests - 1 : -1], rest[-1]
    _, ky_len, kz_len, _ = data.shape
    group = 5 * kz_len
    if ky_len * group < rows.shape[0]:
        rows[ky_len * group :, :] = jnp.zeros((rows.shape[0] - ky_len * group, LANES), F32)
    plain = jnp.concatenate([table_ref[0], table_ref[1]], axis=1)
    slope = jnp.concatenate([table_ref[2], table_ref[3]], axis=1)
    step = 4 if ky_len % 4 == 0 else 2

    def body(idx, carry):
        first = idx * step
        lines = [[data[comp, first + k] for comp in range(3)] for k in range(step)]
        found = both_passes(
            jnp.concatenate([v for line in lines for v in line], axis=0), plain, table_ref[0]
        )
        sloped = both_passes(
            jnp.concatenate([v for line in lines for v in line[1:]], axis=0), slope, table_ref[2]
        )
        for k in range(step):
            base = (first + k) * group
            rows[pl.ds(pl.multiple_of(base, 8), 3 * kz_len), :] = found[
                3 * k * kz_len : 3 * (k + 1) * kz_len
            ]
            rows[pl.ds(pl.multiple_of(base + 3 * kz_len, 8), 2 * kz_len), :] = sloped[
                2 * k * kz_len : 2 * (k + 1) * kz_len
            ]
        return carry

    lax.fori_loop(0, ky_len // step, body, 0)

    core = place_ref[1] if own else 1 - place_ref[1]

    def flip(tile, carry):
        found = rows[pl.ds(pl.multiple_of(tile * LANES, LANES), LANES), :].T
        for idx, out in enumerate(outs):
            chunk, k = chosen[idx // dests], idx % dests
            xc = sizes[chunk]
            at = sum(sizes[:chunk]) * dests + k * xc
            spot = core * (out.shape[0] // 2) + tile * xc
            out[pl.ds(pl.multiple_of(spot, 8), xc), :] = found[at : at + xc]
        return carry

    lax.fori_loop(0, rows.shape[0] // LANES, flip, 0, unroll=2)


def first_synth(place, coeffs, table, dims, chosen, lanes, half):
    sizes, dests = dims
    heights = [2 * (lanes // LANES) * sizes[chunk] for chunk in chosen for _ in range(dests)]
    return pl.pallas_call(
        functools.partial(first_synth_kernel, (sizes, chosen, dests, not half)),
        in_specs=[SMEM, VMEM, VMEM] + [ANY] * len(half),
        out_specs=[VMEM] * len(heights),
        out_shape=[jax.ShapeDtypeStruct((h, LANES), F32) for h in heights],
        input_output_aliases={3 + k: k for k in range(len(half))},
        scratch_shapes=[pltpu.VMEM((lanes, LANES), F32)],
        compiler_params=still(),
        cost_estimate=SHORT,
        name="first_synth",
    )(place, coeffs, table, *half)


def second_synth_kernel(dims, place_ref, *refs):
    rows, xc, ky_len, kz_len, cols, y_len, pack = dims
    groups = rows // 2
    parts, table_ref, out_refs = refs[:groups], refs[groups], refs[groups + 1 : -1]
    a_ref = refs[-1]
    size = parts[0].shape[0] // 2
    stride = a_ref.shape[0] // rows
    for k, part in enumerate(parts):
        for core in range(2):
            spot = pl.multiple_of(((place_ref[0] ^ k) * 2 + core) * stride, 8)
            a_ref[pl.ds(spot, size), :] = part[core * size : (core + 1) * size, :]
    group = 5 * kz_len
    wide = round_up(group, LANES)
    tiles = size // xc

    def body(at, carry):
        turned = []
        for part in range(pack):
            line = [
                a_ref[pl.ds(tile * xc + at * pack + part, rows, stride=stride), :]
                for tile in range(tiles)
            ]
            found = []
            for ky in range(ky_len):
                start = ky * group
                low, off = divmod(start, LANES)
                window = line[low : low + (wide // LANES) + (1 if off else 0)]
                found.append(turn(jnp.concatenate(window, axis=1), -off)[:, :wide])
            turned.append(jnp.concatenate(found, axis=0).T[:group])
        plain = dot_data_left(jnp.concatenate(turned, axis=0), table_ref[0], table_ref[1])
        slope_in = [t[c * kz_len : (c + 1) * kz_len] for t in turned for c in (0, 2)]
        slope = dot_data_left(jnp.concatenate(slope_in, axis=0), table_ref[2], table_ref[3])
        fields = []
        for part in range(pack):
            own = plain[part * group : (part + 1) * group]
            sl = slope[part * 2 * kz_len : (part + 1) * 2 * kz_len]
            fields.append(
                jnp.concatenate(
                    [
                        own[: 3 * kz_len],
                        own[3 * kz_len : 4 * kz_len] - sl[:kz_len],
                        sl[kz_len:],
                        -own[4 * kz_len :],
                    ],
                    axis=0,
                )
            )
        for dest in range(cols):
            tile, off = divmod(dest * y_len, LANES)
            out_refs[dest][at] = lane_pack(
                [f[:, tile * LANES : (tile + 1) * LANES] for f in fields], y_len, off
            )[0]
        return carry

    lax.fori_loop(0, xc // pack, body, 0)


def second_synth(place, arrived, table, dims):
    rows, xc, ky_len, kz_len, cols, y_len, pack = dims
    packs = xc // pack
    return pl.pallas_call(
        functools.partial(second_synth_kernel, dims),
        in_specs=[SMEM] + [VMEM] * (len(arrived) + 1),
        out_specs=[VMEM] * cols,
        out_shape=[jax.ShapeDtypeStruct((packs, 6 * kz_len, LANES), F32)] * cols,
        scratch_shapes=[
            pltpu.VMEM((rows * (arrived[0].shape[0] // 2 + 8), LANES), F32),
        ],
        compiler_params=still(),
        cost_estimate=SHORT,
        name="second_synth",
    )(place, *arrived, table)


def cross(left, right):
    return [
        left[1] * right[2] - left[2] * right[1],
        left[2] * right[0] - left[0] * right[2],
        left[0] * right[1] - left[1] * right[0],
    ]


def earlier_kernel(count, *refs):
    vels, vorts, out_ref = refs[:count], refs[count : 2 * count], refs[2 * count]
    pack, y_len = out_ref.shape[1:3]
    for part in range(pack):
        def body(step, carry):
            at = pl.ds(pl.multiple_of(step * 8, 8), 8)
            total = None
            for vel, vort in zip(vels, vorts):
                term = cross(
                    [vel[0, c, part, at, :] for c in range(3)],
                    [vort[0, c, part, at, :] for c in range(3)],
                )
                total = term if total is None else [a + b for a, b in zip(total, term)]
            for comp in range(3):
                out_ref[comp, part, at, :] = total[comp]
            return carry

        lax.fori_loop(0, y_len // 8, body, 0, unroll=2)


def earlier(velocity, vorticity, start, xc, pack):
    orders, _, _, y_len, grid_len = velocity.shape
    packs = xc // pack
    block = (1, 3, pack, y_len, grid_len)

    def at(order):
        return pl.BlockSpec(block, lambda i: (order, 0, start // pack + i, 0, 0))

    specs = [at(k) for k in range(1, orders)] + [at(orders - k) for k in range(1, orders)]
    size = xc * y_len * grid_len
    return pl.pallas_call(
        functools.partial(earlier_kernel, orders - 1),
        grid=(packs,),
        in_specs=specs,
        out_specs=pl.BlockSpec((3, pack, y_len, grid_len), lambda i: (0, i, 0, 0)),
        out_shape=jax.ShapeDtypeStruct((3, xc, y_len, grid_len), F32),
        compiler_params=params(),
        cost_estimate=SHORT,
        name="earlier_orders",
    )(*[velocity] * (orders - 1), *[vorticity] * (orders - 1))


def third_kernel(dims, place_ref, *refs):
    begin, kz_len, cols, y_len, pack = dims
    b_refs, stored_refs, table_ref = refs[:cols], refs[cols : cols + 3], refs[cols + 3]
    data, sem = refs[-2:]
    out_refs = refs[-2 - cols : -2]
    grid_len = table_ref.shape[2]
    xc = data.shape[2]
    packs = xc // pack

    def copies(at):
        spot = pl.ds(at * pack, pack)
        far = pl.ds(begin + at * pack, pack)
        sources = [ref.at[0, :, far] for ref in stored_refs[:2]] + [stored_refs[2].at[:, spot]]
        return [
            pltpu.make_async_copy(source, data.at[idx, :, spot], sem.at[idx, at])
            for idx, source in enumerate(sources)
        ]

    for at in range(packs):
        for copy in copies(at):
            copy.start()

    def body(at, carry):
        def stack(field):
            return jnp.concatenate(
                [b_refs[k][at, field * kz_len : (field + 1) * kz_len, :] for k in range(cols)], axis=0
            ).T

        lines = jnp.concatenate([stack(field) for field in range(6)], axis=0)
        plain = dot_data_left(lines, table_ref[0], table_ref[1])
        slope = dot_data_left(lines[: 2 * LANES], table_ref[2], table_ref[3])
        new = [plain[f * LANES : (f + 1) * LANES] for f in range(6)]
        vel_new = new[:3]
        vort_new = [new[4] - slope[LANES:], slope[:LANES] + new[5], new[3]]
        for copy in copies(at):
            copy.wait()
        spot = pl.ds(at * pack, pack)
        flat = (pack * y_len, grid_len)
        vel, vort, base = [[data[idx, c, spot].reshape(flat) for c in range(3)] for idx in range(3)]
        one, two = cross(vel_new, vort), cross(vel, vort_new)
        total = [one[c] + two[c] + base[c] for c in range(3)]
        result = dot_data_right(table_ref[0], table_ref[1], jnp.concatenate(total, axis=0))
        for k in range(cols):
            for comp in range(3):
                out_refs[k][at, comp * kz_len : (comp + 1) * kz_len, :] = result[
                    k * kz_len : (k + 1) * kz_len, comp * LANES : (comp + 1) * LANES
                ]
        return carry

    lax.fori_loop(0, packs, body, 0)


def third(place, arrived, velocity, vorticity, base, table, begin, dims):
    kz_len, cols, y_len, pack = dims
    packs = arrived[0].shape[0]
    grid_len = velocity.shape[-1]
    return pl.pallas_call(
        functools.partial(third_kernel, (begin, *dims)),
        in_specs=[SMEM] + [VMEM] * cols + [ANY] * 3 + [VMEM],
        out_specs=[VMEM] * cols,
        out_shape=[jax.ShapeDtypeStruct((packs, 3 * kz_len, LANES), F32)] * cols,
        scratch_shapes=[
            pltpu.VMEM((3, 3, packs * pack, y_len, grid_len), F32),
            pltpu.SemaphoreType.DMA((3, packs)),
        ],
        compiler_params=still(),
        cost_estimate=SHORT,
        name="third_dimension",
    )(place, *arrived, velocity, vorticity, base, table)


def second_back_kernel(dims, place_ref, *refs):
    rows, xc, ky_len, kz_len, cols, y_len, pack = dims
    c_refs, table_ref, outs, all_ref = refs[:cols], refs[cols], refs[cols + 1 : -1], refs[-1]
    width = 3 * kz_len
    high_pad = round_up(width, LANES)

    def body(at, carry):
        lines = []
        for part in range(pack):
            tiles = lane_pack(
                [c_ref[at] for c_ref in c_refs], y_len, part * y_len
            )
            lines.append(jnp.concatenate(tiles, axis=1))
            if high_pad > width:
                lines.append(jnp.zeros((high_pad - width, cols * y_len), F32))
        result = dot_data_right(table_ref[0], table_ref[1], jnp.concatenate(lines, axis=0))
        for part in range(pack):
            own = result[:, part * high_pad : (part + 1) * high_pad]
            tiles = lane_pack([own[ky * rows : (ky + 1) * rows] for ky in range(ky_len)], width)
            for idx, tile in enumerate(tiles):
                spot = idx * xc + at * pack + part
                all_ref[pl.ds(spot, rows, stride=len(tiles) * xc), :] = tile
        return carry

    lax.fori_loop(0, xc // pack, body, 0)
    size = all_ref.shape[0] // len(outs)
    for k, out in enumerate(outs):
        out[...] = all_ref[pl.ds(pl.multiple_of((place_ref[0] ^ k) * size, 8), size), :]


def second_back(place, arrived, table, dims):
    rows, xc, ky_len, kz_len, cols, y_len, pack = dims
    size = round_up(ky_len * 3 * kz_len, LANES) // LANES * xc
    groups = rows // 2
    return pl.pallas_call(
        functools.partial(second_back_kernel, dims),
        in_specs=[SMEM] + [VMEM] * (cols + 1),
        out_specs=[VMEM] * groups,
        out_shape=[jax.ShapeDtypeStruct((2 * size, LANES), F32)] * groups,
        scratch_shapes=[pltpu.VMEM((rows * size, LANES), F32)],
        compiler_params=still(),
        cost_estimate=SHORT,
        name="second_back",
    )(place, *arrived, table)


def first_back_kernel(dims, place_ref, *refs):
    count, sizes, own = dims
    parts, table_ref, out_ref = refs[:count], refs[count], refs[count + 1]
    groups = count // len(sizes)
    core = place_ref[1] if own else 1 - place_ref[1]
    for tile in range(out_ref.shape[1] // LANES):
        found = []
        for idx, part in enumerate(parts):
            xc = sizes[idx // groups]
            spot = pl.multiple_of(core * (part.shape[0] // 2) + tile * xc, 8)
            found.append(part[pl.ds(spot, xc), :])
        out_ref[:, tile * LANES : (tile + 1) * LANES] = dot_data_right(
            table_ref[0], table_ref[1], jnp.concatenate(found, axis=0), NN
        )


def first_back(place, parts, table, sizes, own):
    count = len(parts)
    tiles = parts[0].shape[0] // 2 // sizes[0]
    return pl.pallas_call(
        functools.partial(first_back_kernel, (count, tuple(sizes), own)),
        in_specs=[SMEM] + [VMEM] * (count + 1),
        out_specs=VMEM,
        out_shape=jax.ShapeDtypeStruct((table.shape[1], tiles * LANES), F32),
        compiler_params=still(),
        cost_estimate=SHORT,
        name="first_back",
    )(place, *parts, table)


def last_kernel(dims, *refs):
    kz_len, modes, scale = dims
    wave_y_ref, wave_x_ref, wave_z_ref, *sums, out_ref, rows, held, sem = refs
    pair = 2 * 3 * kz_len
    for tile in range(rows.shape[0] // LANES):
        lanes = slice(tile * LANES, (tile + 1) * LANES)
        rows[lanes, 0:modes] = functools.reduce(jnp.add, [part[:, lanes] for part in sums]).T

    def copy(at):
        spot = pl.ds(2 * at, 2)
        return pltpu.make_async_copy(held.at[:, spot], out_ref.at[:, spot], sem.at[at])

    def body(at, carry):
        project(at)
        copy(at).start()
        return carry

    def finish(at, carry):
        copy(at).wait()
        return carry

    def project(at):
        spec = rows[pl.ds(pl.multiple_of(at * pair, 8), pair), :]
        wide = spec.shape[1]
        wave_x = jnp.broadcast_to(wave_x_ref[0:1, :], (kz_len, wide))
        wave_z = wave_z_ref[...]
        wave_y = wave_y_ref[at]
        even_x = lax.broadcasted_iota(jnp.int32, (kz_len, wide), 1) % 2 == 0
        even_z = lax.broadcasted_iota(jnp.int32, (kz_len, wide), 0) % 2 == 0

        def slope_x(value):
            return jnp.where(even_x, turn(value, -1), -turn(value, 1)) * wave_x

        def slope_z(value):
            return (
                jnp.where(
                    even_z,
                    pltpu.roll(value, kz_len - 1, axis=0),
                    -pltpu.roll(value, 1, axis=0),
                )
                * wave_z
            )

        s = [
            [spec[(y * 3 + c) * kz_len : (y * 3 + c + 1) * kz_len] for c in range(3)] for y in range(2)
        ]
        square = wave_x * wave_x + wave_z * wave_z + wave_y * wave_y
        positive = square > 0
        safe = jnp.where(positive, square, 1.0)
        potential = []
        for y in range(2):
            along_y = s[1 - y][1] * (wave_y if y == 0 else -wave_y)
            divergence = slope_x(s[y][0]) + along_y + slope_z(s[y][2])
            potential.append(jnp.where(positive, divergence / safe, 0.0))
        for y in range(2):
            along_y = potential[1 - y] * (wave_y if y == 0 else -wave_y)
            found = [
                s[y][0] + slope_x(potential[y]),
                s[y][1] + along_y,
                s[y][2] + slope_z(potential[y]),
            ]
            for comp in range(3):
                held[comp, 2 * at + y] = (found[comp] * scale)[:, :modes]

    steps = held.shape[1] // 2
    lax.fori_loop(0, steps, body, 0)
    lax.fori_loop(0, steps, finish, 0)


def last(sums, wave_y, wave_x, wave_z, ky_len, kz_len, scale):
    modes, lanes = sums[0].shape
    return pl.pallas_call(
        functools.partial(last_kernel, (kz_len, modes, scale)),
        in_specs=[SMEM] + [VMEM] * (2 + len(sums)),
        out_specs=ANY,
        out_shape=jax.ShapeDtypeStruct((3, ky_len, kz_len, modes), F32),
        scratch_shapes=[
            pltpu.VMEM((lanes, wave_x.shape[1]), F32),
            pltpu.VMEM((3, ky_len, kz_len, modes), F32),
            pltpu.SemaphoreType.DMA((ky_len // 2,)),
        ],
        compiler_params=still(),
        cost_estimate=SHORT,
        name="last_projection",
    )(wave_y, wave_x, wave_z, *sums)


def after(value, *earlier_values):
    return lax.optimization_barrier((value, earlier_values))[0]


def shards(new_velocity, stored_velocity, stored_vorticity):
    rows = lax.axis_size("row")
    cols = lax.axis_size("col")
    _, ky_len, kz_own, modes = new_velocity.shape
    orders, _, x_len, y_len, grid_len = stored_velocity.shape
    kz_len = round_up(kz_own, 8)
    kmax = modes // 2 - 1
    sizes = chunk_sizes(x_len)
    chunks = len(sizes)
    begins = [sum(sizes[:k]) for k in range(chunks)]
    pack = LANES // y_len
    wide = round_up(modes, LANES)
    group = 5 * kz_len
    lanes = round_up(ky_len * group, 256)

    basis = synth_np(grid_len, modes)
    slope = slope_np(basis, kmax)
    y_order = (np.arange(rows)[None, :] * ky_len + np.arange(ky_len)[:, None]).reshape(-1)

    groups = rows // 2
    row, col = lax.axis_index("row"), lax.axis_index("col")
    place = jnp.stack([row // 2, row % 2, col]).astype(jnp.int32)

    def own_table(tables, axis):
        return lax.dynamic_index_in_dim(jnp.asarray(np.stack(tables)), lax.axis_index(axis), 0, False)

    def x_points(row):
        owner = np.array([row ^ (2 * k) for k in range(groups)])
        return np.concatenate(
            [
                (owner[:, None] * x_len + begin + np.arange(xc)[None, :]).reshape(-1)
                for begin, xc in zip(begins, sizes)
            ]
        )

    def halves_of(plain, sloped):
        return np.stack([part for table in (plain, sloped) for part in halves(table)])

    def y_table(col):
        points = np.concatenate([(col ^ k) * y_len + np.arange(y_len) for k in range(cols)])
        return halves_of(basis[points].T[y_order], slope[points].T[y_order])

    def z_table(col):
        def spread(table):
            parts = table.T.reshape(cols, kz_own, grid_len)[[col ^ k for k in range(cols)]]
            parts = np.pad(parts, ((0, 0), (0, kz_len - kz_own), (0, 0)))
            return parts.reshape(cols * kz_len, grid_len)

        return halves_of(spread(basis), spread(slope))

    table_x = own_table(
        [halves_of(basis[x_points(row)].T, slope[x_points(row)].T) for row in range(rows)], "row"
    )
    table_y = own_table([y_table(col) for col in range(cols)], "col")
    table_z = own_table([z_table(col) for col in range(cols)], "col")

    def wave_of(index):
        return (index // 2).astype(F32) / kmax

    mode = jnp.arange(wide, dtype=jnp.int32)
    wave_x = jnp.broadcast_to(jnp.where(mode < modes, wave_of(mode), 0.0)[None, :], (8, wide))
    ky_first = lax.axis_index("row") * ky_len + 2 * jnp.arange(ky_len // 2, dtype=jnp.int32)
    wave_y = wave_of(ky_first)
    kz = lax.axis_index("col") * kz_own + jnp.arange(kz_len, dtype=jnp.int32)
    wave_z = jnp.broadcast_to(wave_of(kz)[:, None], (kz_len, wide))

    coeffs = new_velocity
    if kz_len > kz_own:
        coeffs = jnp.pad(coeffs, ((0, 0), (0, 0), (0, kz_len - kz_own), (0, 0)))

    def exchange(values, axis, shift, size):
        return [
            lax.ppermute(value, axis, [(src, src ^ (k << shift)) for src in range(size)]) if k else value
            for k, value in enumerate(values)
        ]

    def core_swap(value):
        return lax.ppermute(value, "row", [(src, src ^ 1) for src in range(rows)])

    dims = [(rows, xc, ky_len, kz_len, cols, y_len, pack) for xc in sizes]
    shape = (tuple(sizes), groups)
    other = core_swap(coeffs)
    small = (place, table_x, table_y, table_z, wave_x, wave_y, wave_z)
    place, table_x, table_y, table_z, wave_x, wave_y, wave_z = lax.optimization_barrier(small)

    def run_first(chosen, gate):
        own = coeffs if gate is None else after(coeffs, gate)
        found = first_synth(place, own, table_x, shape, chosen, lanes, ())
        found = first_synth(place, other, table_x, shape, chosen, lanes, found)
        return {chunk: list(found[k * groups : (k + 1) * groups]) for k, chunk in enumerate(chosen)}

    sent = run_first((0,), None)
    if chunks > 1:
        sent.update(run_first(tuple(range(1, chunks)), sent[0][0]))
    latest = sent[chunks - 1][0]

    def ordered(kernel, operands, *others):
        nonlocal latest
        operands = after(operands, latest)
        found = kernel(operands, *others)
        latest = found[0] if isinstance(found, (list, tuple)) else found
        return found

    stored = (stored_velocity, stored_vorticity)

    def run_earlier(chunk):
        return ordered(lambda values: earlier(*values, begins[chunk], sizes[chunk], pack), stored)

    def z_exchange(values, *gates, waves=True):
        found = [values[0]]
        for k in range(1, groups):
            value = values[k]
            if gates:
                value = after(value, found[1]) if waves and 2 * k > groups else after(value, *gates)
            found.append(lax.ppermute(value, "row", [(src, src ^ (2 * k)) for src in range(rows)]))
        return found

    first, second, middle, back, base = {}, {}, {}, {}, {}
    for step in range(chunks):
        first[step] = z_exchange(sent[step], *([first[step - 1]] if step else []))

    def run_second(at):
        found = ordered(lambda values: second_synth(place, values, table_y, dims[at]), first[at])
        if at:
            gates = [second[at - 1]] + ([back[0]] if at == 2 else [])
            found = [found[0]] + [after(value, *gates) for value in found[1:]]
        second[at] = exchange(found, "col", 0, cols)

    def run_third(at):
        found = ordered(
            lambda values: third(
                place, values, *stored, base[at], table_z, begins[at], dims[at][3:]
            ),
            second[at],
        )
        middle[at] = exchange(found, "col", 0, cols)

    def run_back(at):
        found = ordered(lambda values: second_back(place, values, table_y, dims[at]), middle[at])
        gates = [back[0] if at else first[chunks - 1]] if at < 2 else []
        back[at] = found if at == 0 and chunks > 2 else z_exchange(found, *gates, waves=at == 0)

    def run_base(at):
        base[at] = run_earlier(at)
        if at == 1 and chunks > 2:
            back[0] = z_exchange(back[0], first[2], base[1])

    plan = [(run_second, 0), (run_base, 0), (run_third, 0), (run_base, 2), (run_back, 0), (run_second, 1)]
    plan += [(run_base, 1), (run_second, 2), (run_third, 1), (run_third, 2), (run_back, 1), (run_back, 2)]
    for action, at in plan:
        if at < chunks:
            action(at)
    parts = [value for step in range(chunks) for value in back[step]]
    away = first_back(place, parts, table_x, sizes, False)
    home = first_back(place, parts, after(table_x, away), sizes, True)
    sums = [home, core_swap(away)]
    result = last(sums, wave_y, wave_x, wave_z, ky_len, kz_len, 1.0 / (orders + 1))
    return result[:, :, :kz_own] if kz_len > kz_own else result


def solution(mesh):
    return jax.shard_map(
        shards,
        mesh=mesh,
        in_specs=(
            P(None, "row", "col", None),
            P(None, None, "row", "col", None),
            P(None, None, "row", "col", None),
        ),
        out_specs=P(None, "row", "col", None),
        check_vma=False,
    )
```
